32 devices in a mesh: groups: 2 (over y), members: 4 (over z), segment: 2 (over x), rows: 2 (over core).
Axes of the slice: x: 2, y: 2, z: 4, core: 2. Of those that a mesh axis runs over, the one named last changes fastest.
Arguments:
- init_state: bfloat16 [4, 2, 77, 128], P(('groups', 'segment'), 'rows'), parts along dimension 0, may hold values from -6 to 6
- forcing_slots: bfloat16 [4, 4, 2, 2, 4, 128], P('members', ('groups', 'segment'), None, 'rows'), parts along dimension 1, may hold values from -6 to 6
- atmos_owner: int32 [4, 2], P(('groups', 'segment')), parts along dimension 0, may hold values from 0 to 3
- land_mask: int32 [4, 128], P(('groups', 'rows')), parts along dimension 0, may hold values 0 or 1
- param_index: int32 [8], P(('groups', 'members')), parts along dimension 0, may hold values from 0 to 63
- settings: float32 [64, 16], replicated, may hold values from -5 to 5
- scale_weight: float32 [16, 256], replicated, may hold values from -0.75 to 0.75
- shift_weight: float32 [16, 256], replicated, may hold values from -0.75 to 0.75
- encode_weight: bfloat16 [256, 81], replicated, may hold values from -0.625 to 0.625
- conv_weight: bfloat16 [2, 256, 2304], P('segment'), may hold values from -0.125 to 0.125
- point_weight: bfloat16 [2, 256, 256], P('segment'), may hold values from -0.375 to 0.375
- norm_gain: bfloat16 [2, 256], P('segment'), may hold values from 0.099609375 to 1.8984375
- decode_weight: bfloat16 [77, 256], replicated, may hold values from -0.1875 to 0.1875
Outputs:
- final_state: bfloat16 [4, 4, 2, 77, 128], P('members', ('groups', 'segment'), 'rows'), parts along dimension 1
- ensemble_mean: float32 [4, 2, 77, 128], P(('groups', 'segment'), 'rows'), parts along dimension 0
The draws below stay inside these ranges and needn't reach their ends.
There are 2 independent parts, one for each index of `groups`. The reference program is written for one: setup_inputs(seed, part) draws one part's arguments, and reference() takes and returns one part's arrays. A program takes and returns all parts, laid end to end along the dimension named above; an argument that names none is the same for every part. Nothing has to cross between parts.
Inputs may be any that keep to these rules, and one draw needn't show every extreme that they name: `atmos_owner`: a member index of the same group. `param_index`: a row of settings.
All inputs are finite; a program needn't handle non-finite values. No bound on the sum of `land_mask` on one device may be relied on, other than what follows from the above.
Results may differ from the reference program's by a relative error of at most 0.018.
Values may be sent and summed in bfloat16 or wider, within the bound.
No kernel may reach another device: no remote copies, remote signals or barrier semaphores. Data moves between devices by JAX's collectives and lax.ppermute only.
A program may use at most 64 MiB of HBM per device.

```python
import jax
import jax.numpy as jnp
from jax import lax

C = 256
V = 77
F = 4
P_SIZE = 16
NSET = 64
STEPS = 2
LON_DEV = 128
LAYERS = 2
DATES = 2
MEMBERS = 4
LAT = 2


def touch_ends(values, own_key, least, top_value):
    extent = values.shape
    index_at = [jax.random.randint(jax.random.fold_in(own_key, axis), (), 0, extent[axis]) for axis in range(len(extent))]
    values = values.at[tuple(index_at)].set(least)
    longest = extent.index(max(extent))
    index_at[longest] = (index_at[longest] + 1) % extent[longest]
    return values.at[tuple(index_at)].set(top_value)


def levels(stream_key, extent, cuts, low, largest):
    def one(axis_at, parts):
        steps = jax.random.uniform(jax.random.fold_in(jax.random.fold_in(stream_key, 6), axis_at), (parts,), jnp.float32, low / len(cuts), largest / len(cuts))
        return jnp.repeat(jnp.exp(steps), extent[axis_at] // parts).reshape((-1,) + (1,) * (len(extent) - axis_at - 1))

    level = one(*cuts[0])
    for cut in cuts[1:]:
        level = level * one(*cut)
    return level


def scatter_about(own_key, shape, deviation, limit, cuts=(), kind=jnp.bfloat16):
    loudness = levels(own_key, shape, cuts, -0.22, 0.18) if cuts else 1.0
    drawn = jax.random.normal(own_key, shape, jnp.float32) * deviation * loudness
    return jnp.minimum(jnp.maximum(drawn, -limit), limit).astype(kind)


def setup_inputs(seed: int = 0, part: int = 0) -> dict:
    seeds = jax.random.split(jax.random.key(seed), 14)
    part_keys = jax.random.split(jax.random.fold_in(seeds[13], part), 14)
    init_state = scatter_about(part_keys[0], (DATES, LAT, V, LON_DEV), 1.0, 6.0, ((0, 2), (1, 2)))
    forcing_slots = scatter_about(part_keys[1], (MEMBERS, DATES, STEPS, LAT, F, LON_DEV), 1.0, 6.0, ((0, 4), (1, 2), (3, 2)))
    atmos_owner = touch_ends(jax.random.randint(part_keys[2], (DATES, STEPS), 0, MEMBERS), jax.random.fold_in(part_keys[2], 1), 0, MEMBERS - 1).astype(jnp.int32)
    land_mask = touch_ends((jax.random.randint(part_keys[3], (LAT, LON_DEV), 0, 4) < 3).astype(jnp.int32), jax.random.fold_in(part_keys[3], 1), 0, 1)
    param_index = touch_ends(jax.random.randint(part_keys[4], (MEMBERS,), 0, NSET), jax.random.fold_in(part_keys[4], 1), 0, NSET - 1).astype(jnp.int32)
    settings = scatter_about(seeds[5], (NSET, P_SIZE), 1.0, 5.0, (), jnp.float32)
    scale_weight = scatter_about(seeds[6], (P_SIZE, C), (4 * P_SIZE) ** -0.5, 0.75, (), jnp.float32)
    shift_weight = scatter_about(seeds[7], (P_SIZE, C), (4 * P_SIZE) ** -0.5, 0.75, (), jnp.float32)
    encode_weight = scatter_about(seeds[8], (C, V + F), (V + F) ** -0.5, 0.625)
    conv_weight = scatter_about(seeds[9], (LAYERS, C, 9 * C), (9 * C) ** -0.5, 0.125, ((0, 2),))
    point_weight = scatter_about(seeds[10], (LAYERS, C, C), C ** -0.5, 0.375, ((0, 2),))
    norm_gain = jnp.clip(1.0 + 0.18 * jax.random.normal(seeds[11], (LAYERS, C), jnp.float32), 0.099609375, 1.8984375).astype(jnp.bfloat16)
    decode_weight = scatter_about(seeds[12], (V, C), (4 * C) ** -0.5, 0.1875)
    return dict(init_state=init_state, forcing_slots=forcing_slots, atmos_owner=atmos_owner, land_mask=land_mask, param_index=param_index, settings=settings, scale_weight=scale_weight, shift_weight=shift_weight, encode_weight=encode_weight, conv_weight=conv_weight, point_weight=point_weight, norm_gain=norm_gain, decode_weight=decode_weight)


def lat_lon_taps(field, spacing):
    lat_cells = field.shape[-3]
    lon_cells = field.shape[-1]
    padded = jnp.pad(field, [(0, 0)] * (field.ndim - 3) + [(1, 1), (0, 0), (4, 4)])
    pieces = []
    for lat_off in range(3):
        lat_band = padded[..., lat_off:lat_off + lat_cells, :, :]
        for lon_off in (-1, 0, 1):
            begin = 4 + lon_off * spacing
            pieces.append(lat_band[..., begin:begin + lon_cells])
    return jnp.concatenate(pieces, axis=-2)

def section(hidden, conv_here, point_here, gain_here, spacing, land_cells):
    taps = lat_lon_taps(hidden, spacing).astype(jnp.float32)
    conv_out = jnp.einsum('ok,dlkx->dlox', conv_here.astype(jnp.float32), taps)
    chan_mean = lax.optimization_barrier(jnp.mean(conv_out, axis=-2, keepdims=True))
    centred = conv_out - chan_mean
    spread = lax.optimization_barrier(jnp.mean(centred * centred, axis=-2, keepdims=True))
    normed = centred * lax.rsqrt(spread + 1e-05) * gain_here.astype(jnp.float32)[:, None]
    activated = jax.nn.gelu(normed).astype(jnp.bfloat16)
    mixed = jnp.einsum('ok,dlkx->dlox', point_here.astype(jnp.float32), activated.astype(jnp.float32))
    return (land_cells * (hidden.astype(jnp.float32) + mixed)).astype(jnp.bfloat16)

def reference(init_state, forcing_slots, atmos_owner, land_mask, param_index, settings, scale_weight, shift_weight, encode_weight, conv_weight, point_weight, norm_gain, decode_weight):
    land_cells = land_mask.astype(jnp.float32)[:, None, :]
    date_ids = jnp.arange(DATES)
    per_step = []
    for step_no in range(STEPS):
        per_step.append(forcing_slots[atmos_owner[:, step_no], date_ids, step_no])
    forcing = jnp.stack(per_step, axis=1)

    def run_member(member_row):
        setting_row = settings[member_row]
        cond_scale = 1.0 + jnp.dot(setting_row, scale_weight, precision=lax.Precision.HIGHEST)
        cond_shift = jnp.dot(setting_row, shift_weight, precision=lax.Precision.HIGHEST)
        ocean_state = init_state
        for step_no in range(STEPS):
            inputs = jnp.concatenate([ocean_state, forcing[:, step_no]], axis=2).astype(jnp.float32)
            lifted = jnp.einsum('ok,dlkx->dlox', encode_weight.astype(jnp.float32), inputs)
            hidden = (land_cells * (lifted * cond_scale[:, None] + cond_shift[:, None])).astype(jnp.bfloat16)
            for layer in range(LAYERS):
                hidden = section(hidden, conv_weight[layer], point_weight[layer], norm_gain[layer], 2 ** (layer % 3), land_cells)
            change = jnp.einsum('ok,dlkx->dlox', decode_weight.astype(jnp.float32), hidden.astype(jnp.float32))
            ocean_state = (ocean_state.astype(jnp.float32) + land_cells * change).astype(jnp.bfloat16)
        return ocean_state
    finals = lax.map(run_member, param_index)
    return (finals, lax.optimization_barrier(jnp.mean(finals.astype(jnp.float32), axis=0)))
```

```python
import functools

import jax
import jax.numpy as jnp
from jax import lax
from jax.experimental import pallas as pl
from jax.experimental.pallas import tpu as pltpu
from jax.sharding import PartitionSpec as P

BF16_ROWS = 16


def padded_rows(count):
    return -(-count // BF16_ROWS) * BF16_ROWS


def passed_along(block, axis, distance):
    size = lax.axis_size(axis)
    return lax.ppermute(block, axis, [(i, (i + distance) % size) for i in range(size)])


def all_along(block, axis):
    return [block] + [passed_along(block, axis, k) for k in range(1, lax.axis_size(axis))]


def in_order(parts, axis):
    size, here = lax.axis_size(axis), lax.axis_index(axis)
    ordered = []
    for place in range(size):
        chosen = parts[0]
        for k in range(1, size):
            chosen = jnp.where((here - k) % size == place, parts[k], chosen)
        ordered.append(chosen)
    return ordered


def window_kernel(dims, place_ref, field_ref, scale_ref, shift_ref, gain_ref, enc_ref, dec_ref, *rest):
    steps, layers, bands, lat, members, lon, chans, vp, fp = dims
    blocks = rest[: 2 + (layers - 1) * bands]
    final_ref, mean_ref, weights, taps, hidden, conv, act, inputs, total, sems = rest[len(blocks):]
    here, band = place_ref[0], place_ref[1]
    taps_wide = 9 * chans
    part = chans // bands

    pltpu.make_async_copy(blocks[0], weights.at[here, :, pl.ds(0, taps_wide)], sems.at[here]).start()
    pltpu.make_async_copy(blocks[1], weights.at[here, :, pl.ds(taps_wide, chans)], sems.at[here]).start()
    for k in range(1, layers):
        slot = lax.rem(here - k + layers, layers)
        for j in range(bands):
            first = pl.multiple_of(lax.rem(band - j + bands, bands) * part, part)
            pltpu.make_async_copy(
                blocks[2 + (k - 1) * bands + j], weights.at[slot, pl.ds(first, part), :], sems.at[slot]
            ).start()

    def columns(m):
        return slice(m * lon, (m + 1) * lon)

    lane = lax.broadcasted_iota(jnp.int32, (chans, lon), 1)
    land = [field_ref[i, vp + fp * steps : vp + fp * steps + 1, :].astype(jnp.float32) for i in range(lat)]

    def encode(step, turn):
        enc = enc_ref[...]
        for i in range(lat):
            force = field_ref[i, vp + fp * step : vp + fp * (step + 1), :]
            if step == 0:
                fed = jnp.concatenate([field_ref[i, 0:vp, :], force], axis=0)
                shared = jnp.dot(enc, fed, preferred_element_type=jnp.float32)
            else:
                for m in range(members):
                    inputs[i, vp : vp + fp, columns(m)] = force
                lifted = jnp.dot(enc, inputs[i], preferred_element_type=jnp.float32)
            for m in range(members):
                value = shared if step == 0 else lifted[:, columns(m)]
                value = land[i] * (value * scale_ref[turn, :, m : m + 1] + shift_ref[turn, :, m : m + 1])
                hidden[i, :, columns(m)] = value.astype(jnp.bfloat16)

    def block(layer, not_yet):
        spacing = 2 ** (layer % 3)
        for i in range(lat):
            for m in range(members):
                value = hidden[i, :, columns(m)]
                base = 3 * chans * i
                zero = jnp.zeros_like(value)
                before = jnp.where(lane >= spacing, pltpu.roll(value, spacing, 1), zero)
                after = jnp.where(lane < lon - spacing, pltpu.roll(value, lon - spacing, 1), zero)
                taps[base : base + chans, columns(m)] = before
                taps[base + chans : base + 2 * chans, columns(m)] = value
                taps[base + 2 * chans : base + 3 * chans, columns(m)] = after
        if not_yet is not None:
            @pl.when(not_yet)
            def _():
                pltpu.make_async_copy(weights.at[layer], weights.at[layer], sems.at[layer]).wait()
        wide = 3 * chans
        for i in range(lat):
            low, high = max(i - 1, 0), min(i + 1, lat - 1)
            conv[i] = jnp.dot(
                weights[layer, :, (low - i + 1) * wide : (high - i + 2) * wide],
                taps[low * wide : (high + 1) * wide, :],
                preferred_element_type=jnp.float32,
            )
        gain = gain_ref[:, layer : layer + 1]
        for i in range(lat):
            for m in range(members):
                value = conv[i, :, columns(m)]
                centred = value - jnp.mean(value, axis=0, keepdims=True)
                spread = jnp.mean(centred * centred, axis=0, keepdims=True)
                normed = centred * lax.rsqrt(spread + 1e-05) * gain
                act[i, :, columns(m)] = jax.nn.gelu(normed).astype(jnp.bfloat16)
        for i in range(lat):
            mixed = jnp.dot(
                weights[layer, :, taps_wide:], act[i], preferred_element_type=jnp.float32
            )
            for m in range(members):
                kept = hidden[i, :, columns(m)].astype(jnp.float32)
                hidden[i, :, columns(m)] = (land[i] * (kept + mixed[:, columns(m)])).astype(jnp.bfloat16)

    varied = final_ref.shape[1]
    local = final_ref.shape[0]

    def window(turn, first):
        for step in range(steps):
            encode(step, turn)
            for layer in range(layers):
                block(layer, first if step == 0 else None)
            for i in range(lat):
                change = jnp.dot(dec_ref[...], hidden[i], preferred_element_type=jnp.float32)
                for m in range(members):
                    old = field_ref[i, 0:vp, :] if step == 0 else inputs[i, 0:vp, columns(m)]
                    new = old.astype(jnp.float32) + land[i] * change[:, columns(m)]
                    inputs[i, 0:vp, columns(m)] = new.astype(jnp.bfloat16)
        for i in range(local):
            row = band * local + i
            summed = inputs[row, 0:vp, columns(0)].astype(jnp.float32)
            for m in range(1, members):
                summed = summed + inputs[row, 0:vp, columns(m)].astype(jnp.float32)
            if turns == 1:
                total[i] = summed
            else:
                total[i] = jnp.where(first, summed, total[i] + summed)

            @pl.when(first)
            def _():
                final_ref[i] = inputs[row, 0:varied, columns(0)]

    turns = scale_ref.shape[0]
    if turns == 1:
        window(0, True)
    else:
        lax.fori_loop(0, turns, lambda turn, _: window(turn, turn == 0), None)
    for i in range(local):
        mean_ref[i] = total[i, 0:varied] * (1.0 / (members * turns))


def per_device(
    init_state,
    forcing_slots,
    atmos_owner,
    land_mask,
    param_index,
    settings,
    scale_weight,
    shift_weight,
    encode_weight,
    conv_weight,
    point_weight,
    norm_gain,
    decode_weight,
):
    members, layers, bands = (lax.axis_size(a) for a in ("members", "segment", "rows"))
    here, band = lax.axis_index("segment"), lax.axis_index("rows")
    _, local, varied, lon = init_state.shape
    steps, forced = forcing_slots.shape[2], forcing_slots.shape[4]
    chans = conv_weight.shape[1]
    lat = local * bands
    vp, fp = padded_rows(varied), padded_rows(forced)
    part = chans // bands

    mine = jnp.concatenate([conv_weight[0], point_weight[0]], axis=1)
    mine = lax.dynamic_slice_in_dim(mine, band * part, part, 0)
    sections = all_along(mine, "segment")[1:]
    gains = in_order(all_along(norm_gain.astype(jnp.float32), "segment"), "segment")
    gain = jnp.concatenate(gains, axis=0).T

    slots = forcing_slots[0, 0].astype(jnp.float32).reshape(-1, lon)
    index_row = jnp.broadcast_to(param_index.astype(jnp.float32)[:, None], (1, lon))
    group = all_along(jnp.concatenate([slots, index_row], axis=0), "members")
    member = lax.axis_index("members")
    forcing = jnp.zeros((steps, slots.shape[0] // steps, lon), jnp.float32)
    for k in range(members):
        owned = (atmos_owner[0] == (member - k) % members)[:, None, None]
        forcing = jnp.where(owned, group[k][:-1].reshape(forcing.shape), forcing)
    forcing = forcing.reshape(steps, local, forced, lon).astype(jnp.bfloat16)

    picked = jnp.stack([g[-1, 0] for g in group])
    choose = (jnp.arange(settings.shape[0], dtype=jnp.float32)[None] == picked[:, None]).astype(jnp.float32)
    rows = jnp.dot(choose, settings, precision=lax.Precision.HIGHEST)
    scale = 1.0 + jnp.dot(scale_weight.T, rows.T, precision=lax.Precision.HIGHEST)
    shift = jnp.dot(shift_weight.T, rows.T, precision=lax.Precision.HIGHEST)

    rim = ((0, 0), (0, fp - forced), (0, 0))
    field = [jnp.pad(init_state[0], ((0, 0), (0, vp - varied), (0, 0)))]
    field += [jnp.pad(forcing[t], rim) for t in range(steps)]
    field += [jnp.broadcast_to(land_mask.astype(jnp.bfloat16)[:, None, :], (local, BF16_ROWS, lon))]
    field = jnp.concatenate(field, axis=1)
    field = jnp.concatenate(in_order(all_along(field, "rows"), "rows"), axis=0)

    enc = jnp.pad(encode_weight[:, :varied], ((0, 0), (0, vp - varied)))
    enc = jnp.concatenate([enc, jnp.pad(encode_weight[:, varied:], ((0, 0), (0, fp - forced)))], axis=1)
    dec = jnp.pad(decode_weight, ((0, vp - varied), (0, 0)))

    blocks = [conv_weight[0], point_weight[0]]
    for section in sections:
        blocks += all_along(section, "rows")

    place = jnp.stack([here, band]).astype(jnp.int32)
    at_once = next(n for n in (4, 2, 1) if members % n == 0)
    scale, shift = (a.reshape(chans, -1, at_once).swapaxes(0, 1) for a in (scale, shift))
    dims = (steps, layers, bands, lat, at_once, lon, chans, vp, fp)
    wide = at_once * lon
    vmem = pl.BlockSpec(memory_space=pltpu.VMEM)
    final, mean = pl.pallas_call(
        functools.partial(window_kernel, dims),
        out_shape=(
            jax.ShapeDtypeStruct((local, varied, lon), jnp.bfloat16),
            jax.ShapeDtypeStruct((local, varied, lon), jnp.float32),
        ),
        in_specs=[pl.BlockSpec(memory_space=pltpu.SMEM)]
        + [vmem] * 6
        + [pl.BlockSpec(memory_space=pl.ANY)] * len(blocks),
        out_specs=(vmem, vmem),
        scratch_shapes=[
            pltpu.VMEM((layers, chans, 10 * chans), jnp.bfloat16),
            pltpu.VMEM((lat * 3 * chans, wide), jnp.bfloat16),
            pltpu.VMEM((lat, chans, wide), jnp.bfloat16),
            pltpu.VMEM((lat, chans, wide), jnp.float32),
            pltpu.VMEM((lat, chans, wide), jnp.bfloat16),
            pltpu.VMEM((lat, vp + fp, wide), jnp.bfloat16),
            pltpu.VMEM((local, vp, lon), jnp.float32),
            pltpu.SemaphoreType.DMA((layers,)),
        ],
        compiler_params=pltpu.CompilerParams(vmem_limit_bytes=40 * 1024 * 1024),
    )(place, field, scale, shift, gain, enc, dec, *blocks)
    return final[None, None], mean[None]


def solution(mesh):
    in_specs = (
        P(("groups", "segment"), "rows", None, None),
        P("members", ("groups", "segment"), None, "rows", None, None),
        P(("groups", "segment"), None),
        P(("groups", "rows"), None),
        P(("groups", "members")),
        P(),
        P(),
        P(),
        P(),
        P("segment", None, None),
        P("segment", None, None),
        P("segment", None),
        P(),
    )
    out_specs = (
        P("members", ("groups", "segment"), "rows", None, None),
        P(("groups", "segment"), "rows", None, None),
    )
    return jax.shard_map(
        per_device, mesh=mesh, in_specs=in_specs, out_specs=out_specs, check_vma=False
    )
```

```python
import functools

import jax
import jax.numpy as jnp
from jax import lax
from jax.experimental import pallas as pl
from jax.experimental.pallas import tpu as pltpu
from jax.sharding import PartitionSpec as P

BF16_ROWS = 16
VMEM_BYTES = 28 * 1024 * 1024


def padded_rows(count):
    return -(-count // BF16_ROWS) * BF16_ROWS


def passed_along(block, axis, distance):
    size = lax.axis_size(axis)
    return lax.ppermute(block, axis, [(i, (i + distance) % size) for i in range(size)])


def all_along(block, axis):
    return [block] + [passed_along(block, axis, k) for k in range(1, lax.axis_size(axis))]


def from_place(parts, here, place):
    chosen = parts[0]
    for k in range(1, len(parts)):
        chosen = jnp.where(lax.rem(here - k + len(parts), len(parts)) == place, parts[k], chosen)
    return chosen


def field_kernel(dims, scalar_ref, state_ref, land_ref, *rest):
    steps, members, local, forced, vp, fp = dims
    group, out_ref = rest[:members], rest[members]
    varied, lon = state_ref.shape[1:]
    for i in range(local):
        out_ref[i] = jnp.zeros(out_ref.shape[1:], jnp.bfloat16)
        out_ref[i, 0:varied] = state_ref[i]
        for t in range(steps):
            first = (t * local + i) * forced
            force = group[0][first : first + forced, :]
            for k in range(1, members):
                source = lax.rem(scalar_ref[2] - k + members, members)
                force = jnp.where(scalar_ref[3 + t] == source, group[k][first : first + forced, :], force)
            out_ref[i, vp + fp * t : vp + fp * t + forced, :] = force.astype(jnp.bfloat16)
        out_ref[i, vp + fp * steps : vp + fp * steps + 1, :] = land_ref[i : i + 1, :].astype(jnp.bfloat16)


def put_taps(taps, value, row, cols, spacing):
    chans, lon = value.shape
    lane = lax.broadcasted_iota(jnp.int32, (chans, lon), 1)
    zero = jnp.zeros_like(value)
    base = 3 * chans * row
    taps[base : base + chans, cols] = jnp.where(lane >= spacing, pltpu.roll(value, spacing, 1), zero)
    taps[base + chans : base + 2 * chans, cols] = value
    taps[base + 2 * chans : base + 3 * chans, cols] = jnp.where(
        lane < lon - spacing, pltpu.roll(value, lon - spacing, 1), zero
    )


def first_kernel(dims, scalar_ref, enc_ref, settings_ref, scale_w_ref, shift_w_ref, *rest):
    steps, layers, bands, local, members, lon, chans, vp, fp, turns = dims
    fields, rest = rest[:bands], rest[bands:]
    group, rest = rest[: members * turns], rest[members * turns :]
    gains, rest = rest[:layers], rest[layers:]
    field_ref, scale_ref, shift_ref, gain_ref, hidden_ref, taps_ref = rest
    here, band = scalar_ref[0], scalar_ref[1]
    for b in range(bands):
        field_ref[b * local : (b + 1) * local] = from_place([f[...] for f in fields], band, b)

    eye = lax.broadcasted_iota(jnp.int32, (chans, chans), 0) == lax.broadcasted_iota(jnp.int32, (chans, chans), 1)
    for layer in range(layers):
        row = from_place([g[...] for g in gains], here, layer)
        column = jnp.sum(jnp.where(eye, row, 0.0), axis=1, keepdims=True)
        gain_ref[layer] = jnp.broadcast_to(column, (chans, lon))

    settings = settings_ref[...]
    numbers = lax.broadcasted_iota(jnp.int32, settings.shape, 0).astype(jnp.float32)
    for m, entry in enumerate(group):
        chosen = entry[entry.shape[0] - 1 : entry.shape[0], 0 : settings.shape[1]]
        row = jnp.sum(jnp.where(numbers == chosen, settings, 0.0), axis=0, keepdims=True)
        cols = slice((m % members) * lon, (m % members + 1) * lon)
        scale = 1.0 + jnp.sum(scale_w_ref[...] * row, axis=1, keepdims=True)
        shift = jnp.sum(shift_w_ref[...] * row, axis=1, keepdims=True)
        scale_ref[m // members, :, cols] = jnp.broadcast_to(scale, (chans, lon))
        shift_ref[m // members, :, cols] = jnp.broadcast_to(shift, (chans, lon))

    if turns == 1:
        for i in range(bands * local):
            land = field_ref[i, vp + fp * steps : vp + fp * steps + 1, :].astype(jnp.float32)
            lifted = jnp.dot(enc_ref[...], field_ref[i, 0 : vp + fp, :], preferred_element_type=jnp.float32)
            for m in range(members):
                cols = slice(m * lon, (m + 1) * lon)
                value = land * (lifted * scale_ref[0, :, cols] + shift_ref[0, :, cols])
                value = value.astype(jnp.bfloat16)
                hidden_ref[i, :, cols] = value
                put_taps(taps_ref, value, i, cols, 1)


def after_kernel(section_ref, earlier_ref, out_ref):
    pass


def after(section, earlier):
    whole = pl.BlockSpec(memory_space=pl.ANY)
    return pl.pallas_call(
        after_kernel,
        out_shape=jax.ShapeDtypeStruct(section.shape, section.dtype),
        in_specs=[whole, whole],
        out_specs=whole,
        input_output_aliases={0: 0},
        cost_estimate=pl.CostEstimate(flops=0, bytes_accessed=0, transcendentals=0),
    )(section, earlier)


def window_kernel(dims, scalar_ref, field_ref, scale_ref, shift_ref, gain_ref, enc_ref, dec_ref, *rest):
    steps, layers, bands, local, members, lon, chans, vp, fp, turns = dims
    lat = bands * local
    hidden, taps = rest[:2]
    blocks, rest = rest[2 : 4 + (layers - 1) * bands], rest[4 + (layers - 1) * bands :]
    final_ref, mean_ref, weights, conv, act, inputs, total, sems = rest[:8]
    here, band = scalar_ref[0], scalar_ref[1]
    taps_wide, wide = 9 * chans, 3 * chans
    part = chans // bands

    pltpu.make_async_copy(blocks[0], weights.at[here, :, pl.ds(0, taps_wide)], sems.at[here]).start()
    pltpu.make_async_copy(blocks[1], weights.at[here, :, pl.ds(taps_wide, chans)], sems.at[here]).start()
    for k in range(1, layers):
        slot = lax.rem(here - k + layers, layers)
        for j in range(bands):
            first = pl.multiple_of(lax.rem(band - j + bands, bands) * part, part)
            pltpu.make_async_copy(
                blocks[2 + (k - 1) * bands + j], weights.at[slot, pl.ds(first, part), :], sems.at[slot]
            ).start()

    if turns > 1:
        hidden, taps = rest[8:]

    def columns(m):
        return slice(m * lon, (m + 1) * lon)

    land = [field_ref[i, vp + fp * steps : vp + fp * steps + 1, :].astype(jnp.float32) for i in range(lat)]

    def put_hidden(i, m, value, layer):
        value = value.astype(jnp.bfloat16)
        hidden[i, :, columns(m)] = value
        if layer is not None:
            put_taps(taps, value, i, columns(m), 2 ** (layer % 3))

    def encode(step, turn):
        for i in range(lat):
            force = field_ref[i, vp + fp * step : vp + fp * (step + 1), :]
            for m in range(members):
                inputs[i, vp : vp + fp, columns(m)] = force
                if step == 0:
                    inputs[i, 0:vp, columns(m)] = field_ref[i, 0:vp, :]
            lifted = jnp.dot(enc_ref[...], inputs[i], preferred_element_type=jnp.float32)
            for m in range(members):
                value = lifted[:, columns(m)] * scale_ref[turn, :, columns(m)] + shift_ref[turn, :, columns(m)]
                put_hidden(i, m, land[i] * value, 0)

    def activate(value, layer):
        centred = value - jnp.sum(value, axis=0, keepdims=True) * (1.0 / chans)
        spread = jnp.sum(centred * centred, axis=0, keepdims=True) * (1.0 / chans)
        normed = (centred * lax.rsqrt(spread + 1e-05)).astype(jnp.bfloat16) * gain_ref[layer].astype(jnp.bfloat16)
        inner = normed * (normed * normed * 0.0356774081 + 0.7978845608)
        half = normed * 0.5
        return half + half * jnp.tanh(inner)

    def block(layer, not_yet):
        if not_yet is True:
            pltpu.make_async_copy(weights.at[layer], weights.at[layer], sems.at[layer]).wait()
        elif not_yet is not None:

            @pl.when(not_yet)
            def _():
                pltpu.make_async_copy(weights.at[layer], weights.at[layer], sems.at[layer]).wait()

        for i in range(lat):
            low, high = max(i - 1, 0), min(i + 1, lat - 1)
            conv[i] = jnp.dot(
                weights[layer, :, (low - i + 1) * wide : (high - i + 2) * wide],
                taps[low * wide : (high + 1) * wide, :],
                preferred_element_type=jnp.float32,
            )
        for i in range(lat):
            for m in range(members):
                act[i, :, columns(m)] = activate(conv[i, :, columns(m)], layer)
        for i in range(lat):
            mixed = jnp.dot(weights[layer, :, taps_wide:], act[i], preferred_element_type=jnp.float32)
            for m in range(members):
                kept = hidden[i, :, columns(m)].astype(jnp.float32)
                later = layer + 1 if layer + 1 < layers else None
                put_hidden(i, m, land[i] * (kept + mixed[:, columns(m)]), later)

    varied = final_ref.shape[1]

    def window(turn, first):
        for step in range(steps):
            if step > 0 or turns > 1:
                encode(step, turn)
            for layer in range(layers):
                block(layer, first if step == 0 else None)
            for i in range(lat):
                change = jnp.dot(dec_ref[...], hidden[i], preferred_element_type=jnp.float32)
                for m in range(members):
                    old = field_ref[i, 0:vp, :] if step == 0 else inputs[i, 0:vp, columns(m)]
                    new = old.astype(jnp.float32) + land[i] * change[:, columns(m)]
                    inputs[i, 0:vp, columns(m)] = new.astype(jnp.bfloat16)
        for i in range(local):
            row = band * local + i
            summed = inputs[row, 0:vp, columns(0)].astype(jnp.float32)
            for m in range(1, members):
                summed = summed + inputs[row, 0:vp, columns(m)].astype(jnp.float32)
            if turns == 1:
                mean_ref[:, i, :] = summed[0:varied] * (1.0 / members)
                final_ref[i] = inputs[row, 0:varied, columns(0)]
            else:
                total[i] = jnp.where(first, summed, total[i] + summed)
                mean_ref[:, i, :] = total[i, 0:varied] * (1.0 / (members * turns))

                @pl.when(first)
                def _():
                    final_ref[i] = inputs[row, 0:varied, columns(0)]

    if turns == 1:
        window(0, True)
    else:
        lax.fori_loop(0, turns, lambda turn, _: window(turn, turn == 0), None)


def per_device(
    init_state,
    forcing_slots,
    atmos_owner,
    land_mask,
    param_index,
    settings,
    scale_weight,
    shift_weight,
    encode_weight,
    conv_weight,
    point_weight,
    norm_gain,
    decode_weight,
):
    members, layers, bands = (lax.axis_size(a) for a in ("members", "segment", "rows"))
    here, band = lax.axis_index("segment"), lax.axis_index("rows")
    _, local, varied, lon = init_state.shape
    steps, forced = forcing_slots.shape[2], forcing_slots.shape[4]
    chans = conv_weight.shape[1]
    lat = local * bands
    vp, fp = padded_rows(varied), padded_rows(forced)
    part = chans // bands
    at_once = next(n for n in (4, 2, 1) if members % n == 0)
    turns, wide = members // at_once, at_once * lon
    smem, vmem, whole = (pl.BlockSpec(memory_space=s) for s in (pltpu.SMEM, pltpu.VMEM, pl.ANY))
    params = pltpu.CompilerParams(vmem_limit_bytes=VMEM_BYTES)
    free = pl.CostEstimate(flops=0, bytes_accessed=0, transcendentals=0)

    mine = jnp.concatenate([conv_weight[0], point_weight[0]], axis=1)
    mine = lax.dynamic_slice_in_dim(mine, band * part, part, 0)
    sections = all_along(mine, "segment")[1:]

    slots = forcing_slots[0, 0].astype(jnp.float32).reshape(-1, lon)
    index_row = jnp.broadcast_to(param_index.astype(jnp.float32)[:, None], (1, lon))
    group = all_along(jnp.concatenate([slots, index_row], axis=0), "members")
    gains = all_along(norm_gain.astype(jnp.float32), "segment")
    scalars = jnp.concatenate(
        [jnp.stack([here, band, lax.axis_index("members")]).astype(jnp.int32), atmos_owner[0]]
    )
    field = pl.pallas_call(
        functools.partial(field_kernel, (steps, members, local, forced, vp, fp)),
        out_shape=jax.ShapeDtypeStruct((local, vp + fp * steps + BF16_ROWS, lon), jnp.bfloat16),
        in_specs=[smem] + [vmem] * (2 + members),
        out_specs=vmem,
        compiler_params=params,
        cost_estimate=free,
    )(scalars, init_state[0], land_mask, *group)
    fields = all_along(field, "rows")

    enc = jnp.pad(encode_weight[:, :varied], ((0, 0), (0, vp - varied)))
    enc = jnp.concatenate([enc, jnp.pad(encode_weight[:, varied:], ((0, 0), (0, fp - forced)))], axis=1)
    dec = jnp.pad(decode_weight, ((0, vp - varied), (0, 0)))
    dims = (steps, layers, bands, local, at_once, lon, chans, vp, fp, turns)
    field, scale, shift, gain, hidden, taps = pl.pallas_call(
        functools.partial(first_kernel, dims),
        out_shape=(
            jax.ShapeDtypeStruct((lat, vp + fp * steps + BF16_ROWS, lon), jnp.bfloat16),
            jax.ShapeDtypeStruct((turns, chans, wide), jnp.float32),
            jax.ShapeDtypeStruct((turns, chans, wide), jnp.float32),
            jax.ShapeDtypeStruct((layers, chans, lon), jnp.float32),
            jax.ShapeDtypeStruct((lat, chans, wide), jnp.bfloat16),
            jax.ShapeDtypeStruct((lat * 3 * chans, wide), jnp.bfloat16),
        ),
        in_specs=[smem] + [vmem] * (4 + bands + members + layers),
        out_specs=(vmem,) * 6,
        compiler_params=params,
        cost_estimate=free,
    )(scalars, enc, settings, scale_weight.T, shift_weight.T, *fields, *group, *gains)

    blocks = [conv_weight[0], point_weight[0]]
    for section in sections:
        blocks += all_along(after(section, taps), "rows")

    scratch = [
        pltpu.VMEM((layers, chans, 10 * chans), jnp.bfloat16),
        pltpu.VMEM((lat, chans, wide), jnp.float32),
        pltpu.VMEM((lat, chans, wide), jnp.bfloat16),
        pltpu.VMEM((lat, vp + fp, wide), jnp.bfloat16),
        pltpu.VMEM((local, vp, lon), jnp.float32),
        pltpu.SemaphoreType.DMA((layers,)),
    ]
    if turns > 1:
        scratch += [pltpu.VMEM(hidden.shape, jnp.bfloat16), pltpu.VMEM(taps.shape, jnp.bfloat16)]
    final, mean = pl.pallas_call(
        functools.partial(window_kernel, dims),
        out_shape=(
            jax.ShapeDtypeStruct((local, varied, lon), jnp.bfloat16),
            jax.ShapeDtypeStruct((varied, local, lon), jnp.float32),
        ),
        in_specs=[smem] + [vmem] * 8 + [whole] * len(blocks),
        out_specs=(vmem, vmem),
        scratch_shapes=scratch,
        compiler_params=params,
        cost_estimate=free,
    )(scalars, field, scale, shift, gain, enc, dec, hidden, taps, *blocks)
    return final[None, None], jnp.swapaxes(mean, 0, 1)[None]
def solution(mesh):
    in_specs = (
        P(("groups", "segment"), "rows", None, None),
        P("members", ("groups", "segment"), None, "rows", None, None),
        P(("groups", "segment"), None),
        P(("groups", "rows"), None),
        P(("groups", "members")),
        P(),
        P(),
        P(),
        P(),
        P("segment", None, None),
        P("segment", None, None),
        P("segment", None),
        P(),
    )
    out_specs = (
        P("members", ("groups", "segment"), "rows", None, None),
        P(("groups", "segment"), "rows", None, None),
    )
    return jax.shard_map(
        per_device, mesh=mesh, in_specs=in_specs, out_specs=out_specs, check_vma=False
    )
```

```python
import functools

import jax
import jax.numpy as jnp
from jax import lax
from jax.experimental import pallas as pl
from jax.experimental.pallas import tpu as pltpu
from jax.sharding import PartitionSpec as P

BF16_ROWS = 16
MIB = 1024 * 1024


def padded_rows(count):
    return -(-count // BF16_ROWS) * BF16_ROWS


def passed_along(block, axis, distance):
    size = lax.axis_size(axis)
    return lax.ppermute(block, axis, [(i, (i + distance) % size) for i in range(size)])


def all_along(block, axis):
    return [block] + [passed_along(block, axis, k) for k in range(1, lax.axis_size(axis))]


def from_place(parts, here, place):
    chosen = parts[0]
    for k in range(1, len(parts)):
        chosen = jnp.where(lax.rem(here - k + len(parts), len(parts)) == place, parts[k], chosen)
    return chosen


def field_kernel(dims, scalar_ref, state_ref, land_ref, *rest):
    steps, members, local, forced, vp, fp = dims
    group, out_ref = rest[:members], rest[members]
    varied, lon = state_ref.shape[1:]
    for i in range(local):
        out_ref[i] = jnp.zeros(out_ref.shape[1:], jnp.bfloat16)
        out_ref[i, 0:varied] = state_ref[i]
        for t in range(steps):
            first = (t * local + i) * forced
            force = group[0][first : first + forced, :]
            for k in range(1, members):
                source = lax.rem(scalar_ref[2] - k + members, members)
                force = jnp.where(scalar_ref[3 + t] == source, group[k][first : first + forced, :], force)
            out_ref[i, vp + fp * t : vp + fp * t + forced, :] = force.astype(jnp.bfloat16)
        out_ref[i, vp + fp * steps : vp + fp * steps + 1, :] = land_ref[i : i + 1, :].astype(jnp.bfloat16)


def put_taps(taps, value, row, cols, spacing):
    chans, lon = value.shape
    lane = lax.broadcasted_iota(jnp.int32, (chans, lon), 1)
    zero = jnp.zeros_like(value)
    base = 3 * chans * row
    taps[base : base + chans, cols] = jnp.where(lane >= spacing, pltpu.roll(value, spacing, 1), zero)
    taps[base + chans : base + 2 * chans, cols] = value
    taps[base + 2 * chans : base + 3 * chans, cols] = jnp.where(
        lane < lon - spacing, pltpu.roll(value, lon - spacing, 1), zero
    )


def first_kernel(dims, scalar_ref, enc_ref, settings_ref, scale_w_ref, shift_w_ref, *rest):
    steps, layers, bands, local, members, lon, chans, vp, fp, turns = dims
    fields, rest = rest[:bands], rest[bands:]
    group, rest = rest[: members * turns], rest[members * turns :]
    field_ref, scale_ref, shift_ref, hidden_ref, taps_ref = rest
    band = scalar_ref[1]
    for b in range(bands):
        field_ref[b * local : (b + 1) * local] = from_place([f[...] for f in fields], band, b)

    settings = settings_ref[...]
    numbers = lax.broadcasted_iota(jnp.int32, settings.shape, 0).astype(jnp.float32)
    for m, entry in enumerate(group):
        chosen = entry[entry.shape[0] - 1 : entry.shape[0], 0 : settings.shape[1]]
        row = jnp.sum(jnp.where(numbers == chosen, settings, 0.0), axis=0, keepdims=True)
        cols = slice((m % members) * lon, (m % members + 1) * lon)
        scale = 1.0 + jnp.sum(scale_w_ref[...] * row, axis=1, keepdims=True)
        shift = jnp.sum(shift_w_ref[...] * row, axis=1, keepdims=True)
        scale_ref[m // members, :, cols] = jnp.broadcast_to(scale, (chans, lon))
        shift_ref[m // members, :, cols] = jnp.broadcast_to(shift, (chans, lon))

    if turns == 1:
        for i in range(bands * local):
            land = field_ref[i, vp + fp * steps : vp + fp * steps + 1, :].astype(jnp.float32)
            lifted = jnp.dot(enc_ref[...], field_ref[i, 0 : vp + fp, :], preferred_element_type=jnp.float32)
            for m in range(members):
                cols = slice(m * lon, (m + 1) * lon)
                value = land * (lifted * scale_ref[0, :, cols] + shift_ref[0, :, cols])
                value = value.astype(jnp.bfloat16)
                hidden_ref[i, :, cols] = value
                put_taps(taps_ref, value, i, cols, 1)


def after_kernel(section_ref, earlier_ref, out_ref):
    pass


def after(section, earlier):
    whole = pl.BlockSpec(memory_space=pl.ANY)
    return pl.pallas_call(
        after_kernel,
        out_shape=jax.ShapeDtypeStruct(section.shape, section.dtype),
        in_specs=[whole, whole],
        out_specs=whole,
        input_output_aliases={0: 0},
        compiler_params=pltpu.CompilerParams(vmem_limit_bytes=MIB),
        cost_estimate=pl.CostEstimate(flops=0, bytes_accessed=0, transcendentals=0),
    )(section, earlier)


def window_kernel(dims, scalar_ref, field_ref, scale_ref, shift_ref, enc_ref, dec_ref, *rest):
    steps, layers, bands, local, members, lon, chans, vp, fp, turns = dims
    lat = bands * local
    gains, rest = rest[:layers], rest[layers:]
    hidden, taps = rest[:2]
    blocks, rest = rest[2 : 4 + (layers - 1) * bands], rest[4 + (layers - 1) * bands :]
    final_ref, mean_ref, weights, gain_ref, conv, act, inputs, total, sems = rest[:9]
    here, band = scalar_ref[0], scalar_ref[1]
    taps_wide, wide = 9 * chans, 3 * chans
    part = chans // bands

    pltpu.make_async_copy(blocks[0], weights.at[here, :, pl.ds(0, taps_wide)], sems.at[here]).start()
    pltpu.make_async_copy(blocks[1], weights.at[here, :, pl.ds(taps_wide, chans)], sems.at[here]).start()
    for k in range(1, layers):
        slot = lax.rem(here - k + layers, layers)
        for j in range(bands):
            first = pl.multiple_of(lax.rem(band - j + bands, bands) * part, part)
            pltpu.make_async_copy(
                blocks[2 + (k - 1) * bands + j], weights.at[slot, pl.ds(first, part), :], sems.at[slot]
            ).start()

    if turns > 1:
        hidden, taps = rest[9:]

    eye = lax.broadcasted_iota(jnp.int32, (chans, chans), 0) == lax.broadcasted_iota(jnp.int32, (chans, chans), 1)
    for layer in range(layers):
        row = from_place([g[...] for g in gains], here, layer)
        column = jnp.sum(jnp.where(eye, row, 0.0), axis=1, keepdims=True)
        gain_ref[layer] = jnp.broadcast_to(column, (chans, lon)).astype(jnp.bfloat16)

    def columns(m):
        return slice(m * lon, (m + 1) * lon)

    land = [field_ref[i, vp + fp * steps : vp + fp * steps + 1, :].astype(jnp.float32) for i in range(lat)]

    def put_hidden(i, m, value, layer):
        value = value.astype(jnp.bfloat16)
        hidden[i, :, columns(m)] = value
        if layer is not None:
            put_taps(taps, value, i, columns(m), 2 ** (layer % 3))

    def encode(step, turn):
        for i in range(lat):
            force = field_ref[i, vp + fp * step : vp + fp * (step + 1), :]
            for m in range(members):
                inputs[i, vp : vp + fp, columns(m)] = force
                if step == 0:
                    inputs[i, 0:vp, columns(m)] = field_ref[i, 0:vp, :]
            lifted = jnp.dot(enc_ref[...], inputs[i], preferred_element_type=jnp.float32)
            for m in range(members):
                value = lifted[:, columns(m)] * scale_ref[turn, :, columns(m)] + shift_ref[turn, :, columns(m)]
                put_hidden(i, m, land[i] * value, 0)

    def activate(value, layer):
        centred = value - jnp.sum(value, axis=0, keepdims=True) * (1.0 / chans)
        spread = jnp.sum(centred * centred, axis=0, keepdims=True) * (1.0 / chans)
        normed = (centred * lax.rsqrt(spread + 1e-05)).astype(jnp.bfloat16) * gain_ref[layer]
        inner = normed * (normed * normed * 0.0356774081 + 0.7978845608)
        half = normed * 0.5
        return half + half * jnp.tanh(inner)

    def block(layer, not_yet):
        if not_yet is True:
            pltpu.make_async_copy(weights.at[layer], weights.at[layer], sems.at[layer]).wait()
        elif not_yet is not None:

            @pl.when(not_yet)
            def _():
                pltpu.make_async_copy(weights.at[layer], weights.at[layer], sems.at[layer]).wait()

        for i in range(lat):
            low, high = max(i - 1, 0), min(i + 1, lat - 1)
            conv[i] = jnp.dot(
                weights[layer, :, (low - i + 1) * wide : (high - i + 2) * wide],
                taps[low * wide : (high + 1) * wide, :],
                preferred_element_type=jnp.float32,
            )
        for i in range(lat):
            for m in range(members):
                act[i, :, columns(m)] = activate(conv[i, :, columns(m)], layer)
        for i in range(lat):
            mixed = jnp.dot(weights[layer, :, taps_wide:], act[i], preferred_element_type=jnp.float32)
            for m in range(members):
                kept = hidden[i, :, columns(m)].astype(jnp.float32)
                later = layer + 1 if layer + 1 < layers else None
                put_hidden(i, m, land[i] * (kept + mixed[:, columns(m)]), later)

    varied = final_ref.shape[1]

    def window(turn, first):
        for step in range(steps):
            if step > 0 or turns > 1:
                encode(step, turn)
            for layer in range(layers):
                block(layer, first if step == 0 else None)
            for i in range(lat):
                change = jnp.dot(dec_ref[...], hidden[i], preferred_element_type=jnp.float32)
                for m in range(members):
                    old = field_ref[i, 0:vp, :] if step == 0 else inputs[i, 0:vp, columns(m)]
                    new = old.astype(jnp.float32) + land[i] * change[:, columns(m)]
                    inputs[i, 0:vp, columns(m)] = new.astype(jnp.bfloat16)
        for i in range(local):
            row = band * local + i
            summed = inputs[row, 0:vp, columns(0)].astype(jnp.float32)
            for m in range(1, members):
                summed = summed + inputs[row, 0:vp, columns(m)].astype(jnp.float32)
            if turns == 1:
                mean_ref[:, i, :] = summed[0:varied] * (1.0 / members)
                final_ref[i] = inputs[row, 0:varied, columns(0)]
            else:
                total[i] = jnp.where(first, summed, total[i] + summed)
                mean_ref[:, i, :] = total[i, 0:varied] * (1.0 / (members * turns))

                @pl.when(first)
                def _():
                    final_ref[i] = inputs[row, 0:varied, columns(0)]

    if turns == 1:
        window(0, True)
    else:
        lax.fori_loop(0, turns, lambda turn, _: window(turn, turn == 0), None)


def per_device(
    init_state,
    forcing_slots,
    atmos_owner,
    land_mask,
    param_index,
    settings,
    scale_weight,
    shift_weight,
    encode_weight,
    conv_weight,
    point_weight,
    norm_gain,
    decode_weight,
):
    members, layers, bands = (lax.axis_size(a) for a in ("members", "segment", "rows"))
    here, band = lax.axis_index("segment"), lax.axis_index("rows")
    _, local, varied, lon = init_state.shape
    steps, forced = forcing_slots.shape[2], forcing_slots.shape[4]
    chans = conv_weight.shape[1]
    lat = local * bands
    vp, fp = padded_rows(varied), padded_rows(forced)
    part = chans // bands
    at_once = next(n for n in (4, 2, 1) if members % n == 0)
    turns, wide = members // at_once, at_once * lon
    smem, vmem, whole = (pl.BlockSpec(memory_space=s) for s in (pltpu.SMEM, pltpu.VMEM, pl.ANY))
    small, large = (pltpu.CompilerParams(vmem_limit_bytes=n * MIB) for n in (8, 16 + 2 * layers))
    free = pl.CostEstimate(flops=0, bytes_accessed=0, transcendentals=0)

    mine = jnp.concatenate([conv_weight[0], point_weight[0]], axis=1)
    mine = lax.dynamic_slice_in_dim(mine, band * part, part, 0)
    sections = all_along(mine, "segment")[1:]

    slots = forcing_slots[0, 0].astype(jnp.float32).reshape(-1, lon)
    index_row = jnp.broadcast_to(param_index.astype(jnp.float32)[:, None], (1, lon))
    group = all_along(jnp.concatenate([slots, index_row], axis=0), "members")
    gains = all_along(norm_gain.astype(jnp.float32), "segment")
    scalars = jnp.concatenate(
        [jnp.stack([here, band, lax.axis_index("members")]).astype(jnp.int32), atmos_owner[0]]
    )
    field = pl.pallas_call(
        functools.partial(field_kernel, (steps, members, local, forced, vp, fp)),
        out_shape=jax.ShapeDtypeStruct((local, vp + fp * steps + BF16_ROWS, lon), jnp.bfloat16),
        in_specs=[smem] + [vmem] * (2 + members),
        out_specs=vmem,
        compiler_params=small,
        cost_estimate=free,
    )(scalars, init_state[0], land_mask, *group)
    fields = all_along(field, "rows")

    enc = jnp.pad(encode_weight[:, :varied], ((0, 0), (0, vp - varied)))
    enc = jnp.concatenate([enc, jnp.pad(encode_weight[:, varied:], ((0, 0), (0, fp - forced)))], axis=1)
    dec = jnp.pad(decode_weight, ((0, vp - varied), (0, 0)))
    dims = (steps, layers, bands, local, at_once, lon, chans, vp, fp, turns)
    field, scale, shift, hidden, taps = pl.pallas_call(
        functools.partial(first_kernel, dims),
        out_shape=(
            jax.ShapeDtypeStruct((lat, vp + fp * steps + BF16_ROWS, lon), jnp.bfloat16),
            jax.ShapeDtypeStruct((turns, chans, wide), jnp.float32),
            jax.ShapeDtypeStruct((turns, chans, wide), jnp.float32),
            jax.ShapeDtypeStruct((lat, chans, wide), jnp.bfloat16),
            jax.ShapeDtypeStruct((lat * 3 * chans, wide), jnp.bfloat16),
        ),
        in_specs=[smem] + [vmem] * (4 + bands + members),
        out_specs=(vmem,) * 5,
        compiler_params=small,
        cost_estimate=free,
    )(scalars, enc, settings, scale_weight.T, shift_weight.T, *fields, *group)

    blocks = [conv_weight[0], point_weight[0]]
    for section in sections:
        blocks += all_along(after(section, taps), "rows")

    scratch = [
        pltpu.VMEM((layers, chans, 10 * chans), jnp.bfloat16),
        pltpu.VMEM((layers, chans, lon), jnp.bfloat16),
        pltpu.VMEM((lat, chans, wide), jnp.float32),
        pltpu.VMEM((lat, chans, wide), jnp.bfloat16),
        pltpu.VMEM((lat, vp + fp, wide), jnp.bfloat16),
        pltpu.VMEM((local, vp, lon), jnp.float32),
        pltpu.SemaphoreType.DMA((layers,)),
    ]
    if turns > 1:
        scratch += [pltpu.VMEM(hidden.shape, jnp.bfloat16), pltpu.VMEM(taps.shape, jnp.bfloat16)]
    final, mean = pl.pallas_call(
        functools.partial(window_kernel, dims),
        out_shape=(
            jax.ShapeDtypeStruct((local, varied, lon), jnp.bfloat16),
            jax.ShapeDtypeStruct((varied, local, lon), jnp.float32),
        ),
        in_specs=[smem] + [vmem] * (7 + layers) + [whole] * len(blocks),
        out_specs=(vmem, vmem),
        scratch_shapes=scratch,
        compiler_params=large,
        cost_estimate=free,
    )(scalars, field, scale, shift, enc, dec, *gains, hidden, taps, *blocks)
    return final[None, None], jnp.swapaxes(mean, 0, 1)[None]
def solution(mesh):
    in_specs = (
        P(("groups", "segment"), "rows", None, None),
        P("members", ("groups", "segment"), None, "rows", None, None),
        P(("groups", "segment"), None),
        P(("groups", "rows"), None),
        P(("groups", "members")),
        P(),
        P(),
        P(),
        P(),
        P("segment", None, None),
        P("segment", None, None),
        P("segment", None),
        P(),
    )
    out_specs = (
        P("members", ("groups", "segment"), "rows", None, None),
        P(("groups", "segment"), "rows", None, None),
    )
    return jax.shard_map(
        per_device, mesh=mesh, in_specs=in_specs, out_specs=out_specs, check_vma=False
    )
```

```python
import functools

import jax
import jax.numpy as jnp
from jax import lax
from jax.experimental import pallas as pl
from jax.experimental.pallas import tpu as pltpu
from jax.sharding import PartitionSpec as P

BF16_ROWS = 16
MIB = 1024 * 1024


def padded_rows(count):
    return -(-count // BF16_ROWS) * BF16_ROWS


def passed_along(block, axis, distance):
    size = lax.axis_size(axis)
    return lax.ppermute(block, axis, [(i, (i + distance) % size) for i in range(size)])


def all_along(block, axis):
    return [block] + [passed_along(block, axis, k) for k in range(1, lax.axis_size(axis))]


def from_place(parts, here, place):
    chosen = parts[0]
    for k in range(1, len(parts)):
        chosen = jnp.where(lax.rem(here - k + len(parts), len(parts)) == place, parts[k], chosen)
    return chosen


def pack_kernel(bands, scalar_ref, conv_ref, point_ref, out_ref, sems):
    part, wide = out_ref.shape[0], conv_ref.shape[1]
    rows = pl.ds(pl.multiple_of(scalar_ref[1] * part, part), part)
    copies = [
        pltpu.make_async_copy(conv_ref.at[rows, :], out_ref.at[:, pl.ds(0, wide)], sems.at[0]),
        pltpu.make_async_copy(point_ref.at[rows, :], out_ref.at[:, pl.ds(wide, point_ref.shape[1])], sems.at[1]),
    ]
    for copy in copies:
        copy.start()
    for copy in copies:
        copy.wait()


def field_kernel(dims, scalar_ref, state_ref, land_ref, *rest):
    steps, members, local, forced, vp, fp = dims
    group, out_ref = rest[:members], rest[members]
    varied, lon = state_ref.shape[1:]
    for i in range(local):
        out_ref[i] = jnp.zeros(out_ref.shape[1:], jnp.bfloat16)
        out_ref[i, 0:varied] = state_ref[i]
        for t in range(steps):
            first = (t * local + i) * forced
            force = group[0][first : first + forced, :]
            for k in range(1, members):
                source = lax.rem(scalar_ref[2] - k + members, members)
                force = jnp.where(scalar_ref[3 + t] == source, group[k][first : first + forced, :], force)
            out_ref[i, vp + fp * t : vp + fp * t + forced, :] = force.astype(jnp.bfloat16)
        out_ref[i, vp + fp * steps : vp + fp * steps + 1, :] = land_ref[i : i + 1, :].astype(jnp.bfloat16)


def put_taps(taps, value, row, cols, spacing):
    chans, lon = value.shape
    lane = lax.broadcasted_iota(jnp.int32, (chans, lon), 1)
    zero = jnp.zeros_like(value)
    base = 3 * chans * row
    taps[base : base + chans, cols] = jnp.where(lane >= spacing, pltpu.roll(value, spacing, 1), zero)
    taps[base + chans : base + 2 * chans, cols] = value
    taps[base + 2 * chans : base + 3 * chans, cols] = jnp.where(
        lane < lon - spacing, pltpu.roll(value, lon - spacing, 1), zero
    )


def first_kernel(dims, scalar_ref, enc_ref, settings_ref, scale_w_ref, shift_w_ref, *rest):
    steps, layers, bands, local, members, lon, chans, vp, fp, turns = dims
    fields, rest = rest[:bands], rest[bands:]
    group, rest = rest[: members * turns], rest[members * turns :]
    field_ref, scale_ref, shift_ref, hidden_ref, taps_ref = rest
    band = scalar_ref[1]
    for b in range(bands):
        field_ref[b * local : (b + 1) * local] = from_place([f[...] for f in fields], band, b)

    settings = settings_ref[...]
    numbers = lax.broadcasted_iota(jnp.int32, settings.shape, 0).astype(jnp.float32)
    for m, entry in enumerate(group):
        chosen = entry[entry.shape[0] - 1 : entry.shape[0], 0 : settings.shape[1]]
        row = jnp.sum(jnp.where(numbers == chosen, settings, 0.0), axis=0, keepdims=True)
        cols = slice((m % members) * lon, (m % members + 1) * lon)
        scale = 1.0 + jnp.sum(scale_w_ref[...] * row, axis=1, keepdims=True)
        shift = jnp.sum(shift_w_ref[...] * row, axis=1, keepdims=True)
        scale_ref[m // members, :, cols] = jnp.broadcast_to(scale, (chans, lon))
        shift_ref[m // members, :, cols] = jnp.broadcast_to(shift, (chans, lon))

    if turns == 1:
        for i in range(bands * local):
            land = field_ref[i, vp + fp * steps : vp + fp * steps + 1, :].astype(jnp.float32)
            lifted = jnp.dot(enc_ref[...], field_ref[i, 0 : vp + fp, :], preferred_element_type=jnp.float32)
            for m in range(members):
                cols = slice(m * lon, (m + 1) * lon)
                value = land * (lifted * scale_ref[0, :, cols] + shift_ref[0, :, cols])
                value = value.astype(jnp.bfloat16)
                hidden_ref[i, :, cols] = value
                put_taps(taps_ref, value, i, cols, 1)


def after_kernel(*refs):
    pass


def after(section, *earlier):
    whole = pl.BlockSpec(memory_space=pl.ANY)
    return pl.pallas_call(
        after_kernel,
        out_shape=jax.ShapeDtypeStruct(section.shape, section.dtype),
        in_specs=[whole] * (1 + len(earlier)),
        out_specs=whole,
        input_output_aliases={0: 0},
        compiler_params=pltpu.CompilerParams(vmem_limit_bytes=MIB),
        cost_estimate=pl.CostEstimate(flops=0, bytes_accessed=0, transcendentals=0),
    )(section, *earlier)


def window_kernel(dims, scalar_ref, field_ref, scale_ref, shift_ref, enc_ref, dec_ref, *rest):
    steps, layers, bands, local, members, lon, chans, vp, fp, turns = dims
    lat = bands * local
    gains, rest = rest[:layers], rest[layers:]
    hidden, taps = rest[:2]
    blocks, rest = rest[2 : 4 + (layers - 1) * bands], rest[4 + (layers - 1) * bands :]
    final_ref, mean_ref, weights, gain_ref, conv, act, inputs, total, sems = rest[:9]
    here, band = scalar_ref[0], scalar_ref[1]
    taps_wide, wide = 9 * chans, 3 * chans
    part = chans // bands

    pltpu.make_async_copy(blocks[0], weights.at[here, :, pl.ds(0, taps_wide)], sems.at[here]).start()
    pltpu.make_async_copy(blocks[1], weights.at[here, :, pl.ds(taps_wide, chans)], sems.at[here]).start()
    for k in range(1, layers):
        slot = lax.rem(here - k + layers, layers)
        for j in range(bands):
            first = pl.multiple_of(lax.rem(band - j + bands, bands) * part, part)
            pltpu.make_async_copy(
                blocks[2 + (k - 1) * bands + j], weights.at[slot, pl.ds(first, part), :], sems.at[slot]
            ).start()

    if turns > 1:
        hidden, taps = rest[9:]

    eye = lax.broadcasted_iota(jnp.int32, (chans, chans), 0) == lax.broadcasted_iota(jnp.int32, (chans, chans), 1)
    for layer in range(layers):
        row = from_place([g[...] for g in gains], here, layer)
        column = jnp.sum(jnp.where(eye, row, 0.0), axis=1, keepdims=True)
        gain_ref[layer] = jnp.broadcast_to(column, (chans, lon)).astype(jnp.bfloat16)

    def columns(m):
        return slice(m * lon, (m + 1) * lon)

    land = [field_ref[i, vp + fp * steps : vp + fp * steps + 1, :].astype(jnp.float32) for i in range(lat)]

    def put_hidden(i, m, value, layer):
        value = value.astype(jnp.bfloat16)
        hidden[i, :, columns(m)] = value
        if layer is not None:
            put_taps(taps, value, i, columns(m), 2 ** (layer % 3))

    def encode(step, turn):
        for i in range(lat):
            force = field_ref[i, vp + fp * step : vp + fp * (step + 1), :]
            for m in range(members):
                inputs[i, vp : vp + fp, columns(m)] = force
                if step == 0:
                    inputs[i, 0:vp, columns(m)] = field_ref[i, 0:vp, :]
            lifted = jnp.dot(enc_ref[...], inputs[i], preferred_element_type=jnp.float32)
            for m in range(members):
                value = lifted[:, columns(m)] * scale_ref[turn, :, columns(m)] + shift_ref[turn, :, columns(m)]
                put_hidden(i, m, land[i] * value, 0)

    def activate(value, layer):
        centred = value - jnp.sum(value, axis=0, keepdims=True) * (1.0 / chans)
        spread = jnp.sum(centred * centred, axis=0, keepdims=True) * (1.0 / chans)
        normed = (centred * lax.rsqrt(spread + 1e-05)).astype(jnp.bfloat16) * gain_ref[layer]
        inner = normed * (normed * normed * 0.0356774081 + 0.7978845608)
        half = normed * 0.5
        return half + half * jnp.tanh(inner)

    def block(layer, not_yet):
        if not_yet is True:
            pltpu.make_async_copy(weights.at[layer], weights.at[layer], sems.at[layer]).wait()
        elif not_yet is not None:

            @pl.when(not_yet)
            def _():
                pltpu.make_async_copy(weights.at[layer], weights.at[layer], sems.at[layer]).wait()

        for i in range(lat):
            low, high = max(i - 1, 0), min(i + 1, lat - 1)
            conv[i] = jnp.dot(
                weights[layer, :, (low - i + 1) * wide : (high - i + 2) * wide],
                taps[low * wide : (high + 1) * wide, :],
                preferred_element_type=jnp.float32,
            )
        for i in range(lat):
            mix(i, i, land[i], layer)

    def mix(i, row, sea, layer):
        for m in range(members):
            act[i, :, columns(m)] = activate(conv[i, :, columns(m)], layer)
        mixed = jnp.dot(weights[layer, :, taps_wide:], act[i], preferred_element_type=jnp.float32)
        for m in range(members):
            kept = hidden[row, :, columns(m)].astype(jnp.float32)
            later = layer + 1 if layer + 1 < layers else None
            put_hidden(row, m, sea * (kept + mixed[:, columns(m)]), later)

    def decode(row, sea, step):
        change = jnp.dot(dec_ref[...], hidden[row], preferred_element_type=jnp.float32)
        for m in range(members):
            old = field_ref[row, 0:vp, :] if step == 0 else inputs[row, 0:vp, columns(m)]
            new = old.astype(jnp.float32) + sea * change[:, columns(m)]
            inputs[row, 0:vp, columns(m)] = new.astype(jnp.bfloat16)

    def last_block(layer):
        first = pl.multiple_of((1 - band) * wide, wide)
        conv[0] = jnp.dot(weights[layer, :, pl.ds(first, 2 * wide)], taps[...], preferred_element_type=jnp.float32)
        sea = field_ref[band, vp + fp * steps : vp + fp * steps + 1, :].astype(jnp.float32)
        mix(0, band, sea, layer)
        decode(band, sea, steps - 1)

    varied = final_ref.shape[1]

    def window(turn, first):
        for step in range(steps):
            if step > 0 or turns > 1:
                encode(step, turn)
            own_row = step == steps - 1 and step > 0 and lat == 2 and local == 1
            for layer in range(layers):
                if own_row and layer == layers - 1:
                    last_block(layer)
                else:
                    block(layer, first if step == 0 else None)
            if not own_row:
                for i in range(lat):
                    decode(i, land[i], step)
        for i in range(local):
            row = band * local + i
            summed = inputs[row, 0:vp, columns(0)].astype(jnp.float32)
            for m in range(1, members):
                summed = summed + inputs[row, 0:vp, columns(m)].astype(jnp.float32)
            if turns == 1:
                mean_ref[:, i, :] = summed[0:varied] * (1.0 / members)
                final_ref[i] = inputs[row, 0:varied, columns(0)]
            else:
                total[i] = jnp.where(first, summed, total[i] + summed)
                mean_ref[:, i, :] = total[i, 0:varied] * (1.0 / (members * turns))

                @pl.when(first)
                def _():
                    final_ref[i] = inputs[row, 0:varied, columns(0)]

    if turns == 1:
        window(0, True)
    else:
        lax.fori_loop(0, turns, lambda turn, _: window(turn, turn == 0), None)


def per_device(
    init_state,
    forcing_slots,
    atmos_owner,
    land_mask,
    param_index,
    settings,
    scale_weight,
    shift_weight,
    encode_weight,
    conv_weight,
    point_weight,
    norm_gain,
    decode_weight,
):
    members, layers, bands = (lax.axis_size(a) for a in ("members", "segment", "rows"))
    here, band = lax.axis_index("segment"), lax.axis_index("rows")
    _, local, varied, lon = init_state.shape
    steps, forced = forcing_slots.shape[2], forcing_slots.shape[4]
    chans = conv_weight.shape[1]
    lat = local * bands
    vp, fp = padded_rows(varied), padded_rows(forced)
    part = chans // bands
    at_once = next(n for n in (4, 2, 1) if members % n == 0)
    turns, wide = members // at_once, at_once * lon
    smem, vmem, whole = (pl.BlockSpec(memory_space=s) for s in (pltpu.SMEM, pltpu.VMEM, pl.ANY))
    small, large = (pltpu.CompilerParams(vmem_limit_bytes=n * MIB) for n in (8, 16 + 2 * layers))
    free = pl.CostEstimate(flops=0, bytes_accessed=0, transcendentals=0)

    places = jnp.stack([here, band, lax.axis_index("members")]).astype(jnp.int32)
    mine = pl.pallas_call(
        functools.partial(pack_kernel, bands),
        out_shape=jax.ShapeDtypeStruct((part, 10 * chans), jnp.bfloat16),
        in_specs=[smem, whole, whole],
        out_specs=whole,
        scratch_shapes=[pltpu.SemaphoreType.DMA((2,))],
        compiler_params=pltpu.CompilerParams(vmem_limit_bytes=MIB),
        cost_estimate=free,
    )(places, conv_weight[0], point_weight[0])
    sections = all_along(mine, "segment")[1:]

    slots = forcing_slots[0, 0].astype(jnp.float32).reshape(-1, lon)
    index_row = jnp.broadcast_to(param_index.astype(jnp.float32)[:, None], (1, lon))
    group = all_along(jnp.concatenate([slots, index_row], axis=0), "members")
    gains = all_along(norm_gain.astype(jnp.float32), "segment")
    scalars = jnp.concatenate([places, atmos_owner[0]])
    field = pl.pallas_call(
        functools.partial(field_kernel, (steps, members, local, forced, vp, fp)),
        out_shape=jax.ShapeDtypeStruct((local, vp + fp * steps + BF16_ROWS, lon), jnp.bfloat16),
        in_specs=[smem] + [vmem] * (2 + members),
        out_specs=vmem,
        compiler_params=small,
        cost_estimate=free,
    )(scalars, init_state[0], land_mask, *group)
    fields = all_along(field, "rows")

    enc = jnp.pad(encode_weight[:, :varied], ((0, 0), (0, vp - varied)))
    enc = jnp.concatenate([enc, jnp.pad(encode_weight[:, varied:], ((0, 0), (0, fp - forced)))], axis=1)
    dec = jnp.pad(decode_weight, ((0, vp - varied), (0, 0)))
    dims = (steps, layers, bands, local, at_once, lon, chans, vp, fp, turns)
    field, scale, shift, hidden, taps = pl.pallas_call(
        functools.partial(first_kernel, dims),
        out_shape=(
            jax.ShapeDtypeStruct((lat, vp + fp * steps + BF16_ROWS, lon), jnp.bfloat16),
            jax.ShapeDtypeStruct((turns, chans, wide), jnp.float32),
            jax.ShapeDtypeStruct((turns, chans, wide), jnp.float32),
            jax.ShapeDtypeStruct((lat, chans, wide), jnp.bfloat16),
            jax.ShapeDtypeStruct((lat * 3 * chans, wide), jnp.bfloat16),
        ),
        in_specs=[smem] + [vmem] * (4 + bands + members),
        out_specs=(vmem,) * 5,
        compiler_params=small,
        cost_estimate=free,
    )(scalars, enc, settings, scale_weight.T, shift_weight.T, *fields, *group)

    blocks = [conv_weight[0], point_weight[0]]
    for section in sections:
        blocks += all_along(after(section, taps, *gains), "rows")

    scratch = [
        pltpu.VMEM((layers, chans, 10 * chans), jnp.bfloat16),
        pltpu.VMEM((layers, chans, lon), jnp.bfloat16),
        pltpu.VMEM((lat, chans, wide), jnp.float32),
        pltpu.VMEM((lat, chans, wide), jnp.bfloat16),
        pltpu.VMEM((lat, vp + fp, wide), jnp.bfloat16),
        pltpu.VMEM((local, vp, lon), jnp.float32),
        pltpu.SemaphoreType.DMA((layers,)),
    ]
    if turns > 1:
        scratch += [pltpu.VMEM(hidden.shape, jnp.bfloat16), pltpu.VMEM(taps.shape, jnp.bfloat16)]
    final, mean = pl.pallas_call(
        functools.partial(window_kernel, dims),
        out_shape=(
            jax.ShapeDtypeStruct((local, varied, lon), jnp.bfloat16),
            jax.ShapeDtypeStruct((varied, local, lon), jnp.float32),
        ),
        in_specs=[smem] + [vmem] * (7 + layers) + [whole] * len(blocks),
        out_specs=(vmem, vmem),
        scratch_shapes=scratch,
        compiler_params=large,
        cost_estimate=free,
    )(scalars, field, scale, shift, enc, dec, *gains, hidden, taps, *blocks)
    return final[None, None], jnp.swapaxes(mean, 0, 1)[None]
def solution(mesh):
    in_specs = (
        P(("groups", "segment"), "rows", None, None),
        P("members", ("groups", "segment"), None, "rows", None, None),
        P(("groups", "segment"), None),
        P(("groups", "rows"), None),
        P(("groups", "members")),
        P(),
        P(),
        P(),
        P(),
        P("segment", None, None),
        P("segment", None, None),
        P("segment", None),
        P(),
    )
    out_specs = (
        P("members", ("groups", "segment"), "rows", None, None),
        P(("groups", "segment"), "rows", None, None),
    )
    return jax.shard_map(
        per_device, mesh=mesh, in_specs=in_specs, out_specs=out_specs, check_vma=False
    )
```

```python
import functools

import jax
import jax.numpy as jnp
from jax import lax
from jax.experimental import pallas as pl
from jax.experimental.pallas import tpu as pltpu
from jax.sharding import PartitionSpec as P

BF16_ROWS = 16
MIB = 1024 * 1024


def padded_rows(count):
    return -(-count // BF16_ROWS) * BF16_ROWS


def passed_along(block, axis, distance):
    size = lax.axis_size(axis)
    return lax.ppermute(block, axis, [(i, (i + distance) % size) for i in range(size)])


def all_along(block, axis):
    return [block] + [passed_along(block, axis, k) for k in range(1, lax.axis_size(axis))]


def from_place(parts, here, place):
    chosen = parts[0]
    for k in range(1, len(parts)):
        chosen = jnp.where(lax.rem(here - k + len(parts), len(parts)) == place, parts[k], chosen)
    return chosen


def pack_kernel(scalar_ref, conv_ref, point_ref, relayed_ref, direct_ref, sems):
    part, wide, share = direct_ref.shape[0], conv_ref.shape[1], relayed_ref.shape[1]
    rest = wide + point_ref.shape[1] - direct_ref.shape[1]
    rows = pl.ds(pl.multiple_of(scalar_ref[1] * part, part), part)
    mine = pl.ds(pl.multiple_of(scalar_ref[3] * share, 128), share)
    copies = [
        pltpu.make_async_copy(conv_ref.at[rows, mine], relayed_ref, sems.at[0]),
        pltpu.make_async_copy(
            conv_ref.at[rows, pl.ds(rest, wide - rest)], direct_ref.at[:, pl.ds(0, wide - rest)], sems.at[1]
        ),
        pltpu.make_async_copy(
            point_ref.at[rows, :], direct_ref.at[:, pl.ds(wide - rest, point_ref.shape[1])], sems.at[2]
        ),
    ]
    for copy in copies:
        copy.start()
    for copy in copies:
        copy.wait()


def field_kernel(dims, scalar_ref, state_ref, land_ref, *rest):
    steps, members, local, forced, vp, fp = dims
    group, out_ref = rest[:members], rest[members]
    varied, lon = state_ref.shape[1:]
    for i in range(local):
        out_ref[i] = jnp.zeros(out_ref.shape[1:], jnp.bfloat16)
        out_ref[i, 0:varied] = state_ref[i]
        for t in range(steps):
            first = (t * local + i) * forced
            force = group[0][first : first + forced, :]
            for k in range(1, members):
                source = lax.rem(scalar_ref[2] - k + members, members)
                force = jnp.where(scalar_ref[4 + t] == source, group[k][first : first + forced, :], force)
            out_ref[i, vp + fp * t : vp + fp * t + forced, :] = force.astype(jnp.bfloat16)
        out_ref[i, vp + fp * steps : vp + fp * steps + 1, :] = land_ref[i : i + 1, :].astype(jnp.bfloat16)


def put_taps(taps, value, row, cols, spacing):
    chans, lon = value.shape
    lane = lax.broadcasted_iota(jnp.int32, (chans, lon), 1)
    zero = jnp.zeros_like(value)
    base = 3 * chans * row
    taps[base : base + chans, cols] = jnp.where(lane >= spacing, pltpu.roll(value, spacing, 1), zero)
    taps[base + chans : base + 2 * chans, cols] = value
    taps[base + 2 * chans : base + 3 * chans, cols] = jnp.where(
        lane < lon - spacing, pltpu.roll(value, lon - spacing, 1), zero
    )


def first_kernel(dims, scalar_ref, enc_ref, settings_ref, scale_w_ref, shift_w_ref, *rest):
    steps, layers, bands, local, members, lon, chans, vp, fp, turns = dims
    fields, rest = rest[:bands], rest[bands:]
    group, rest = rest[: members * turns], rest[members * turns :]
    field_ref, scale_ref, shift_ref, hidden_ref, taps_ref = rest
    band = scalar_ref[1]
    for b in range(bands):
        field_ref[b * local : (b + 1) * local] = from_place([f[...] for f in fields], band, b)

    settings = settings_ref[...]
    numbers = lax.broadcasted_iota(jnp.int32, settings.shape, 0).astype(jnp.float32)
    for m, entry in enumerate(group):
        chosen = entry[entry.shape[0] - 1 : entry.shape[0], 0 : settings.shape[1]]
        row = jnp.sum(jnp.where(numbers == chosen, settings, 0.0), axis=0, keepdims=True)
        cols = slice((m % members) * lon, (m % members + 1) * lon)
        scale = 1.0 + jnp.sum(scale_w_ref[...] * row, axis=1, keepdims=True)
        shift = jnp.sum(shift_w_ref[...] * row, axis=1, keepdims=True)
        scale_ref[m // members, :, cols] = jnp.broadcast_to(scale, (chans, lon))
        shift_ref[m // members, :, cols] = jnp.broadcast_to(shift, (chans, lon))

    if turns == 1:
        for i in range(bands * local):
            land = field_ref[i, vp + fp * steps : vp + fp * steps + 1, :].astype(jnp.float32)
            lifted = jnp.dot(enc_ref[...], field_ref[i, 0 : vp + fp, :], preferred_element_type=jnp.float32)
            for m in range(members):
                cols = slice(m * lon, (m + 1) * lon)
                value = land * (lifted * scale_ref[0, :, cols] + shift_ref[0, :, cols])
                value = value.astype(jnp.bfloat16)
                hidden_ref[i, :, cols] = value
                put_taps(taps_ref, value, i, cols, 1)


def after_kernel(*refs):
    pass


def after(section, *earlier):
    whole = pl.BlockSpec(memory_space=pl.ANY)
    return pl.pallas_call(
        after_kernel,
        out_shape=jax.ShapeDtypeStruct(section.shape, section.dtype),
        in_specs=[whole] * (1 + len(earlier)),
        out_specs=whole,
        input_output_aliases={0: 0},
        compiler_params=pltpu.CompilerParams(vmem_limit_bytes=MIB),
        cost_estimate=pl.CostEstimate(flops=0, bytes_accessed=0, transcendentals=0),
    )(section, *earlier)


def window_kernel(dims, scalar_ref, field_ref, scale_ref, shift_ref, enc_ref, dec_ref, *rest):
    steps, layers, bands, local, members, lon, chans, vp, fp, turns, groups = dims
    lat = bands * local
    gains, rest = rest[:layers], rest[layers:]
    hidden, taps = rest[:2]
    pieces = 2 + (layers - 1) * (groups + 1) * bands
    blocks, rest = rest[2 : 2 + pieces], rest[2 + pieces :]
    final_ref, mean_ref, weights, gain_ref, conv, act, inputs, total, sems = rest[:9]
    here, band = scalar_ref[0], scalar_ref[1]
    taps_wide, wide = 9 * chans, 3 * chans
    part = chans // bands

    pltpu.make_async_copy(blocks[0], weights.at[here, :, pl.ds(0, taps_wide)], sems.at[here]).start()
    pltpu.make_async_copy(blocks[1], weights.at[here, :, pl.ds(taps_wide, chans)], sems.at[here]).start()
    share = 4 * chans // groups
    for k in range(1, layers):
        slot = lax.rem(here - k + layers, layers)
        for g in range(groups + 1):
            if g < groups:
                place = lax.rem(scalar_ref[3] - g + groups, groups)
                cols = pl.ds(pl.multiple_of(place * share, 128), share)
            else:
                cols = pl.ds(groups * share, 10 * chans - groups * share)
            for j in range(bands):
                rows = pl.ds(pl.multiple_of(lax.rem(band - j + bands, bands) * part, part), part)
                block = blocks[2 + ((k - 1) * (groups + 1) + g) * bands + j]
                pltpu.make_async_copy(block, weights.at[slot, rows, cols], sems.at[slot]).start()

    if turns > 1:
        hidden, taps = rest[9:]

    eye = lax.broadcasted_iota(jnp.int32, (chans, chans), 0) == lax.broadcasted_iota(jnp.int32, (chans, chans), 1)
    for layer in range(layers):
        row = from_place([g[...] for g in gains], here, layer)
        column = jnp.sum(jnp.where(eye, row, 0.0), axis=1, keepdims=True)
        gain_ref[layer] = jnp.broadcast_to(column, (chans, lon)).astype(jnp.bfloat16)

    def columns(m):
        return slice(m * lon, (m + 1) * lon)

    land = [field_ref[i, vp + fp * steps : vp + fp * steps + 1, :].astype(jnp.float32) for i in range(lat)]

    def put_hidden(i, m, value, layer):
        value = value.astype(jnp.bfloat16)
        hidden[i, :, columns(m)] = value
        if layer is not None:
            put_taps(taps, value, i, columns(m), 2 ** (layer % 3))

    def encode(step, turn):
        for i in range(lat):
            force = field_ref[i, vp + fp * step : vp + fp * (step + 1), :]
            for m in range(members):
                inputs[i, vp : vp + fp, columns(m)] = force
                if step == 0:
                    inputs[i, 0:vp, columns(m)] = field_ref[i, 0:vp, :]
            lifted = jnp.dot(enc_ref[...], inputs[i], preferred_element_type=jnp.float32)
            for m in range(members):
                value = lifted[:, columns(m)] * scale_ref[turn, :, columns(m)] + shift_ref[turn, :, columns(m)]
                put_hidden(i, m, land[i] * value, 0)

    def activate(value, layer):
        centred = value - jnp.sum(value, axis=0, keepdims=True) * (1.0 / chans)
        spread = jnp.sum(centred * centred, axis=0, keepdims=True) * (1.0 / chans)
        normed = (centred * lax.rsqrt(spread + 1e-05)).astype(jnp.bfloat16) * gain_ref[layer]
        inner = normed * (normed * normed * 0.0356774081 + 0.7978845608)
        half = normed * 0.5
        return half + half * jnp.tanh(inner)

    def block(layer, not_yet):
        if not_yet is True:
            pltpu.make_async_copy(weights.at[layer], weights.at[layer], sems.at[layer]).wait()
        elif not_yet is not None:

            @pl.when(not_yet)
            def _():
                pltpu.make_async_copy(weights.at[layer], weights.at[layer], sems.at[layer]).wait()

        for i in range(lat):
            low, high = max(i - 1, 0), min(i + 1, lat - 1)
            conv[i] = jnp.dot(
                weights[layer, :, (low - i + 1) * wide : (high - i + 2) * wide],
                taps[low * wide : (high + 1) * wide, :],
                preferred_element_type=jnp.float32,
            )
        for i in range(lat):
            mix(i, i, land[i], layer)

    def mix(i, row, sea, layer):
        for m in range(members):
            act[i, :, columns(m)] = activate(conv[i, :, columns(m)], layer)
        mixed = jnp.dot(weights[layer, :, taps_wide:], act[i], preferred_element_type=jnp.float32)
        for m in range(members):
            kept = hidden[row, :, columns(m)].astype(jnp.float32)
            later = layer + 1 if layer + 1 < layers else None
            put_hidden(row, m, sea * (kept + mixed[:, columns(m)]), later)

    def decode(row, sea, step):
        change = jnp.dot(dec_ref[...], hidden[row], preferred_element_type=jnp.float32)
        for m in range(members):
            old = field_ref[row, 0:vp, :] if step == 0 else inputs[row, 0:vp, columns(m)]
            new = old.astype(jnp.float32) + sea * change[:, columns(m)]
            inputs[row, 0:vp, columns(m)] = new.astype(jnp.bfloat16)

    def last_block(layer):
        first = pl.multiple_of((1 - band) * wide, wide)
        conv[0] = jnp.dot(weights[layer, :, pl.ds(first, 2 * wide)], taps[...], preferred_element_type=jnp.float32)
        sea = field_ref[band, vp + fp * steps : vp + fp * steps + 1, :].astype(jnp.float32)
        mix(0, band, sea, layer)
        decode(band, sea, steps - 1)

    varied = final_ref.shape[1]

    def window(turn, first):
        for step in range(steps):
            if step > 0 or turns > 1:
                encode(step, turn)
            own_row = step == steps - 1 and step > 0 and lat == 2 and local == 1
            for layer in range(layers):
                if own_row and layer == layers - 1:
                    last_block(layer)
                else:
                    block(layer, first if step == 0 else None)
            if not own_row:
                for i in range(lat):
                    decode(i, land[i], step)
        for i in range(local):
            row = band * local + i
            summed = inputs[row, 0:vp, columns(0)].astype(jnp.float32)
            for m in range(1, members):
                summed = summed + inputs[row, 0:vp, columns(m)].astype(jnp.float32)
            if turns == 1:
                mean_ref[:, i, :] = summed[0:varied] * (1.0 / members)
                final_ref[i] = inputs[row, 0:varied, columns(0)]
            else:
                total[i] = jnp.where(first, summed, total[i] + summed)
                mean_ref[:, i, :] = total[i, 0:varied] * (1.0 / (members * turns))

                @pl.when(first)
                def _():
                    final_ref[i] = inputs[row, 0:varied, columns(0)]

    if turns == 1:
        window(0, True)
    else:
        lax.fori_loop(0, turns, lambda turn, _: window(turn, turn == 0), None)


def per_device(
    init_state,
    forcing_slots,
    atmos_owner,
    land_mask,
    param_index,
    settings,
    scale_weight,
    shift_weight,
    encode_weight,
    conv_weight,
    point_weight,
    norm_gain,
    decode_weight,
):
    members, layers, bands = (lax.axis_size(a) for a in ("members", "segment", "rows"))
    here, band = lax.axis_index("segment"), lax.axis_index("rows")
    _, local, varied, lon = init_state.shape
    steps, forced = forcing_slots.shape[2], forcing_slots.shape[4]
    chans = conv_weight.shape[1]
    lat = local * bands
    vp, fp = padded_rows(varied), padded_rows(forced)
    part = chans // bands
    at_once = next(n for n in (4, 2, 1) if members % n == 0)
    turns, wide = members // at_once, at_once * lon
    smem, vmem, whole = (pl.BlockSpec(memory_space=s) for s in (pltpu.SMEM, pltpu.VMEM, pl.ANY))
    small, large = (pltpu.CompilerParams(vmem_limit_bytes=n * MIB) for n in (8, 16 + 2 * layers))
    free = pl.CostEstimate(flops=0, bytes_accessed=0, transcendentals=0)

    groups = lax.axis_size("groups")
    share = 4 * chans // groups
    places = [here, band, lax.axis_index("members"), lax.axis_index("groups")]
    places = jnp.stack(places).astype(jnp.int32)
    hbm = pl.BlockSpec(memory_space=pltpu.HBM)
    relayed, direct = pl.pallas_call(
        pack_kernel,
        out_shape=(
            jax.ShapeDtypeStruct((part, share), jnp.bfloat16),
            jax.ShapeDtypeStruct((part, 10 * chans - groups * share), jnp.bfloat16),
        ),
        in_specs=[smem, hbm, hbm],
        out_specs=(whole, whole),
        scratch_shapes=[pltpu.SemaphoreType.DMA((3,))],
        compiler_params=pltpu.CompilerParams(vmem_limit_bytes=MIB),
        cost_estimate=free,
    )(places, conv_weight[0], point_weight[0])
    relayed = all_along(relayed, "segment")[1:]
    direct = all_along(direct, "segment")[1:]

    slots = forcing_slots[0, 0].astype(jnp.float32).reshape(-1, lon)
    index_row = jnp.broadcast_to(param_index.astype(jnp.float32)[:, None], (1, lon))
    group = all_along(jnp.concatenate([slots, index_row], axis=0), "members")
    gains = all_along(norm_gain.astype(jnp.float32), "segment")
    scalars = jnp.concatenate([places, atmos_owner[0]])
    field = pl.pallas_call(
        functools.partial(field_kernel, (steps, members, local, forced, vp, fp)),
        out_shape=jax.ShapeDtypeStruct((local, vp + fp * steps + BF16_ROWS, lon), jnp.bfloat16),
        in_specs=[smem] + [vmem] * (2 + members),
        out_specs=vmem,
        compiler_params=small,
        cost_estimate=free,
    )(scalars, init_state[0], land_mask, *group)
    fields = all_along(field, "rows")

    enc = jnp.pad(encode_weight[:, :varied], ((0, 0), (0, vp - varied)))
    enc = jnp.concatenate([enc, jnp.pad(encode_weight[:, varied:], ((0, 0), (0, fp - forced)))], axis=1)
    dec = jnp.pad(decode_weight, ((0, vp - varied), (0, 0)))
    dims = (steps, layers, bands, local, at_once, lon, chans, vp, fp, turns)
    field, scale, shift, hidden, taps = pl.pallas_call(
        functools.partial(first_kernel, dims),
        out_shape=(
            jax.ShapeDtypeStruct((lat, vp + fp * steps + BF16_ROWS, lon), jnp.bfloat16),
            jax.ShapeDtypeStruct((turns, chans, wide), jnp.float32),
            jax.ShapeDtypeStruct((turns, chans, wide), jnp.float32),
            jax.ShapeDtypeStruct((lat, chans, wide), jnp.bfloat16),
            jax.ShapeDtypeStruct((lat * 3 * chans, wide), jnp.bfloat16),
        ),
        in_specs=[smem] + [vmem] * (4 + bands + members),
        out_specs=(vmem,) * 5,
        compiler_params=small,
        cost_estimate=free,
    )(scalars, enc, settings, scale_weight.T, shift_weight.T, *fields, *group)

    blocks = [conv_weight[0], point_weight[0]]
    for k in range(layers - 1):
        shares = all_along(relayed[k], "groups")
        for shared in shares:
            blocks += all_along(shared, "rows")
        blocks += all_along(after(direct[k], taps, *gains, *shares[1:]), "rows")

    scratch = [
        pltpu.VMEM((layers, chans, 10 * chans), jnp.bfloat16),
        pltpu.VMEM((layers, chans, lon), jnp.bfloat16),
        pltpu.VMEM((lat, chans, wide), jnp.float32),
        pltpu.VMEM((lat, chans, wide), jnp.bfloat16),
        pltpu.VMEM((lat, vp + fp, wide), jnp.bfloat16),
        pltpu.VMEM((local, vp, lon), jnp.float32),
        pltpu.SemaphoreType.DMA((layers,)),
    ]
    if turns > 1:
        scratch += [pltpu.VMEM(hidden.shape, jnp.bfloat16), pltpu.VMEM(taps.shape, jnp.bfloat16)]
    final, mean = pl.pallas_call(
        functools.partial(window_kernel, dims + (groups,)),
        out_shape=(
            jax.ShapeDtypeStruct((local, varied, lon), jnp.bfloat16),
            jax.ShapeDtypeStruct((varied, local, lon), jnp.float32),
        ),
        in_specs=[smem] + [vmem] * (7 + layers) + [whole] * len(blocks),
        out_specs=(vmem, vmem),
        scratch_shapes=scratch,
        compiler_params=large,
        cost_estimate=free,
    )(scalars, field, scale, shift, enc, dec, *gains, hidden, taps, *blocks)
    return final[None, None], jnp.swapaxes(mean, 0, 1)[None]
def solution(mesh):
    in_specs = (
        P(("groups", "segment"), "rows", None, None),
        P("members", ("groups", "segment"), None, "rows", None, None),
        P(("groups", "segment"), None),
        P(("groups", "rows"), None),
        P(("groups", "members")),
        P(),
        P(),
        P(),
        P(),
        P("segment", None, None),
        P("segment", None, None),
        P("segment", None),
        P(),
    )
    out_specs = (
        P("members", ("groups", "segment"), "rows", None, None),
        P(("groups", "segment"), "rows", None, None),
    )
    return jax.shard_map(
        per_device, mesh=mesh, in_specs=in_specs, out_specs=out_specs, check_vma=False
    )
```

```python
import functools

import jax
import jax.numpy as jnp
from jax import lax
from jax.experimental import pallas as pl
from jax.experimental.pallas import tpu as pltpu
from jax.sharding import PartitionSpec as P

BF16_ROWS = 16
LANES = 128
MIB = 1024 * 1024


def padded_rows(count):
    return -(-count // BF16_ROWS) * BF16_ROWS


def passed_along(block, axis, distance):
    size = lax.axis_size(axis)
    return lax.ppermute(block, axis, [(i, (i + distance) % size) for i in range(size)])


def all_along(block, axis):
    return [block] + [passed_along(block, axis, k) for k in range(1, lax.axis_size(axis))]


def from_place(parts, here, place):
    chosen = parts[0]
    for k in range(1, len(parts)):
        chosen = jnp.where(lax.rem(here - k + len(parts), len(parts)) == place, parts[k], chosen)
    return chosen


def run_copies(*copies):
    for copy in copies:
        copy.start()
    for copy in copies:
        copy.wait()


def pack_kernel(scalar_ref, gain_ref, conv_ref, point_ref, slots_ref, *rest):
    relayed_ref, middle_ref, direct_ref, spread_ref, group_ref, slots, gain, sems = rest
    part, share = relayed_ref.shape
    wide, chans = conv_ref.shape[1], point_ref.shape[1]
    left = direct_ref.shape[1] - chans - LANES
    rows = pl.ds(pl.multiple_of(scalar_ref[1] * part, part), part)
    mine = pl.ds(pl.multiple_of(scalar_ref[3] * share, LANES), share)
    small = [
        pltpu.make_async_copy(gain_ref, gain, sems.at[0]),
        pltpu.make_async_copy(slots_ref, slots, sems.at[1]),
    ]
    large = [
        pltpu.make_async_copy(conv_ref.at[rows, mine], relayed_ref, sems.at[2]),
        pltpu.make_async_copy(
            conv_ref.at[rows, pl.ds(wide - left - middle_ref.shape[1], middle_ref.shape[1])], middle_ref, sems.at[6]
        ),
        pltpu.make_async_copy(conv_ref.at[rows, pl.ds(wide - left, left)], direct_ref.at[:, pl.ds(0, left)], sems.at[3]),
        pltpu.make_async_copy(point_ref.at[rows, :], direct_ref.at[:, pl.ds(left, chans)], sems.at[4]),
    ]
    for copy in small + large:
        copy.start()
    for copy in small:
        copy.wait()
    eye = lax.broadcasted_iota(jnp.int32, (chans, chans), 0) == lax.broadcasted_iota(jnp.int32, (chans, chans), 1)
    column = jnp.sum(jnp.where(eye, gain[...].astype(jnp.float32), 0.0), axis=1, keepdims=True)
    spread_ref[...] = jnp.broadcast_to(column, (chans, LANES)).astype(jnp.bfloat16)
    large.append(
        pltpu.make_async_copy(spread_ref.at[rows, :], direct_ref.at[:, pl.ds(left + chans, LANES)], sems.at[5])
    )
    large[-1].start()
    count = slots.shape[0]
    group_ref[0:count] = slots[...].astype(jnp.float32)
    index = jnp.full((1, group_ref.shape[1]), scalar_ref[4], jnp.int32)
    group_ref[count : count + 1] = index.astype(jnp.float32)
    for copy in large:
        copy.wait()


def field_kernel(dims, scalar_ref, state_ref, land_ref, *rest):
    steps, members, local, forced, vp, fp = dims
    group, out_ref = rest[:members], rest[members]
    varied, lon = state_ref.shape[1:]
    for i in range(local):
        out_ref[i] = jnp.zeros(out_ref.shape[1:], jnp.bfloat16)
        out_ref[i, 0:varied] = state_ref[i]
        for t in range(steps):
            first = (t * local + i) * forced
            force = group[0][first : first + forced, :]
            for k in range(1, members):
                source = lax.rem(scalar_ref[2] - k + members, members)
                force = jnp.where(scalar_ref[5 + t] == source, group[k][first : first + forced, :], force)
            out_ref[i, vp + fp * t : vp + fp * t + forced, :] = force.astype(jnp.bfloat16)
        out_ref[i, vp + fp * steps : vp + fp * steps + 1, :] = land_ref[i : i + 1, :].astype(jnp.bfloat16)


def put_taps(taps, value, row, cols, spacing):
    chans, lon = value.shape
    lane = lax.broadcasted_iota(jnp.int32, (chans, lon), 1)
    zero = jnp.zeros_like(value)
    base = 3 * chans * row
    taps[base : base + chans, cols] = jnp.where(lane >= spacing, pltpu.roll(value, spacing, 1), zero)
    taps[base + chans : base + 2 * chans, cols] = value
    taps[base + 2 * chans : base + 3 * chans, cols] = jnp.where(
        lane < lon - spacing, pltpu.roll(value, lon - spacing, 1), zero
    )


def first_kernel(dims, scalar_ref, enc_w_ref, dec_w_ref, settings_ref, scale_w_ref, shift_w_ref, *rest):
    steps, layers, bands, local, members, lon, chans, vp, fp, turns = dims
    fields, rest = rest[:bands], rest[bands:]
    group, rest = rest[: members * turns], rest[members * turns :]
    field_ref, scale_ref, shift_ref, enc_ref, dec_ref, hidden_ref, taps_ref = rest
    varied = dec_w_ref.shape[0]
    forced = enc_w_ref.shape[1] - varied
    enc_ref[...] = jnp.zeros(enc_ref.shape, enc_ref.dtype)
    enc_ref[:, 0:varied] = enc_w_ref[:, 0:varied]
    enc_ref[:, vp : vp + forced] = enc_w_ref[:, varied : varied + forced]
    dec_ref[...] = jnp.zeros(dec_ref.shape, dec_ref.dtype)
    dec_ref[0:varied, :] = dec_w_ref[...]
    band = scalar_ref[1]
    for b in range(bands):
        field_ref[b * local : (b + 1) * local] = from_place([f[...] for f in fields], band, b)

    settings = settings_ref[...]
    numbers = lax.broadcasted_iota(jnp.int32, settings.shape, 0).astype(jnp.float32)
    for m, entry in enumerate(group):
        chosen = entry[entry.shape[0] - 1 : entry.shape[0], 0 : settings.shape[1]]
        row = jnp.sum(jnp.where(numbers == chosen, settings, 0.0), axis=0, keepdims=True)
        cols = slice((m % members) * lon, (m % members + 1) * lon)
        scale = 1.0 + jnp.sum(scale_w_ref[...] * row, axis=1, keepdims=True)
        shift = jnp.sum(shift_w_ref[...] * row, axis=1, keepdims=True)
        scale_ref[m // members, :, cols] = jnp.broadcast_to(scale, (chans, lon))
        shift_ref[m // members, :, cols] = jnp.broadcast_to(shift, (chans, lon))

    if turns == 1:
        for i in range(bands * local):
            land = field_ref[i, vp + fp * steps : vp + fp * steps + 1, :].astype(jnp.float32)
            lifted = jnp.dot(enc_ref[...], field_ref[i, 0 : vp + fp, :], preferred_element_type=jnp.float32)
            for m in range(members):
                cols = slice(m * lon, (m + 1) * lon)
                value = land * (lifted * scale_ref[0, :, cols] + shift_ref[0, :, cols])
                value = value.astype(jnp.bfloat16)
                hidden_ref[i, :, cols] = value
                put_taps(taps_ref, value, i, cols, 1)


def after_kernel(*refs):
    pass


def after(section, *earlier):
    whole = pl.BlockSpec(memory_space=pl.ANY)
    return pl.pallas_call(
        after_kernel,
        out_shape=jax.ShapeDtypeStruct(section.shape, section.dtype),
        in_specs=[whole] * (1 + len(earlier)),
        out_specs=whole,
        input_output_aliases={0: 0},
        compiler_params=pltpu.CompilerParams(vmem_limit_bytes=MIB),
        cost_estimate=pl.CostEstimate(flops=0, bytes_accessed=0, transcendentals=0),
    )(section, *earlier)


def window_kernel(dims, scalar_ref, field_ref, scale_ref, shift_ref, enc_ref, dec_ref, *rest):
    steps, layers, bands, local, members, lon, chans, vp, fp, turns, groups = dims
    lat = bands * local
    hidden, taps = rest[:2]
    pieces = 3 + (layers - 1) * (groups + 2) * bands
    blocks, rest = rest[2 : 2 + pieces], rest[2 + pieces :]
    final_ref, mean_ref, weights, conv, act, inputs, total, sems = rest[:8]
    here, band = scalar_ref[0], scalar_ref[1]
    taps_wide, wide = 9 * chans, 3 * chans
    part = chans // bands

    pltpu.make_async_copy(blocks[0], weights.at[here, :, pl.ds(0, taps_wide)], sems.at[here]).start()
    pltpu.make_async_copy(blocks[1], weights.at[here, :, pl.ds(taps_wide, chans)], sems.at[here]).start()
    pltpu.make_async_copy(blocks[2], weights.at[here, :, pl.ds(10 * chans, LANES)], sems.at[here]).start()
    share = 4 * chans // groups
    middle = groups * share + blocks[3 + groups * bands].shape[1] if layers > 1 else 0
    for k in range(1, layers):
        slot = lax.rem(here - k + layers, layers)
        for g in range(groups + 2):
            if g < groups:
                place = lax.rem(scalar_ref[3] - g + groups, groups)
                cols = pl.ds(pl.multiple_of(place * share, LANES), share)
            elif g == groups:
                cols = pl.ds(groups * share, middle - groups * share)
            else:
                cols = pl.ds(middle, 10 * chans + LANES - middle)
            for j in range(bands):
                rows = pl.ds(pl.multiple_of(lax.rem(band - j + bands, bands) * part, part), part)
                block = blocks[3 + ((k - 1) * (groups + 2) + g) * bands + j]
                pltpu.make_async_copy(block, weights.at[slot, rows, cols], sems.at[slot]).start()

    if turns > 1:
        hidden, taps = rest[8:]

    def columns(m):
        return slice(m * lon, (m + 1) * lon)

    land = [field_ref[i, vp + fp * steps : vp + fp * steps + 1, :].astype(jnp.float32) for i in range(lat)]

    def put_hidden(i, m, value, layer):
        value = value.astype(jnp.bfloat16)
        hidden[i, :, columns(m)] = value
        if layer is not None:
            put_taps(taps, value, i, columns(m), 2 ** (layer % 3))

    def encode(step, turn):
        for i in range(lat):
            force = field_ref[i, vp + fp * step : vp + fp * (step + 1), :]
            for m in range(members):
                inputs[i, vp : vp + fp, columns(m)] = force
                if step == 0:
                    inputs[i, 0:vp, columns(m)] = field_ref[i, 0:vp, :]
            lifted = jnp.dot(enc_ref[...], inputs[i], preferred_element_type=jnp.float32)
            for m in range(members):
                value = lifted[:, columns(m)] * scale_ref[turn, :, columns(m)] + shift_ref[turn, :, columns(m)]
                put_hidden(i, m, land[i] * value, 0)

    def activate(value, layer):
        centred = value - jnp.sum(value, axis=0, keepdims=True) * (1.0 / chans)
        spread = jnp.sum(centred * centred, axis=0, keepdims=True) * (1.0 / chans)
        normed = (centred * lax.rsqrt(spread + 1e-05)).astype(jnp.bfloat16) * weights[layer, :, 10 * chans :]
        inner = normed * (normed * normed * 0.0356774081 + 0.7978845608)
        half = normed * 0.5
        return half + half * jnp.tanh(inner)

    def block(layer, not_yet):
        if not_yet is True:
            pltpu.make_async_copy(weights.at[layer], weights.at[layer], sems.at[layer]).wait()
        elif not_yet is not None:

            @pl.when(not_yet)
            def _():
                pltpu.make_async_copy(weights.at[layer], weights.at[layer], sems.at[layer]).wait()

        for i in range(lat):
            low, high = max(i - 1, 0), min(i + 1, lat - 1)
            conv[i] = jnp.dot(
                weights[layer, :, (low - i + 1) * wide : (high - i + 2) * wide],
                taps[low * wide : (high + 1) * wide, :],
                preferred_element_type=jnp.float32,
            )
        for i in range(lat):
            mix(i, i, land[i], layer)

    def mix(i, row, sea, layer):
        for m in range(members):
            act[i, :, columns(m)] = activate(conv[i, :, columns(m)], layer)
        mixed = jnp.dot(weights[layer, :, taps_wide : 10 * chans], act[i], preferred_element_type=jnp.float32)
        for m in range(members):
            kept = hidden[row, :, columns(m)].astype(jnp.float32)
            later = layer + 1 if layer + 1 < layers else None
            put_hidden(row, m, sea * (kept + mixed[:, columns(m)]), later)

    def decode(row, sea, step):
        change = jnp.dot(dec_ref[...], hidden[row], preferred_element_type=jnp.float32)
        for m in range(members):
            old = field_ref[row, 0:vp, :] if step == 0 else inputs[row, 0:vp, columns(m)]
            new = old.astype(jnp.float32) + sea * change[:, columns(m)]
            inputs[row, 0:vp, columns(m)] = new.astype(jnp.bfloat16)

    def last_block(layer):
        first = pl.multiple_of((1 - band) * wide, wide)
        conv[0] = jnp.dot(weights[layer, :, pl.ds(first, 2 * wide)], taps[...], preferred_element_type=jnp.float32)
        sea = field_ref[band, vp + fp * steps : vp + fp * steps + 1, :].astype(jnp.float32)
        mix(0, band, sea, layer)
        decode(band, sea, steps - 1)

    varied = final_ref.shape[1]

    def window(turn, first):
        for step in range(steps):
            if step > 0 or turns > 1:
                encode(step, turn)
            own_row = step == steps - 1 and step > 0 and lat == 2 and local == 1
            for layer in range(layers):
                if own_row and layer == layers - 1:
                    last_block(layer)
                else:
                    block(layer, first if step == 0 else None)
            if not own_row:
                for i in range(lat):
                    decode(i, land[i], step)
        for i in range(local):
            row = band * local + i
            summed = inputs[row, 0:vp, columns(0)].astype(jnp.float32)
            for m in range(1, members):
                summed = summed + inputs[row, 0:vp, columns(m)].astype(jnp.float32)
            if turns == 1:
                mean_ref[:, i, :] = summed[0:varied] * (1.0 / members)
                final_ref[i] = inputs[row, 0:varied, columns(0)]
            else:
                total[i] = jnp.where(first, summed, total[i] + summed)
                mean_ref[:, i, :] = total[i, 0:varied] * (1.0 / (members * turns))

                @pl.when(first)
                def _():
                    final_ref[i] = inputs[row, 0:varied, columns(0)]

    if turns == 1:
        window(0, True)
    else:
        lax.fori_loop(0, turns, lambda turn, _: window(turn, turn == 0), None)


def per_device(
    init_state,
    forcing_slots,
    atmos_owner,
    land_mask,
    param_index,
    settings,
    scale_weight,
    shift_weight,
    encode_weight,
    conv_weight,
    point_weight,
    norm_gain,
    decode_weight,
):
    members, layers, bands = (lax.axis_size(a) for a in ("members", "segment", "rows"))
    here, band = lax.axis_index("segment"), lax.axis_index("rows")
    _, local, varied, lon = init_state.shape
    steps, forced = forcing_slots.shape[2], forcing_slots.shape[4]
    chans = conv_weight.shape[1]
    lat = local * bands
    vp, fp = padded_rows(varied), padded_rows(forced)
    part = chans // bands
    at_once = next(n for n in (4, 2, 1) if members % n == 0)
    turns, wide = members // at_once, at_once * lon
    smem, vmem, whole = (pl.BlockSpec(memory_space=s) for s in (pltpu.SMEM, pltpu.VMEM, pl.ANY))
    small, large = (pltpu.CompilerParams(vmem_limit_bytes=n * MIB) for n in (8, 16 + 2 * layers))
    free = pl.CostEstimate(flops=0, bytes_accessed=0, transcendentals=0)

    groups = lax.axis_size("groups")
    share = 4 * chans // groups
    places = [here, band, lax.axis_index("members"), lax.axis_index("groups")]
    scalars = jnp.concatenate([jnp.stack(places).astype(jnp.int32), param_index, atmos_owner[0]])
    slots = forcing_slots[0, 0].reshape(-1, lon)
    crowded = pltpu.CompilerParams(vmem_limit_bytes=60 * MIB)
    middle = groups * share + (9 * chans - groups * share) * 7 // 10 // LANES * LANES
    relayed, between, direct, spread, group = pl.pallas_call(
        pack_kernel,
        out_shape=(
            jax.ShapeDtypeStruct((part, share), jnp.bfloat16),
            jax.ShapeDtypeStruct((part, middle - groups * share), jnp.bfloat16),
            jax.ShapeDtypeStruct((part, 10 * chans + LANES - middle), jnp.bfloat16),
            jax.ShapeDtypeStruct((chans, LANES), jnp.bfloat16),
            jax.ShapeDtypeStruct((slots.shape[0] + 1, lon), jnp.float32),
        ),
        in_specs=[smem] + [whole] * 4,
        out_specs=(whole, whole, whole, vmem, vmem),
        scratch_shapes=[
            pltpu.VMEM(slots.shape, jnp.bfloat16),
            pltpu.VMEM(norm_gain.shape, jnp.bfloat16),
            pltpu.SemaphoreType.DMA((7,)),
        ],
        compiler_params=crowded,
        cost_estimate=free,
    )(scalars, norm_gain, conv_weight[0], point_weight[0], slots)
    relayed, between, direct = (all_along(piece, "segment")[1:] for piece in (relayed, between, direct))
    group = all_along(group, "members")
    field = pl.pallas_call(
        functools.partial(field_kernel, (steps, members, local, forced, vp, fp)),
        out_shape=jax.ShapeDtypeStruct((local, vp + fp * steps + BF16_ROWS, lon), jnp.bfloat16),
        in_specs=[smem] + [vmem] * (2 + members),
        out_specs=vmem,
        compiler_params=small,
        cost_estimate=free,
    )(scalars, init_state[0], land_mask, *group)
    fields = all_along(field, "rows")

    dims = (steps, layers, bands, local, at_once, lon, chans, vp, fp, turns)
    field, scale, shift, enc, dec, hidden, taps = pl.pallas_call(
        functools.partial(first_kernel, dims),
        out_shape=(
            jax.ShapeDtypeStruct((lat, vp + fp * steps + BF16_ROWS, lon), jnp.bfloat16),
            jax.ShapeDtypeStruct((turns, chans, wide), jnp.float32),
            jax.ShapeDtypeStruct((turns, chans, wide), jnp.float32),
            jax.ShapeDtypeStruct((chans, vp + fp), jnp.bfloat16),
            jax.ShapeDtypeStruct((vp, chans), jnp.bfloat16),
            jax.ShapeDtypeStruct((lat, chans, wide), jnp.bfloat16),
            jax.ShapeDtypeStruct((lat * 3 * chans, wide), jnp.bfloat16),
        ),
        in_specs=[smem] + [vmem] * (5 + bands + members),
        out_specs=(vmem,) * 7,
        compiler_params=small,
        cost_estimate=free,
    )(scalars, encode_weight, decode_weight, settings, scale_weight.T, shift_weight.T, *fields, *group)

    blocks = [conv_weight[0], point_weight[0], spread]
    for k in range(layers - 1):
        shares = all_along(after(relayed[k], *group[1:]), "groups")
        early = all_along(shares[0], "rows")
        blocks += early
        for shared in shares[1:]:
            blocks += all_along(shared, "rows")
        blocks += all_along(after(between[k], taps, *shares[1:]), "rows")
        blocks += all_along(after(direct[k], taps, *shares[1:], *early[1:]), "rows")

    scratch = [
        pltpu.VMEM((layers, chans, 10 * chans + LANES), jnp.bfloat16),
        pltpu.VMEM((lat, chans, wide), jnp.float32),
        pltpu.VMEM((lat, chans, wide), jnp.bfloat16),
        pltpu.VMEM((lat, vp + fp, wide), jnp.bfloat16),
        pltpu.VMEM((local, vp, lon), jnp.float32),
        pltpu.SemaphoreType.DMA((layers,)),
    ]
    if turns > 1:
        scratch += [pltpu.VMEM(hidden.shape, jnp.bfloat16), pltpu.VMEM(taps.shape, jnp.bfloat16)]
    final, mean = pl.pallas_call(
        functools.partial(window_kernel, dims + (groups,)),
        out_shape=(
            jax.ShapeDtypeStruct((local, varied, lon), jnp.bfloat16),
            jax.ShapeDtypeStruct((varied, local, lon), jnp.float32),
        ),
        in_specs=[smem] + [vmem] * 7 + [whole] * len(blocks),
        out_specs=(vmem, vmem),
        scratch_shapes=scratch,
        compiler_params=large,
        cost_estimate=free,
    )(scalars, field, scale, shift, enc, dec, hidden, taps, *blocks)
    return final[None, None], jnp.swapaxes(mean, 0, 1)[None]
def solution(mesh):
    in_specs = (
        P(("groups", "segment"), "rows", None, None),
        P("members", ("groups", "segment"), None, "rows", None, None),
        P(("groups", "segment"), None),
        P(("groups", "rows"), None),
        P(("groups", "members")),
        P(),
        P(),
        P(),
        P(),
        P("segment", None, None),
        P("segment", None, None),
        P("segment", None),
        P(),
    )
    out_specs = (
        P("members", ("groups", "segment"), "rows", None, None),
        P(("groups", "segment"), "rows", None, None),
    )
    return jax.shard_map(
        per_device, mesh=mesh, in_specs=in_specs, out_specs=out_specs, check_vma=False
    )
```

```python
import functools

import jax
import jax.numpy as jnp
from jax import lax
from jax.experimental import pallas as pl
from jax.experimental.pallas import tpu as pltpu
from jax.sharding import PartitionSpec as P

BF16_ROWS = 16
LANES = 128
MIB = 1024 * 1024


def padded_rows(count):
    return -(-count // BF16_ROWS) * BF16_ROWS


def passed_along(block, axis, distance):
    size = lax.axis_size(axis)
    return lax.ppermute(block, axis, [(i, (i + distance) % size) for i in range(size)])


def all_along(block, axis):
    return [block] + [passed_along(block, axis, k) for k in range(1, lax.axis_size(axis))]


def by_doubling(block, axis):
    size, reach = lax.axis_size(axis), 1
    while reach < size:
        partner = lax.ppermute(block, axis, [(i, i ^ reach) for i in range(size)])
        block = jnp.concatenate([block, partner], axis=0)
        reach *= 2
    return block


def from_place(parts, here, place):
    chosen = parts[0]
    for k in range(1, len(parts)):
        chosen = jnp.where(lax.rem(here - k + len(parts), len(parts)) == place, parts[k], chosen)
    return chosen


def pack_kernel(dims, place_ref, gain_ref, conv_ref, point_ref, slots_ref, state_ref, land_ref, *rest):
    steps, local, forced, vp, fp = dims
    relayed_ref, direct_ref, spread_ref, field_ref, slots, gain, state, land, sems = rest
    part, share = relayed_ref.shape
    wide, chans = conv_ref.shape[1], point_ref.shape[1]
    left = direct_ref.shape[1] - chans - LANES
    rows = pl.ds(pl.multiple_of(place_ref[1] * part, part), part)
    mine = pl.ds(pl.multiple_of(place_ref[3] * share, LANES), share)
    small = [
        pltpu.make_async_copy(gain_ref, gain, sems.at[0]),
        pltpu.make_async_copy(slots_ref, slots, sems.at[1]),
        pltpu.make_async_copy(state_ref, state, sems.at[2]),
        pltpu.make_async_copy(land_ref, land, sems.at[3]),
    ]
    large = [
        pltpu.make_async_copy(conv_ref.at[rows, mine], relayed_ref, sems.at[4]),
        pltpu.make_async_copy(conv_ref.at[rows, pl.ds(wide - left, left)], direct_ref.at[:, pl.ds(0, left)], sems.at[5]),
        pltpu.make_async_copy(point_ref.at[rows, :], direct_ref.at[:, pl.ds(left, chans)], sems.at[6]),
    ]
    for copy in small + large:
        copy.start()
    for copy in small:
        copy.wait()
    eye = lax.broadcasted_iota(jnp.int32, (chans, chans), 0) == lax.broadcasted_iota(jnp.int32, (chans, chans), 1)
    column = jnp.sum(jnp.where(eye, gain[...].astype(jnp.float32), 0.0), axis=1, keepdims=True)
    spread_ref[...] = jnp.broadcast_to(column, (chans, LANES)).astype(jnp.bfloat16)
    direct_ref[:, left + chans :] = spread_ref[rows, :]
    field_ref[...] = jnp.zeros(field_ref.shape, field_ref.dtype)
    for i in range(local):
        field_ref[i, 0 : state.shape[1]] = state[i]
        for t in range(steps):
            first = (t * local + i) * forced
            field_ref[i, vp + fp * t : vp + fp * t + forced] = slots[first : first + forced]
        field_ref[i, vp + fp * steps : vp + fp * steps + 1] = land[i : i + 1].astype(jnp.bfloat16)
    for copy in large:
        copy.wait()


def group_kernel(dims, place_ref, index_ref, *rest):
    steps, bands, local, forced, vp, fp = dims
    fields, group_ref = rest[:bands], rest[bands]
    for b in range(bands):
        field = from_place([f[...] for f in fields], place_ref[1], b)
        for i in range(local):
            for t in range(steps):
                first = ((b * local + i) * steps + t) * forced
                group_ref[first : first + forced] = field[i, vp + fp * t : vp + fp * t + forced].astype(jnp.float32)
    last = bands * local * steps * forced
    group_ref[last : last + 1] = jnp.full((1, group_ref.shape[1]), index_ref[0], jnp.int32).astype(jnp.float32)


def put_taps(taps, value, row, cols, spacing):
    chans, lon = value.shape
    lane = lax.broadcasted_iota(jnp.int32, (chans, lon), 1)
    zero = jnp.zeros_like(value)
    base = 3 * chans * row
    taps[base : base + chans, cols] = jnp.where(lane >= spacing, pltpu.roll(value, spacing, 1), zero)
    taps[base + chans : base + 2 * chans, cols] = value
    taps[base + 2 * chans : base + 3 * chans, cols] = jnp.where(
        lane < lon - spacing, pltpu.roll(value, lon - spacing, 1), zero
    )


def first_kernel(dims, scalar_ref, owner_ref, enc_w_ref, dec_w_ref, settings_ref, scale_w_ref, shift_w_ref, *rest):
    steps, layers, bands, local, members, lon, chans, vp, fp, turns = dims
    fields, rest = rest[:bands], rest[bands:]
    everyone, rest = rest[0], rest[1:]
    forced = enc_w_ref.shape[1] - dec_w_ref.shape[0]
    used = bands * local * steps * forced
    group = [everyone.at[k * (used + 8) : (k + 1) * (used + 8)] for k in range(members * turns)]
    field_ref, scale_ref, shift_ref, enc_ref, dec_ref, hidden_ref, taps_ref = rest
    varied = dec_w_ref.shape[0]
    forced = enc_w_ref.shape[1] - varied
    enc_ref[...] = jnp.zeros(enc_ref.shape, enc_ref.dtype)
    enc_ref[:, 0:varied] = enc_w_ref[:, 0:varied]
    enc_ref[:, vp : vp + forced] = enc_w_ref[:, varied : varied + forced]
    dec_ref[...] = jnp.zeros(dec_ref.shape, dec_ref.dtype)
    dec_ref[0:varied, :] = dec_w_ref[...]
    band = scalar_ref[1]
    for b in range(bands):
        field_ref[b * local : (b + 1) * local] = from_place([f[...] for f in fields], band, b)
    for i in range(bands * local):
        for t in range(steps):
            rows = slice((i * steps + t) * forced, (i * steps + t + 1) * forced)
            place = scalar_ref[2] ^ owner_ref[t]
            force = group[0][rows, :]
            for k in range(1, members * turns):
                force = jnp.where(place == k, group[k][rows, :], force)
            field_ref[i, vp + fp * t : vp + fp * t + forced, :] = force.astype(jnp.bfloat16)

    settings = settings_ref[...]
    numbers = lax.broadcasted_iota(jnp.int32, settings.shape, 0).astype(jnp.float32)
    for m, entry in enumerate(group):
        chosen = entry[used : used + 1, 0 : settings.shape[1]]
        row = jnp.sum(jnp.where(numbers == chosen, settings, 0.0), axis=0, keepdims=True)
        cols = slice((m % members) * lon, (m % members + 1) * lon)
        scale = 1.0 + jnp.sum(scale_w_ref[...] * row, axis=1, keepdims=True)
        shift = jnp.sum(shift_w_ref[...] * row, axis=1, keepdims=True)
        scale_ref[m // members, :, cols] = jnp.broadcast_to(scale, (chans, lon))
        shift_ref[m // members, :, cols] = jnp.broadcast_to(shift, (chans, lon))

    if turns == 1:
        for i in range(bands * local):
            land = field_ref[i, vp + fp * steps : vp + fp * steps + 1, :].astype(jnp.float32)
            lifted = jnp.dot(enc_ref[...], field_ref[i, 0 : vp + fp, :], preferred_element_type=jnp.float32)
            for m in range(members):
                cols = slice(m * lon, (m + 1) * lon)
                value = land * (lifted * scale_ref[0, :, cols] + shift_ref[0, :, cols])
                value = value.astype(jnp.bfloat16)
                hidden_ref[i, :, cols] = value
                put_taps(taps_ref, value, i, cols, 1)


def after_kernel(*refs):
    pass


def after(section, *earlier):
    whole = pl.BlockSpec(memory_space=pl.ANY)
    return pl.pallas_call(
        after_kernel,
        out_shape=jax.ShapeDtypeStruct(section.shape, section.dtype),
        in_specs=[whole] * (1 + len(earlier)),
        out_specs=whole,
        input_output_aliases={0: 0},
        compiler_params=pltpu.CompilerParams(vmem_limit_bytes=MIB),
        cost_estimate=pl.CostEstimate(flops=0, bytes_accessed=0, transcendentals=0),
    )(section, *earlier)


def window_kernel(dims, scalar_ref, field_ref, scale_ref, shift_ref, enc_ref, dec_ref, *rest):
    steps, layers, bands, local, members, lon, chans, vp, fp, turns, groups = dims
    lat = bands * local
    hidden, taps = rest[:2]
    pieces = 3 + (layers - 1) * (groups + 1) * bands
    blocks, rest = rest[2 : 2 + pieces], rest[2 + pieces :]
    final_ref, mean_ref, weights, conv, act, inputs, total, sems = rest[:8]
    here, band = scalar_ref[0], scalar_ref[1]
    taps_wide, wide = 9 * chans, 3 * chans
    part = chans // bands

    pltpu.make_async_copy(blocks[0], weights.at[here, :, pl.ds(0, taps_wide)], sems.at[here]).start()
    pltpu.make_async_copy(blocks[1], weights.at[here, :, pl.ds(taps_wide, chans)], sems.at[here]).start()
    pltpu.make_async_copy(blocks[2], weights.at[here, :, pl.ds(10 * chans, LANES)], sems.at[here]).start()
    share = 5 * chans // groups
    for k in range(1, layers):
        slot = lax.rem(here - k + layers, layers)
        for g in range(groups + 1):
            if g < groups:
                place = lax.rem(scalar_ref[3] - g + groups, groups)
                cols = pl.ds(pl.multiple_of(place * share, LANES), share)
            else:
                cols = pl.ds(groups * share, 10 * chans + LANES - groups * share)
            for j in range(bands):
                rows = pl.ds(pl.multiple_of(lax.rem(band - j + bands, bands) * part, part), part)
                block = blocks[3 + ((k - 1) * (groups + 1) + g) * bands + j]
                pltpu.make_async_copy(block, weights.at[slot, rows, cols], sems.at[slot]).start()

    if turns > 1:
        hidden, taps = rest[8:]

    def columns(m):
        return slice(m * lon, (m + 1) * lon)

    land = [field_ref[i, vp + fp * steps : vp + fp * steps + 1, :].astype(jnp.float32) for i in range(lat)]

    def put_hidden(i, m, value, layer):
        value = value.astype(jnp.bfloat16)
        hidden[i, :, columns(m)] = value
        if layer is not None:
            put_taps(taps, value, i, columns(m), 2 ** (layer % 3))

    def encode(step, turn):
        for i in range(lat):
            force = field_ref[i, vp + fp * step : vp + fp * (step + 1), :]
            for m in range(members):
                inputs[i, vp : vp + fp, columns(m)] = force
                if step == 0:
                    inputs[i, 0:vp, columns(m)] = field_ref[i, 0:vp, :]
            lifted = jnp.dot(enc_ref[...], inputs[i], preferred_element_type=jnp.float32)
            for m in range(members):
                value = lifted[:, columns(m)] * scale_ref[turn, :, columns(m)] + shift_ref[turn, :, columns(m)]
                put_hidden(i, m, land[i] * value, 0)

    def activate(value, layer):
        centred = value - jnp.sum(value, axis=0, keepdims=True) * (1.0 / chans)
        spread = jnp.sum(centred * centred, axis=0, keepdims=True) * (1.0 / chans)
        normed = (centred * lax.rsqrt(spread + 1e-05)).astype(jnp.bfloat16) * weights[layer, :, 10 * chans :]
        inner = normed * (normed * normed * 0.0356774081 + 0.7978845608)
        half = normed * 0.5
        return half + half * jnp.tanh(inner)

    def block(layer, not_yet):
        if not_yet is True:
            pltpu.make_async_copy(weights.at[layer], weights.at[layer], sems.at[layer]).wait()
        elif not_yet is not None:

            @pl.when(not_yet)
            def _():
                pltpu.make_async_copy(weights.at[layer], weights.at[layer], sems.at[layer]).wait()

        for i in range(lat):
            low, high = max(i - 1, 0), min(i + 1, lat - 1)
            conv[i] = jnp.dot(
                weights[layer, :, (low - i + 1) * wide : (high - i + 2) * wide],
                taps[low * wide : (high + 1) * wide, :],
                preferred_element_type=jnp.float32,
            )
        for i in range(lat):
            mix(i, i, land[i], layer)

    def mix(i, row, sea, layer):
        for m in range(members):
            act[i, :, columns(m)] = activate(conv[i, :, columns(m)], layer)
        mixed = jnp.dot(weights[layer, :, taps_wide : 10 * chans], act[i], preferred_element_type=jnp.float32)
        for m in range(members):
            kept = hidden[row, :, columns(m)].astype(jnp.float32)
            later = layer + 1 if layer + 1 < layers else None
            put_hidden(row, m, sea * (kept + mixed[:, columns(m)]), later)

    def decode(row, sea, step):
        change = jnp.dot(dec_ref[...], hidden[row], preferred_element_type=jnp.float32)
        for m in range(members):
            old = field_ref[row, 0:vp, :] if step == 0 else inputs[row, 0:vp, columns(m)]
            new = old.astype(jnp.float32) + sea * change[:, columns(m)]
            inputs[row, 0:vp, columns(m)] = new.astype(jnp.bfloat16)

    def last_block(layer):
        first = pl.multiple_of((1 - band) * wide, wide)
        conv[0] = jnp.dot(weights[layer, :, pl.ds(first, 2 * wide)], taps[...], preferred_element_type=jnp.float32)
        sea = field_ref[band, vp + fp * steps : vp + fp * steps + 1, :].astype(jnp.float32)
        mix(0, band, sea, layer)
        decode(band, sea, steps - 1)

    varied = final_ref.shape[1]

    def window(turn, first):
        for step in range(steps):
            if step > 0 or turns > 1:
                encode(step, turn)
            own_row = step == steps - 1 and step > 0 and lat == 2 and local == 1
            for layer in range(layers):
                if own_row and layer == layers - 1:
                    last_block(layer)
                else:
                    block(layer, first if step == 0 else None)
            if not own_row:
                for i in range(lat):
                    decode(i, land[i], step)
        for i in range(local):
            row = band * local + i
            summed = inputs[row, 0:vp, columns(0)].astype(jnp.float32)
            for m in range(1, members):
                summed = summed + inputs[row, 0:vp, columns(m)].astype(jnp.float32)
            if turns == 1:
                mean_ref[:, i, :] = summed[0:varied] * (1.0 / members)
                final_ref[i] = inputs[row, 0:varied, columns(0)]
            else:
                total[i] = jnp.where(first, summed, total[i] + summed)
                mean_ref[:, i, :] = total[i, 0:varied] * (1.0 / (members * turns))

                @pl.when(first)
                def _():
                    final_ref[i] = inputs[row, 0:varied, columns(0)]

    if turns == 1:
        window(0, True)
    else:
        lax.fori_loop(0, turns, lambda turn, _: window(turn, turn == 0), None)


def per_device(
    init_state,
    forcing_slots,
    atmos_owner,
    land_mask,
    param_index,
    settings,
    scale_weight,
    shift_weight,
    encode_weight,
    conv_weight,
    point_weight,
    norm_gain,
    decode_weight,
):
    members, layers, bands = (lax.axis_size(a) for a in ("members", "segment", "rows"))
    here, band = lax.axis_index("segment"), lax.axis_index("rows")
    _, local, varied, lon = init_state.shape
    steps, forced = forcing_slots.shape[2], forcing_slots.shape[4]
    chans = conv_weight.shape[1]
    lat = local * bands
    vp, fp = padded_rows(varied), padded_rows(forced)
    part = chans // bands
    at_once = next(n for n in (4, 2, 1) if members % n == 0)
    turns, wide = members // at_once, at_once * lon
    smem, vmem, whole = (pl.BlockSpec(memory_space=s) for s in (pltpu.SMEM, pltpu.VMEM, pl.ANY))
    small, large = (pltpu.CompilerParams(vmem_limit_bytes=n * MIB) for n in (8, 16 + 2 * layers))
    free = pl.CostEstimate(flops=0, bytes_accessed=0, transcendentals=0)

    groups = lax.axis_size("groups")
    share = 5 * chans // groups
    places = [here, band, lax.axis_index("members"), lax.axis_index("groups")]
    scalars = jnp.stack(places).astype(jnp.int32)
    slots = forcing_slots[0, 0].reshape(-1, lon)
    relayed, direct, spread, field = pl.pallas_call(
        functools.partial(pack_kernel, (steps, local, forced, vp, fp)),
        out_shape=(
            jax.ShapeDtypeStruct((part, share), jnp.bfloat16),
            jax.ShapeDtypeStruct((part, 10 * chans + LANES - groups * share), jnp.bfloat16),
            jax.ShapeDtypeStruct((chans, LANES), jnp.bfloat16),
            jax.ShapeDtypeStruct((local, vp + fp * steps + BF16_ROWS, lon), jnp.bfloat16),
        ),
        in_specs=[smem] + [whole] * 6,
        out_specs=(vmem,) * 4,
        scratch_shapes=[
            pltpu.VMEM(slots.shape, jnp.bfloat16),
            pltpu.VMEM(norm_gain.shape, jnp.bfloat16),
            pltpu.VMEM(init_state.shape[1:], jnp.bfloat16),
            pltpu.VMEM(land_mask.shape, jnp.int32),
            pltpu.SemaphoreType.DMA((7,)),
        ],
        compiler_params=pltpu.CompilerParams(vmem_limit_bytes=60 * MIB),
        cost_estimate=free,
    )(scalars, norm_gain, conv_weight[0], point_weight[0], slots, init_state[0], land_mask)
    relayed, direct = (all_along(piece, "segment")[1:] for piece in (relayed, direct))
    fields = all_along(field, "rows")
    group = pl.pallas_call(
        functools.partial(group_kernel, (steps, bands, local, forced, vp, fp)),
        out_shape=jax.ShapeDtypeStruct((lat * steps * forced + 8, lon), jnp.float32),
        in_specs=[smem, smem] + [vmem] * bands,
        out_specs=vmem,
        compiler_params=small,
        cost_estimate=free,
    )(scalars, param_index, *fields)
    group = by_doubling(group, "members")

    dims = (steps, layers, bands, local, at_once, lon, chans, vp, fp, turns)
    field, scale, shift, enc, dec, hidden, taps = pl.pallas_call(
        functools.partial(first_kernel, dims),
        out_shape=(
            jax.ShapeDtypeStruct((lat, vp + fp * steps + BF16_ROWS, lon), jnp.bfloat16),
            jax.ShapeDtypeStruct((turns, chans, wide), jnp.float32),
            jax.ShapeDtypeStruct((turns, chans, wide), jnp.float32),
            jax.ShapeDtypeStruct((chans, vp + fp), jnp.bfloat16),
            jax.ShapeDtypeStruct((vp, chans), jnp.bfloat16),
            jax.ShapeDtypeStruct((lat, chans, wide), jnp.bfloat16),
            jax.ShapeDtypeStruct((lat * 3 * chans, wide), jnp.bfloat16),
        ),
        in_specs=[smem, smem] + [vmem] * (6 + bands),
        out_specs=(vmem,) * 7,
        compiler_params=small,
        cost_estimate=free,
    )(scalars, atmos_owner[0], encode_weight, decode_weight, settings, scale_weight.T, shift_weight.T, *fields, group)

    blocks = [conv_weight[0], point_weight[0], spread]
    for k in range(layers - 1):
        shares = all_along(relayed[k], "groups")
        early = all_along(shares[0], "rows")
        blocks += early
        for shared in shares[1:]:
            blocks += all_along(shared, "rows")
        blocks += all_along(after(direct[k], group, *shares[1:], *early[1:]), "rows")

    scratch = [
        pltpu.VMEM((layers, chans, 10 * chans + LANES), jnp.bfloat16),
        pltpu.VMEM((lat, chans, wide), jnp.float32),
        pltpu.VMEM((lat, chans, wide), jnp.bfloat16),
        pltpu.VMEM((lat, vp + fp, wide), jnp.bfloat16),
        pltpu.VMEM((local, vp, lon), jnp.float32),
        pltpu.SemaphoreType.DMA((layers,)),
    ]
    if turns > 1:
        scratch += [pltpu.VMEM(hidden.shape, jnp.bfloat16), pltpu.VMEM(taps.shape, jnp.bfloat16)]
    final, mean = pl.pallas_call(
        functools.partial(window_kernel, dims + (groups,)),
        out_shape=(
            jax.ShapeDtypeStruct((local, varied, lon), jnp.bfloat16),
            jax.ShapeDtypeStruct((varied, local, lon), jnp.float32),
        ),
        in_specs=[smem] + [vmem] * 7 + [whole] * len(blocks),
        out_specs=(vmem, vmem),
        scratch_shapes=scratch,
        compiler_params=large,
        cost_estimate=free,
    )(scalars, field, scale, shift, enc, dec, hidden, taps, *blocks)
    return final[None, None], jnp.swapaxes(mean, 0, 1)[None]
def solution(mesh):
    in_specs = (
        P(("groups", "segment"), "rows", None, None),
        P("members", ("groups", "segment"), None, "rows", None, None),
        P(("groups", "segment"), None),
        P(("groups", "rows"), None),
        P(("groups", "members")),
        P(),
        P(),
        P(),
        P(),
        P("segment", None, None),
        P("segment", None, None),
        P("segment", None),
        P(),
    )
    out_specs = (
        P("members", ("groups", "segment"), "rows", None, None),
        P(("groups", "segment"), "rows", None, None),
    )
    return jax.shard_map(
        per_device, mesh=mesh, in_specs=in_specs, out_specs=out_specs, check_vma=False
    )
```

```python
import functools

import jax
import jax.numpy as jnp
from jax import lax
from jax.experimental import pallas as pl
from jax.experimental.pallas import tpu as pltpu
from jax.sharding import PartitionSpec as P

BF16_ROWS = 16
LANES = 128
MIB = 1024 * 1024


def padded_rows(count):
    return -(-count // BF16_ROWS) * BF16_ROWS


def passed_along(block, axis, distance):
    size = lax.axis_size(axis)
    return lax.ppermute(block, axis, [(i, (i + distance) % size) for i in range(size)])


def all_along(block, axis):
    return [block] + [passed_along(block, axis, k) for k in range(1, lax.axis_size(axis))]


def by_doubling(block, axis):
    size, reach = lax.axis_size(axis), 1
    while reach < size:
        partner = lax.ppermute(block, axis, [(i, i ^ reach) for i in range(size)])
        block = jnp.concatenate([block, partner], axis=0)
        reach *= 2
    return block


def from_place(parts, here, place):
    chosen = parts[0]
    for k in range(1, len(parts)):
        chosen = jnp.where(lax.rem(here - k + len(parts), len(parts)) == place, parts[k], chosen)
    return chosen


def pack_kernel(dims, gain_ref, slots_ref, state_ref, land_ref, earlier_ref, spread_ref, field_ref):
    steps, local, forced, vp, fp = dims
    chans = gain_ref.shape[1]
    eye = lax.broadcasted_iota(jnp.int32, (chans, chans), 0) == lax.broadcasted_iota(jnp.int32, (chans, chans), 1)
    column = jnp.sum(jnp.where(eye, gain_ref[...].astype(jnp.float32), 0.0), axis=1, keepdims=True)
    spread_ref[...] = jnp.broadcast_to(column, (chans, LANES)).astype(jnp.bfloat16)
    field_ref[...] = jnp.zeros(field_ref.shape, field_ref.dtype)
    for i in range(local):
        field_ref[i, 0 : state_ref.shape[1]] = state_ref[i]
        for t in range(steps):
            first = (t * local + i) * forced
            field_ref[i, vp + fp * t : vp + fp * t + forced] = slots_ref[first : first + forced]
        field_ref[i, vp + fp * steps : vp + fp * steps + 1] = land_ref[i : i + 1].astype(jnp.bfloat16)


def group_kernel(dims, place_ref, index_ref, *rest):
    steps, bands, local, forced, vp, fp = dims
    fields, group_ref = rest[:bands], rest[bands]
    for b in range(bands):
        field = from_place([f[...] for f in fields], place_ref[1], b)
        for i in range(local):
            for t in range(steps):
                first = ((b * local + i) * steps + t) * forced
                group_ref[first : first + forced] = field[i, vp + fp * t : vp + fp * t + forced].astype(jnp.float32)
    last = bands * local * steps * forced
    group_ref[last : last + 1] = jnp.full((1, group_ref.shape[1]), index_ref[0], jnp.int32).astype(jnp.float32)


def put_taps(taps, value, row, cols, spacing):
    chans, lon = value.shape
    lane = lax.broadcasted_iota(jnp.int32, (chans, lon), 1)
    zero = jnp.zeros_like(value)
    base = 3 * chans * row
    taps[base : base + chans, cols] = jnp.where(lane >= spacing, pltpu.roll(value, spacing, 1), zero)
    taps[base + chans : base + 2 * chans, cols] = value
    taps[base + 2 * chans : base + 3 * chans, cols] = jnp.where(
        lane < lon - spacing, pltpu.roll(value, lon - spacing, 1), zero
    )


def first_kernel(dims, scalar_ref, owner_ref, enc_w_ref, dec_w_ref, settings_ref, scale_w_ref, shift_w_ref, *rest):
    steps, layers, bands, local, members, lon, chans, vp, fp, turns = dims
    fields, rest = rest[:bands], rest[bands:]
    everyone, rest = rest[0], rest[1:]
    forced = enc_w_ref.shape[0] - dec_w_ref.shape[0]
    used = bands * local * steps * forced
    group = [everyone.at[k * (used + 8) : (k + 1) * (used + 8)] for k in range(members * turns)]
    field_ref, scale_ref, shift_ref, enc_ref, dec_ref, hidden_ref, taps_ref, turned = rest
    varied = dec_w_ref.shape[0]
    turned[...] = jnp.zeros(turned.shape, turned.dtype)
    turned[0:varied] = enc_w_ref[0:varied].astype(jnp.float32)
    turned[vp : vp + forced] = enc_w_ref[varied : varied + forced].astype(jnp.float32)
    enc_ref[...] = turned[...].T.astype(jnp.bfloat16)
    dec_ref[...] = jnp.zeros(dec_ref.shape, dec_ref.dtype)
    dec_ref[0:varied, :] = dec_w_ref[...]
    band = scalar_ref[1]
    for b in range(bands):
        field_ref[b * local : (b + 1) * local] = from_place([f[...] for f in fields], band, b)
    for i in range(bands * local):
        for t in range(steps):
            rows = slice((i * steps + t) * forced, (i * steps + t + 1) * forced)
            place = scalar_ref[2] ^ owner_ref[t]
            force = group[0][rows, :]
            for k in range(1, members * turns):
                force = jnp.where(place == k, group[k][rows, :], force)
            field_ref[i, vp + fp * t : vp + fp * t + forced, :] = force.astype(jnp.bfloat16)

    settings = settings_ref[...]
    numbers = lax.broadcasted_iota(jnp.int32, settings.shape, 0).astype(jnp.float32)
    for m, entry in enumerate(group):
        chosen = entry[used : used + 1, 0 : settings.shape[1]]
        row = jnp.sum(jnp.where(numbers == chosen, settings, 0.0), axis=0, keepdims=True)
        cols = slice((m % members) * lon, (m % members + 1) * lon)
        scale = 1.0 + jnp.sum(scale_w_ref[...] * row, axis=1, keepdims=True)
        shift = jnp.sum(shift_w_ref[...] * row, axis=1, keepdims=True)
        scale_ref[m // members, :, cols] = jnp.broadcast_to(scale, (chans, lon))
        shift_ref[m // members, :, cols] = jnp.broadcast_to(shift, (chans, lon))

    if turns == 1:
        for i in range(bands * local):
            land = field_ref[i, vp + fp * steps : vp + fp * steps + 1, :].astype(jnp.float32)
            lifted = jnp.dot(enc_ref[...], field_ref[i, 0 : vp + fp, :], preferred_element_type=jnp.float32)
            for m in range(members):
                cols = slice(m * lon, (m + 1) * lon)
                value = land * (lifted * scale_ref[0, :, cols] + shift_ref[0, :, cols])
                value = value.astype(jnp.bfloat16)
                hidden_ref[i, :, cols] = value
                put_taps(taps_ref, value, i, cols, 1)


def after_kernel(*refs):
    pass


def after(section, *earlier):
    whole = pl.BlockSpec(memory_space=pl.ANY)
    return pl.pallas_call(
        after_kernel,
        out_shape=jax.ShapeDtypeStruct(section.shape, section.dtype),
        in_specs=[whole] * (1 + len(earlier)),
        out_specs=whole,
        input_output_aliases={0: 0},
        compiler_params=pltpu.CompilerParams(vmem_limit_bytes=MIB),
        cost_estimate=pl.CostEstimate(flops=0, bytes_accessed=0, transcendentals=0),
    )(section, *earlier)


def window_kernel(dims, scalar_ref, field_ref, scale_ref, shift_ref, enc_ref, dec_ref, *rest):
    steps, layers, bands, local, members, lon, chans, vp, fp, turns, groups = dims
    lat = bands * local
    hidden, taps = rest[:2]
    pieces = 3 + (layers - 1) * (groups + 1) * bands
    blocks, rest = rest[2 : 2 + pieces], rest[2 + pieces :]
    final_ref, mean_ref, weights, conv, act, inputs, total, sems = rest[:8]
    here, band = scalar_ref[0], scalar_ref[1]
    taps_wide, wide = 9 * chans, 3 * chans
    part = chans // bands

    pltpu.make_async_copy(blocks[0], weights.at[here, :, pl.ds(0, taps_wide)], sems.at[here]).start()
    pltpu.make_async_copy(blocks[1], weights.at[here, :, pl.ds(taps_wide, chans)], sems.at[here]).start()
    pltpu.make_async_copy(blocks[2], weights.at[here, :, pl.ds(10 * chans, LANES)], sems.at[here]).start()
    share = 5 * chans // groups
    for k in range(1, layers):
        slot = lax.rem(here - k + layers, layers)
        for g in range(groups + 1):
            if g < groups:
                place = lax.rem(scalar_ref[3] - g + groups, groups)
                cols = pl.ds(pl.multiple_of(place * share, LANES), share)
            else:
                cols = pl.ds(groups * share, 10 * chans + LANES - groups * share)
            for j in range(bands):
                rows = pl.ds(pl.multiple_of(lax.rem(band - j + bands, bands) * part, part), part)
                block = blocks[3 + ((k - 1) * (groups + 1) + g) * bands + j]
                pltpu.make_async_copy(block, weights.at[slot, rows, cols], sems.at[slot]).start()

    if turns > 1:
        hidden, taps = rest[8:]

    def columns(m):
        return slice(m * lon, (m + 1) * lon)

    land = [field_ref[i, vp + fp * steps : vp + fp * steps + 1, :].astype(jnp.float32) for i in range(lat)]

    def put_hidden(i, m, value, layer):
        value = value.astype(jnp.bfloat16)
        hidden[i, :, columns(m)] = value
        if layer is not None:
            put_taps(taps, value, i, columns(m), 2 ** (layer % 3))

    def encode(step, turn):
        for i in range(lat):
            force = field_ref[i, vp + fp * step : vp + fp * (step + 1), :]
            for m in range(members):
                inputs[i, vp : vp + fp, columns(m)] = force
                if step == 0:
                    inputs[i, 0:vp, columns(m)] = field_ref[i, 0:vp, :]
            lifted = jnp.dot(enc_ref[...], inputs[i], preferred_element_type=jnp.float32)
            for m in range(members):
                value = lifted[:, columns(m)] * scale_ref[turn, :, columns(m)] + shift_ref[turn, :, columns(m)]
                put_hidden(i, m, land[i] * value, 0)

    def activate(value, layer):
        centred = value - jnp.sum(value, axis=0, keepdims=True) * (1.0 / chans)
        spread = jnp.sum(centred * centred, axis=0, keepdims=True) * (1.0 / chans)
        normed = (centred * lax.rsqrt(spread + 1e-05)).astype(jnp.bfloat16) * weights[layer, :, 10 * chans :]
        inner = normed * (normed * normed * 0.0356774081 + 0.7978845608)
        half = normed * 0.5
        return half + half * jnp.tanh(inner)

    def block(layer, not_yet):
        if not_yet is True:
            pltpu.make_async_copy(weights.at[layer], weights.at[layer], sems.at[layer]).wait()
        elif not_yet is not None:

            @pl.when(not_yet)
            def _():
                pltpu.make_async_copy(weights.at[layer], weights.at[layer], sems.at[layer]).wait()

        for i in range(lat):
            low, high = max(i - 1, 0), min(i + 1, lat - 1)
            conv[i] = jnp.dot(
                weights[layer, :, (low - i + 1) * wide : (high - i + 2) * wide],
                taps[low * wide : (high + 1) * wide, :],
                preferred_element_type=jnp.float32,
            )
        for i in range(lat):
            mix(i, i, land[i], layer)

    def mix(i, row, sea, layer):
        for m in range(members):
            act[i, :, columns(m)] = activate(conv[i, :, columns(m)], layer)
        mixed = jnp.dot(weights[layer, :, taps_wide : 10 * chans], act[i], preferred_element_type=jnp.float32)
        for m in range(members):
            kept = hidden[row, :, columns(m)].astype(jnp.float32)
            later = layer + 1 if layer + 1 < layers else None
            put_hidden(row, m, sea * (kept + mixed[:, columns(m)]), later)

    def decode(row, sea, step):
        change = jnp.dot(dec_ref[...], hidden[row], preferred_element_type=jnp.float32)
        for m in range(members):
            old = field_ref[row, 0:vp, :] if step == 0 else inputs[row, 0:vp, columns(m)]
            new = old.astype(jnp.float32) + sea * change[:, columns(m)]
            inputs[row, 0:vp, columns(m)] = new.astype(jnp.bfloat16)

    def last_block(layer):
        first = pl.multiple_of((1 - band) * wide, wide)
        conv[0] = jnp.dot(weights[layer, :, pl.ds(first, 2 * wide)], taps[...], preferred_element_type=jnp.float32)
        sea = field_ref[band, vp + fp * steps : vp + fp * steps + 1, :].astype(jnp.float32)
        mix(0, band, sea, layer)
        decode(band, sea, steps - 1)

    varied = final_ref.shape[1]

    def window(turn, first):
        for step in range(steps):
            if step > 0 or turns > 1:
                encode(step, turn)
            own_row = step == steps - 1 and step > 0 and lat == 2 and local == 1
            for layer in range(layers):
                if own_row and layer == layers - 1:
                    last_block(layer)
                else:
                    block(layer, first if step == 0 else None)
            if not own_row:
                for i in range(lat):
                    decode(i, land[i], step)
        for i in range(local):
            row = band * local + i
            summed = inputs[row, 0:vp, columns(0)].astype(jnp.float32)
            for m in range(1, members):
                summed = summed + inputs[row, 0:vp, columns(m)].astype(jnp.float32)
            if turns == 1:
                mean_ref[:, i, :] = summed[0:varied] * (1.0 / members)
                final_ref[i] = inputs[row, 0:varied, columns(0)]
            else:
                total[i] = jnp.where(first, summed, total[i] + summed)
                mean_ref[:, i, :] = total[i, 0:varied] * (1.0 / (members * turns))

                @pl.when(first)
                def _():
                    final_ref[i] = inputs[row, 0:varied, columns(0)]

    if turns == 1:
        window(0, True)
    else:
        lax.fori_loop(0, turns, lambda turn, _: window(turn, turn == 0), None)


def per_device(
    init_state,
    forcing_slots,
    atmos_owner,
    land_mask,
    param_index,
    settings,
    scale_weight,
    shift_weight,
    encode_weight,
    conv_weight,
    point_weight,
    norm_gain,
    decode_weight,
):
    members, layers, bands = (lax.axis_size(a) for a in ("members", "segment", "rows"))
    here, band = lax.axis_index("segment"), lax.axis_index("rows")
    _, local, varied, lon = init_state.shape
    steps, forced = forcing_slots.shape[2], forcing_slots.shape[4]
    chans = conv_weight.shape[1]
    lat = local * bands
    vp, fp = padded_rows(varied), padded_rows(forced)
    part = chans // bands
    at_once = next(n for n in (4, 2, 1) if members % n == 0)
    turns, wide = members // at_once, at_once * lon
    smem, vmem, whole = (pl.BlockSpec(memory_space=s) for s in (pltpu.SMEM, pltpu.VMEM, pl.ANY))
    small, large = (pltpu.CompilerParams(vmem_limit_bytes=n * MIB) for n in (8, 16 + 2 * layers))
    free = pl.CostEstimate(flops=0, bytes_accessed=0, transcendentals=0)

    groups = lax.axis_size("groups")
    share = 5 * chans // groups
    places = [here, band, lax.axis_index("members"), lax.axis_index("groups")]
    scalars = jnp.stack(places).astype(jnp.int32)
    slots = forcing_slots[0, 0].reshape(-1, lon)
    relayed = lax.dynamic_slice(conv_weight[0], (band * part, places[3] * share), (part, share))
    spread, field = pl.pallas_call(
        functools.partial(pack_kernel, (steps, local, forced, vp, fp)),
        out_shape=(
            jax.ShapeDtypeStruct((chans, LANES), jnp.bfloat16),
            jax.ShapeDtypeStruct((local, vp + fp * steps + BF16_ROWS, lon), jnp.bfloat16),
        ),
        in_specs=[vmem] * 4 + [whole],
        out_specs=(vmem,) * 2,
        compiler_params=small,
        cost_estimate=free,
    )(norm_gain, slots, init_state[0], land_mask, relayed)
    direct = jnp.concatenate([conv_weight[0][:, groups * share :], point_weight[0], spread], axis=1)
    direct = lax.dynamic_slice_in_dim(direct, band * part, part, 0)
    relayed, direct = (all_along(piece, "segment")[1:] for piece in (relayed, direct))
    fields = all_along(field, "rows")
    group = pl.pallas_call(
        functools.partial(group_kernel, (steps, bands, local, forced, vp, fp)),
        out_shape=jax.ShapeDtypeStruct((lat * steps * forced + 8, lon), jnp.float32),
        in_specs=[smem, smem] + [vmem] * bands,
        out_specs=vmem,
        compiler_params=small,
        cost_estimate=free,
    )(scalars, param_index, *fields)
    group = by_doubling(group, "members")

    dims = (steps, layers, bands, local, at_once, lon, chans, vp, fp, turns)
    field, scale, shift, enc, dec, hidden, taps = pl.pallas_call(
        functools.partial(first_kernel, dims),
        out_shape=(
            jax.ShapeDtypeStruct((lat, vp + fp * steps + BF16_ROWS, lon), jnp.bfloat16),
            jax.ShapeDtypeStruct((turns, chans, wide), jnp.float32),
            jax.ShapeDtypeStruct((turns, chans, wide), jnp.float32),
            jax.ShapeDtypeStruct((chans, vp + fp), jnp.bfloat16),
            jax.ShapeDtypeStruct((vp, chans), jnp.bfloat16),
            jax.ShapeDtypeStruct((lat, chans, wide), jnp.bfloat16),
            jax.ShapeDtypeStruct((lat * 3 * chans, wide), jnp.bfloat16),
        ),
        in_specs=[smem, smem] + [vmem] * (6 + bands),
        out_specs=(vmem,) * 7,
        scratch_shapes=[pltpu.VMEM((vp + fp, chans), jnp.float32)],
        compiler_params=small,
        cost_estimate=free,
    )(scalars, atmos_owner[0], encode_weight.T, decode_weight, settings, scale_weight.T, shift_weight.T, *fields, group)

    blocks = [conv_weight[0], point_weight[0], spread]
    for k in range(layers - 1):
        shares = all_along(relayed[k], "groups")
        early = all_along(shares[0], "rows")
        blocks += early
        for shared in shares[1:]:
            blocks += all_along(shared, "rows")
        blocks += all_along(after(direct[k], group, *shares[1:], *early[1:]), "rows")

    scratch = [
        pltpu.VMEM((layers, chans, 10 * chans + LANES), jnp.bfloat16),
        pltpu.VMEM((lat, chans, wide), jnp.float32),
        pltpu.VMEM((lat, chans, wide), jnp.bfloat16),
        pltpu.VMEM((lat, vp + fp, wide), jnp.bfloat16),
        pltpu.VMEM((local, vp, lon), jnp.float32),
        pltpu.SemaphoreType.DMA((layers,)),
    ]
    if turns > 1:
        scratch += [pltpu.VMEM(hidden.shape, jnp.bfloat16), pltpu.VMEM(taps.shape, jnp.bfloat16)]
    final, mean = pl.pallas_call(
        functools.partial(window_kernel, dims + (groups,)),
        out_shape=(
            jax.ShapeDtypeStruct((local, varied, lon), jnp.bfloat16),
            jax.ShapeDtypeStruct((varied, local, lon), jnp.float32),
        ),
        in_specs=[smem] + [vmem] * 7 + [whole] * len(blocks),
        out_specs=(vmem, vmem),
        scratch_shapes=scratch,
        compiler_params=large,
        cost_estimate=free,
    )(scalars, field, scale, shift, enc, dec, hidden, taps, *blocks)
    return final[None, None], jnp.swapaxes(mean, 0, 1)[None]
def solution(mesh):
    in_specs = (
        P(("groups", "segment"), "rows", None, None),
        P("members", ("groups", "segment"), None, "rows", None, None),
        P(("groups", "segment"), None),
        P(("groups", "rows"), None),
        P(("groups", "members")),
        P(),
        P(),
        P(),
        P(),
        P("segment", None, None),
        P("segment", None, None),
        P("segment", None),
        P(),
    )
    out_specs = (
        P("members", ("groups", "segment"), "rows", None, None),
        P(("groups", "segment"), "rows", None, None),
    )
    return jax.shard_map(
        per_device, mesh=mesh, in_specs=in_specs, out_specs=out_specs, check_vma=False
    )
```

```python
import functools

import jax
import jax.numpy as jnp
from jax import lax
from jax.experimental import pallas as pl
from jax.experimental.pallas import tpu as pltpu
from jax.sharding import PartitionSpec as P

BF16_ROWS = 16
LANES = 128
MIB = 1024 * 1024


def padded_rows(count):
    return -(-count // BF16_ROWS) * BF16_ROWS


def passed_along(block, axis, distance):
    size = lax.axis_size(axis)
    return lax.ppermute(block, axis, [(i, (i + distance) % size) for i in range(size)])


def all_along(block, axis):
    return [block] + [passed_along(block, axis, k) for k in range(1, lax.axis_size(axis))]


def by_doubling(block, axis):
    size, reach = lax.axis_size(axis), 1
    while reach < size:
        partner = lax.ppermute(block, axis, [(i, i ^ reach) for i in range(size)])
        block = jnp.concatenate([block, partner], axis=0)
        reach *= 2
    return block


def from_place(parts, here, place):
    chosen = parts[0]
    for k in range(1, len(parts)):
        chosen = jnp.where(lax.rem(here - k + len(parts), len(parts)) == place, parts[k], chosen)
    return chosen


def pack_kernel(dims, slots_ref, state_ref, land_ref, earlier_ref, field_ref):
    steps, local, forced, vp, fp = dims
    field_ref[...] = jnp.zeros(field_ref.shape, field_ref.dtype)
    for i in range(local):
        field_ref[i, 0 : state_ref.shape[1]] = state_ref[i]
        for t in range(steps):
            first = (t * local + i) * forced
            field_ref[i, vp + fp * t : vp + fp * t + forced] = slots_ref[first : first + forced]
        field_ref[i, vp + fp * steps : vp + fp * steps + 1] = land_ref[i : i + 1].astype(jnp.bfloat16)


def group_kernel(dims, place_ref, index_ref, *rest):
    steps, bands, local, forced, vp, fp = dims
    fields, group_ref = rest[:bands], rest[bands]
    for b in range(bands):
        field = from_place([f[...] for f in fields], place_ref[1], b)
        for i in range(local):
            for t in range(steps):
                first = ((b * local + i) * steps + t) * forced
                group_ref[first : first + forced] = field[i, vp + fp * t : vp + fp * t + forced].astype(jnp.float32)
    last = bands * local * steps * forced
    group_ref[last : last + 1] = jnp.full((1, group_ref.shape[1]), index_ref[0], jnp.int32).astype(jnp.float32)


def put_taps(taps, value, row, cols, spacing):
    chans, lon = value.shape
    lane = lax.broadcasted_iota(jnp.int32, (chans, lon), 1)
    zero = jnp.zeros_like(value)
    base = 3 * chans * row
    taps[base : base + chans, cols] = jnp.where(lane >= spacing, pltpu.roll(value, spacing, 1), zero)
    taps[base + chans : base + 2 * chans, cols] = value
    taps[base + 2 * chans : base + 3 * chans, cols] = jnp.where(
        lane < lon - spacing, pltpu.roll(value, lon - spacing, 1), zero
    )


def first_kernel(dims, scalar_ref, owner_ref, enc_w_ref, dec_w_ref, settings_ref, scale_w_ref, shift_w_ref, *rest):
    steps, layers, bands, local, members, lon, chans, vp, fp, turns = dims
    fields, rest = rest[:bands], rest[bands:]
    everyone, rest = rest[0], rest[1:]
    forced = enc_w_ref.shape[0] - dec_w_ref.shape[0]
    used = bands * local * steps * forced
    group = [everyone.at[k * (used + 8) : (k + 1) * (used + 8)] for k in range(members * turns)]
    field_ref, scale_ref, shift_ref, enc_ref, dec_ref, hidden_ref, taps_ref, turned = rest
    varied = dec_w_ref.shape[0]
    turned[...] = jnp.zeros(turned.shape, turned.dtype)
    turned[0:varied] = enc_w_ref[0:varied].astype(jnp.float32)
    turned[vp : vp + forced] = enc_w_ref[varied : varied + forced].astype(jnp.float32)
    enc_ref[...] = turned[...].T.astype(jnp.bfloat16)
    dec_ref[...] = jnp.zeros(dec_ref.shape, dec_ref.dtype)
    dec_ref[0:varied, :] = dec_w_ref[...]
    band = scalar_ref[1]
    for b in range(bands):
        field_ref[b * local : (b + 1) * local] = from_place([f[...] for f in fields], band, b)
    for i in range(bands * local):
        for t in range(steps):
            rows = slice((i * steps + t) * forced, (i * steps + t + 1) * forced)
            place = scalar_ref[2] ^ owner_ref[t]
            force = group[0][rows, :]
            for k in range(1, members * turns):
                force = jnp.where(place == k, group[k][rows, :], force)
            field_ref[i, vp + fp * t : vp + fp * t + forced, :] = force.astype(jnp.bfloat16)

    settings = settings_ref[...]
    numbers = lax.broadcasted_iota(jnp.int32, settings.shape, 0).astype(jnp.float32)
    for m, entry in enumerate(group):
        chosen = entry[used : used + 1, 0 : settings.shape[1]]
        row = jnp.sum(jnp.where(numbers == chosen, settings, 0.0), axis=0, keepdims=True)
        cols = slice((m % members) * lon, (m % members + 1) * lon)
        scale = 1.0 + jnp.sum(scale_w_ref[...] * row, axis=1, keepdims=True)
        shift = jnp.sum(shift_w_ref[...] * row, axis=1, keepdims=True)
        scale_ref[m // members, :, cols] = jnp.broadcast_to(scale, (chans, lon))
        shift_ref[m // members, :, cols] = jnp.broadcast_to(shift, (chans, lon))

    if turns == 1:
        for i in range(bands * local):
            land = field_ref[i, vp + fp * steps : vp + fp * steps + 1, :].astype(jnp.float32)
            lifted = jnp.dot(enc_ref[...], field_ref[i, 0 : vp + fp, :], preferred_element_type=jnp.float32)
            for m in range(members):
                cols = slice(m * lon, (m + 1) * lon)
                value = land * (lifted * scale_ref[0, :, cols] + shift_ref[0, :, cols])
                value = value.astype(jnp.bfloat16)
                hidden_ref[i, :, cols] = value
                put_taps(taps_ref, value, i, cols, 1)


def after_kernel(*refs):
    pass


def after(section, *earlier):
    whole = pl.BlockSpec(memory_space=pl.ANY)
    return pl.pallas_call(
        after_kernel,
        out_shape=jax.ShapeDtypeStruct(section.shape, section.dtype),
        in_specs=[whole] * (1 + len(earlier)),
        out_specs=whole,
        input_output_aliases={0: 0},
        compiler_params=pltpu.CompilerParams(vmem_limit_bytes=MIB),
        cost_estimate=pl.CostEstimate(flops=0, bytes_accessed=0, transcendentals=0),
    )(section, *earlier)


def window_kernel(dims, scalar_ref, field_ref, scale_ref, shift_ref, enc_ref, dec_ref, *rest):
    steps, layers, bands, local, members, lon, chans, vp, fp, turns, groups = dims
    lat = bands * local
    hidden, taps = rest[:2]
    pieces = 3 + (layers - 1) * (groups + 1) * bands
    blocks, rest = rest[2 : 2 + pieces], rest[2 + pieces :]
    final_ref, mean_ref, weights, conv, act, inputs, total, sems = rest[:8]
    here, band = scalar_ref[0], scalar_ref[1]
    taps_wide, wide = 9 * chans, 3 * chans
    part = chans // bands

    pltpu.make_async_copy(blocks[0], weights.at[here, :, pl.ds(0, taps_wide)], sems.at[here]).start()
    pltpu.make_async_copy(blocks[1], weights.at[here, :, pl.ds(taps_wide, chans)], sems.at[here]).start()
    pltpu.make_async_copy(blocks[2], weights.at[here, :, pl.ds(10 * chans, LANES)], sems.at[here]).start()
    share = 5 * chans // groups
    for k in range(1, layers):
        slot = lax.rem(here - k + layers, layers)
        for g in range(groups + 1):
            if g < groups:
                place = lax.rem(scalar_ref[3] - g + groups, groups)
                cols = pl.ds(pl.multiple_of(place * share, LANES), share)
            else:
                cols = pl.ds(groups * share, 10 * chans + LANES - groups * share)
            for j in range(bands):
                rows = pl.ds(pl.multiple_of(lax.rem(band - j + bands, bands) * part, part), part)
                block = blocks[3 + ((k - 1) * (groups + 1) + g) * bands + j]
                pltpu.make_async_copy(block, weights.at[slot, rows, cols], sems.at[slot]).start()

    if turns > 1:
        hidden, taps = rest[8:]

    def columns(m):
        return slice(m * lon, (m + 1) * lon)

    land = [field_ref[i, vp + fp * steps : vp + fp * steps + 1, :].astype(jnp.float32) for i in range(lat)]

    def put_hidden(i, m, value, layer):
        value = value.astype(jnp.bfloat16)
        hidden[i, :, columns(m)] = value
        if layer is not None:
            put_taps(taps, value, i, columns(m), 2 ** (layer % 3))

    def encode(step, turn):
        for i in range(lat):
            force = field_ref[i, vp + fp * step : vp + fp * (step + 1), :]
            for m in range(members):
                inputs[i, vp : vp + fp, columns(m)] = force
                if step == 0:
                    inputs[i, 0:vp, columns(m)] = field_ref[i, 0:vp, :]
            lifted = jnp.dot(enc_ref[...], inputs[i], preferred_element_type=jnp.float32)
            for m in range(members):
                value = lifted[:, columns(m)] * scale_ref[turn, :, columns(m)] + shift_ref[turn, :, columns(m)]
                put_hidden(i, m, land[i] * value, 0)

    def activate(value, layer):
        centred = value - jnp.sum(value, axis=0, keepdims=True) * (1.0 / chans)
        spread = jnp.sum(centred * centred, axis=0, keepdims=True) * (1.0 / chans)
        normed = (centred * lax.rsqrt(spread + 1e-05)).astype(jnp.bfloat16) * weights[layer, :, 10 * chans :]
        inner = normed * (normed * normed * 0.0356774081 + 0.7978845608)
        half = normed * 0.5
        return half + half * jnp.tanh(inner)

    def block(layer, not_yet):
        if not_yet is True:
            pltpu.make_async_copy(weights.at[layer], weights.at[layer], sems.at[layer]).wait()
        elif not_yet is not None:

            @pl.when(not_yet)
            def _():
                pltpu.make_async_copy(weights.at[layer], weights.at[layer], sems.at[layer]).wait()

        for i in range(lat):
            low, high = max(i - 1, 0), min(i + 1, lat - 1)
            conv[i] = jnp.dot(
                weights[layer, :, (low - i + 1) * wide : (high - i + 2) * wide],
                taps[low * wide : (high + 1) * wide, :],
                preferred_element_type=jnp.float32,
            )
        for i in range(lat):
            mix(i, i, land[i], layer)

    def mix(i, row, sea, layer):
        for m in range(members):
            act[i, :, columns(m)] = activate(conv[i, :, columns(m)], layer)
        mixed = jnp.dot(weights[layer, :, taps_wide : 10 * chans], act[i], preferred_element_type=jnp.float32)
        for m in range(members):
            kept = hidden[row, :, columns(m)].astype(jnp.float32)
            later = layer + 1 if layer + 1 < layers else None
            put_hidden(row, m, sea * (kept + mixed[:, columns(m)]), later)

    def decode(row, sea, step):
        change = jnp.dot(dec_ref[...], hidden[row], preferred_element_type=jnp.float32)
        for m in range(members):
            old = field_ref[row, 0:vp, :] if step == 0 else inputs[row, 0:vp, columns(m)]
            new = old.astype(jnp.float32) + sea * change[:, columns(m)]
            inputs[row, 0:vp, columns(m)] = new.astype(jnp.bfloat16)

    def last_block(layer):
        first = pl.multiple_of((1 - band) * wide, wide)
        conv[0] = jnp.dot(weights[layer, :, pl.ds(first, 2 * wide)], taps[...], preferred_element_type=jnp.float32)
        sea = field_ref[band, vp + fp * steps : vp + fp * steps + 1, :].astype(jnp.float32)
        mix(0, band, sea, layer)
        decode(band, sea, steps - 1)

    varied = final_ref.shape[1]

    def window(turn, first):
        for step in range(steps):
            if step > 0 or turns > 1:
                encode(step, turn)
            own_row = step == steps - 1 and step > 0 and lat == 2 and local == 1
            for layer in range(layers):
                if own_row and layer == layers - 1:
                    last_block(layer)
                else:
                    block(layer, first if step == 0 else None)
            if not own_row:
                for i in range(lat):
                    decode(i, land[i], step)
        for i in range(local):
            row = band * local + i
            summed = inputs[row, 0:vp, columns(0)].astype(jnp.float32)
            for m in range(1, members):
                summed = summed + inputs[row, 0:vp, columns(m)].astype(jnp.float32)
            if turns == 1:
                mean_ref[:, i, :] = summed[0:varied] * (1.0 / members)
                final_ref[i] = inputs[row, 0:varied, columns(0)]
            else:
                total[i] = jnp.where(first, summed, total[i] + summed)
                mean_ref[:, i, :] = total[i, 0:varied] * (1.0 / (members * turns))

                @pl.when(first)
                def _():
                    final_ref[i] = inputs[row, 0:varied, columns(0)]

    if turns == 1:
        window(0, True)
    else:
        lax.fori_loop(0, turns, lambda turn, _: window(turn, turn == 0), None)


def per_device(
    init_state,
    forcing_slots,
    atmos_owner,
    land_mask,
    param_index,
    settings,
    scale_weight,
    shift_weight,
    encode_weight,
    conv_weight,
    point_weight,
    norm_gain,
    decode_weight,
):
    members, layers, bands = (lax.axis_size(a) for a in ("members", "segment", "rows"))
    here, band = lax.axis_index("segment"), lax.axis_index("rows")
    _, local, varied, lon = init_state.shape
    steps, forced = forcing_slots.shape[2], forcing_slots.shape[4]
    chans = conv_weight.shape[1]
    lat = local * bands
    vp, fp = padded_rows(varied), padded_rows(forced)
    part = chans // bands
    at_once = next(n for n in (4, 2, 1) if members % n == 0)
    turns, wide = members // at_once, at_once * lon
    smem, vmem, whole = (pl.BlockSpec(memory_space=s) for s in (pltpu.SMEM, pltpu.VMEM, pl.ANY))
    small, large = (pltpu.CompilerParams(vmem_limit_bytes=n * MIB) for n in (8, 16 + 2 * layers))
    free = pl.CostEstimate(flops=0, bytes_accessed=0, transcendentals=0)

    groups = lax.axis_size("groups")
    share = 5 * chans // groups
    places = [here, band, lax.axis_index("members"), lax.axis_index("groups")]
    scalars = jnp.stack(places).astype(jnp.int32)
    slots = forcing_slots[0, 0].reshape(-1, lon)
    conv = conv_weight[0]
    relayed = lax.dynamic_slice(conv, (band * part, places[3] * share), (part, share))
    spread = jnp.broadcast_to(norm_gain[0][:, None], (chans, LANES))
    direct = jnp.concatenate([conv[:, groups * share :], point_weight[0], spread], axis=1)
    direct = lax.dynamic_slice_in_dim(direct, band * part, part, 0)
    field = pl.pallas_call(
        functools.partial(pack_kernel, (steps, local, forced, vp, fp)),
        out_shape=jax.ShapeDtypeStruct((local, vp + fp * steps + BF16_ROWS, lon), jnp.bfloat16),
        in_specs=[vmem] * 3 + [whole],
        out_specs=vmem,
        compiler_params=small,
        cost_estimate=free,
    )(slots, init_state[0], land_mask, direct)
    relayed, direct = (all_along(piece, "segment")[1:] for piece in (relayed, direct))
    fields = all_along(field, "rows")
    group = pl.pallas_call(
        functools.partial(group_kernel, (steps, bands, local, forced, vp, fp)),
        out_shape=jax.ShapeDtypeStruct((lat * steps * forced + 8, lon), jnp.float32),
        in_specs=[smem, smem] + [vmem] * bands,
        out_specs=vmem,
        compiler_params=small,
        cost_estimate=free,
    )(scalars, param_index, *fields)
    group = by_doubling(group, "members")

    dims = (steps, layers, bands, local, at_once, lon, chans, vp, fp, turns)
    field, scale, shift, enc, dec, hidden, taps = pl.pallas_call(
        functools.partial(first_kernel, dims),
        out_shape=(
            jax.ShapeDtypeStruct((lat, vp + fp * steps + BF16_ROWS, lon), jnp.bfloat16),
            jax.ShapeDtypeStruct((turns, chans, wide), jnp.float32),
            jax.ShapeDtypeStruct((turns, chans, wide), jnp.float32),
            jax.ShapeDtypeStruct((chans, vp + fp), jnp.bfloat16),
            jax.ShapeDtypeStruct((vp, chans), jnp.bfloat16),
            jax.ShapeDtypeStruct((lat, chans, wide), jnp.bfloat16),
            jax.ShapeDtypeStruct((lat * 3 * chans, wide), jnp.bfloat16),
        ),
        in_specs=[smem, smem] + [vmem] * (6 + bands),
        out_specs=(vmem,) * 7,
        scratch_shapes=[pltpu.VMEM((vp + fp, chans), jnp.float32)],
        compiler_params=small,
        cost_estimate=free,
    )(scalars, atmos_owner[0], encode_weight.T, decode_weight, settings, scale_weight.T, shift_weight.T, *fields, group)

    blocks = [conv_weight[0], point_weight[0], spread]
    for k in range(layers - 1):
        shares = all_along(relayed[k], "groups")
        early = all_along(shares[0], "rows")
        blocks += early
        for shared in shares[1:]:
            blocks += all_along(shared, "rows")
        blocks += all_along(after(direct[k], group, *shares[1:], *early[1:]), "rows")

    scratch = [
        pltpu.VMEM((layers, chans, 10 * chans + LANES), jnp.bfloat16),
        pltpu.VMEM((lat, chans, wide), jnp.float32),
        pltpu.VMEM((lat, chans, wide), jnp.bfloat16),
        pltpu.VMEM((lat, vp + fp, wide), jnp.bfloat16),
        pltpu.VMEM((local, vp, lon), jnp.float32),
        pltpu.SemaphoreType.DMA((layers,)),
    ]
    if turns > 1:
        scratch += [pltpu.VMEM(hidden.shape, jnp.bfloat16), pltpu.VMEM(taps.shape, jnp.bfloat16)]
    final, mean = pl.pallas_call(
        functools.partial(window_kernel, dims + (groups,)),
        out_shape=(
            jax.ShapeDtypeStruct((local, varied, lon), jnp.bfloat16),
            jax.ShapeDtypeStruct((varied, local, lon), jnp.float32),
        ),
        in_specs=[smem] + [vmem] * 7 + [whole] * len(blocks),
        out_specs=(vmem, vmem),
        scratch_shapes=scratch,
        compiler_params=large,
        cost_estimate=free,
    )(scalars, field, scale, shift, enc, dec, hidden, taps, *blocks)
    return final[None, None], jnp.swapaxes(mean, 0, 1)[None]
def solution(mesh):
    in_specs = (
        P(("groups", "segment"), "rows", None, None),
        P("members", ("groups", "segment"), None, "rows", None, None),
        P(("groups", "segment"), None),
        P(("groups", "rows"), None),
        P(("groups", "members")),
        P(),
        P(),
        P(),
        P(),
        P("segment", None, None),
        P("segment", None, None),
        P("segment", None),
        P(),
    )
    out_specs = (
        P("members", ("groups", "segment"), "rows", None, None),
        P(("groups", "segment"), "rows", None, None),
    )
    return jax.shard_map(
        per_device, mesh=mesh, in_specs=in_specs, out_specs=out_specs, check_vma=False
    )
```

```python
import functools

import jax
import jax.numpy as jnp
from jax import lax
from jax.experimental import pallas as pl
from jax.experimental.pallas import tpu as pltpu
from jax.sharding import PartitionSpec as P

BF16_ROWS = 16
LANES = 128
MIB = 1024 * 1024


def padded_rows(count):
    return -(-count // BF16_ROWS) * BF16_ROWS


def passed_along(block, axis, distance):
    size = lax.axis_size(axis)
    return lax.ppermute(block, axis, [(i, (i + distance) % size) for i in range(size)])


def all_along(block, axis):
    return [block] + [passed_along(block, axis, k) for k in range(1, lax.axis_size(axis))]


def by_doubling(block, axis):
    size, reach = lax.axis_size(axis), 1
    while reach < size:
        partner = lax.ppermute(block, axis, [(i, i ^ reach) for i in range(size)])
        block = jnp.concatenate([block, partner], axis=0)
        reach *= 2
    return block


def from_place(parts, here, place):
    chosen = parts[0]
    for k in range(1, len(parts)):
        chosen = jnp.where(lax.rem(here - k + len(parts), len(parts)) == place, parts[k], chosen)
    return chosen


def pack_kernel(dims, slots_ref, state_ref, land_ref, index_ref, earlier_ref, field_ref):
    steps, local, forced, vp, fp = dims
    field_ref[...] = jnp.zeros(field_ref.shape, field_ref.dtype)
    for i in range(local):
        field_ref[i, 0 : state_ref.shape[1]] = state_ref[i]
        for t in range(steps):
            first = (t * local + i) * forced
            field_ref[i, vp + fp * t : vp + fp * t + forced] = slots_ref[first : first + forced]
        last = vp + fp * steps
        field_ref[i, last : last + 1] = land_ref[i : i + 1].astype(jnp.bfloat16)
        index = jnp.broadcast_to(index_ref[...], land_ref[i : i + 1].shape)
        field_ref[i, last + 1 : last + 2] = (index & 255).astype(jnp.float32).astype(jnp.bfloat16)
        field_ref[i, last + 2 : last + 3] = (index >> 8).astype(jnp.float32).astype(jnp.bfloat16)


def group_kernel(dims, place_ref, *rest):
    steps, bands, local, forced, vp, fp = dims
    fields, group_ref = rest[:bands], rest[bands]
    for b in range(bands):
        field = from_place([f[...] for f in fields], place_ref[1], b)
        for i in range(local):
            for t in range(steps):
                first = ((b * local + i) * steps + t) * forced
                group_ref[first : first + forced] = field[i, vp + fp * t : vp + fp * t + forced].astype(jnp.float32)
    last = bands * local * steps * forced
    row = vp + fp * steps + 1
    low, high = (fields[0][0, r : r + 1].astype(jnp.float32) for r in (row, row + 1))
    group_ref[last : last + 1] = low + 256.0 * high


def put_taps(taps, value, row, cols, spacing):
    chans, lon = value.shape
    lane = lax.broadcasted_iota(jnp.int32, (chans, lon), 1)
    zero = jnp.zeros_like(value)
    base = 3 * chans * row
    taps[base : base + chans, cols] = jnp.where(lane >= spacing, pltpu.roll(value, spacing, 1), zero)
    taps[base + chans : base + 2 * chans, cols] = value
    taps[base + 2 * chans : base + 3 * chans, cols] = jnp.where(
        lane < lon - spacing, pltpu.roll(value, lon - spacing, 1), zero
    )


def first_kernel(dims, scalar_ref, owner_ref, enc_w_ref, dec_w_ref, settings_ref, scale_w_ref, shift_w_ref, *rest):
    steps, layers, bands, local, members, lon, chans, vp, fp, turns = dims
    fields, rest = rest[:bands], rest[bands:]
    everyone, rest = rest[0], rest[1:]
    forced = enc_w_ref.shape[0] - dec_w_ref.shape[0]
    used = bands * local * steps * forced
    group = [everyone.at[k * (used + 8) : (k + 1) * (used + 8)] for k in range(members * turns)]
    field_ref, scale_ref, shift_ref, enc_ref, dec_ref, hidden_ref, taps_ref, turned = rest
    varied = dec_w_ref.shape[0]
    turned[...] = jnp.zeros(turned.shape, turned.dtype)
    turned[0:varied] = enc_w_ref[0:varied].astype(jnp.float32)
    turned[vp : vp + forced] = enc_w_ref[varied : varied + forced].astype(jnp.float32)
    enc_ref[...] = turned[...].T.astype(jnp.bfloat16)
    dec_ref[...] = jnp.zeros(dec_ref.shape, dec_ref.dtype)
    dec_ref[0:varied, :] = dec_w_ref[...]
    band = scalar_ref[1]
    for b in range(bands):
        field_ref[b * local : (b + 1) * local] = from_place([f[...] for f in fields], band, b)
    for i in range(bands * local):
        for t in range(steps):
            rows = slice((i * steps + t) * forced, (i * steps + t + 1) * forced)
            place = scalar_ref[2] ^ owner_ref[t]
            force = group[0][rows, :]
            for k in range(1, members * turns):
                force = jnp.where(place == k, group[k][rows, :], force)
            field_ref[i, vp + fp * t : vp + fp * t + forced, :] = force.astype(jnp.bfloat16)

    settings = settings_ref[...]
    numbers = lax.broadcasted_iota(jnp.int32, settings.shape, 0).astype(jnp.float32)
    for m, entry in enumerate(group):
        chosen = entry[used : used + 1, 0 : settings.shape[1]]
        row = jnp.sum(jnp.where(numbers == chosen, settings, 0.0), axis=0, keepdims=True)
        cols = slice((m % members) * lon, (m % members + 1) * lon)
        scale = 1.0 + jnp.sum(scale_w_ref[...] * row, axis=1, keepdims=True)
        shift = jnp.sum(shift_w_ref[...] * row, axis=1, keepdims=True)
        scale_ref[m // members, :, cols] = jnp.broadcast_to(scale, (chans, lon))
        shift_ref[m // members, :, cols] = jnp.broadcast_to(shift, (chans, lon))

    if turns == 1:
        for i in range(bands * local):
            land = field_ref[i, vp + fp * steps : vp + fp * steps + 1, :].astype(jnp.float32)
            lifted = jnp.dot(enc_ref[...], field_ref[i, 0 : vp + fp, :], preferred_element_type=jnp.float32)
            for m in range(members):
                cols = slice(m * lon, (m + 1) * lon)
                value = land * (lifted * scale_ref[0, :, cols] + shift_ref[0, :, cols])
                value = value.astype(jnp.bfloat16)
                hidden_ref[i, :, cols] = value
                put_taps(taps_ref, value, i, cols, 1)


def after_kernel(*refs):
    pass


def after(section, *earlier):
    whole = pl.BlockSpec(memory_space=pl.ANY)
    return pl.pallas_call(
        after_kernel,
        out_shape=jax.ShapeDtypeStruct(section.shape, section.dtype),
        in_specs=[whole] * (1 + len(earlier)),
        out_specs=whole,
        input_output_aliases={0: 0},
        compiler_params=pltpu.CompilerParams(vmem_limit_bytes=MIB),
        cost_estimate=pl.CostEstimate(flops=0, bytes_accessed=0, transcendentals=0),
    )(section, *earlier)


def window_kernel(dims, scalar_ref, field_ref, scale_ref, shift_ref, enc_ref, dec_ref, *rest):
    steps, layers, bands, local, members, lon, chans, vp, fp, turns, groups = dims
    lat = bands * local
    hidden, taps = rest[:2]
    pieces = 3 + (layers - 1) * (groups + 1) * bands
    blocks, rest = rest[2 : 2 + pieces], rest[2 + pieces :]
    final_ref, mean_ref, weights, conv, act, inputs, total, sems = rest[:8]
    here, band = scalar_ref[0], scalar_ref[1]
    taps_wide, wide = 9 * chans, 3 * chans
    part = chans // bands

    def own_block():
        pltpu.make_async_copy(blocks[0], weights.at[here, :, pl.ds(0, taps_wide)], sems.at[here]).start()
        pltpu.make_async_copy(blocks[1], weights.at[here, :, pl.ds(taps_wide, chans)], sems.at[here]).start()
        pltpu.make_async_copy(blocks[2], weights.at[here, :, pl.ds(10 * chans, LANES)], sems.at[here]).start()

    pl.when(here == 0)(own_block)
    share = 5 * chans // groups
    for k in range(1, layers):
        slot = lax.rem(here - k + layers, layers)
        for g in range(groups + 1):
            if g < groups:
                place = lax.rem(scalar_ref[3] - g + groups, groups)
                cols = pl.ds(pl.multiple_of(place * share, LANES), share)
            else:
                cols = pl.ds(groups * share, 10 * chans + LANES - groups * share)
            for j in range(bands):
                rows = pl.ds(pl.multiple_of(lax.rem(band - j + bands, bands) * part, part), part)
                block = blocks[3 + ((k - 1) * (groups + 1) + g) * bands + j]
                pltpu.make_async_copy(block, weights.at[slot, rows, cols], sems.at[slot]).start()

    pl.when(here != 0)(own_block)
    if turns > 1:
        hidden, taps = rest[8:]

    def columns(m):
        return slice(m * lon, (m + 1) * lon)

    land = [field_ref[i, vp + fp * steps : vp + fp * steps + 1, :].astype(jnp.float32) for i in range(lat)]

    def put_hidden(i, m, value, layer):
        value = value.astype(jnp.bfloat16)
        hidden[i, :, columns(m)] = value
        if layer is not None:
            put_taps(taps, value, i, columns(m), 2 ** (layer % 3))

    def encode(step, turn):
        for i in range(lat):
            force = field_ref[i, vp + fp * step : vp + fp * (step + 1), :]
            for m in range(members):
                inputs[i, vp : vp + fp, columns(m)] = force
                if step == 0:
                    inputs[i, 0:vp, columns(m)] = field_ref[i, 0:vp, :]
            lifted = jnp.dot(enc_ref[...], inputs[i], preferred_element_type=jnp.float32)
            for m in range(members):
                value = lifted[:, columns(m)] * scale_ref[turn, :, columns(m)] + shift_ref[turn, :, columns(m)]
                put_hidden(i, m, land[i] * value, 0)

    def activate(value, layer):
        centred = value - jnp.sum(value, axis=0, keepdims=True) * (1.0 / chans)
        spread = jnp.sum(centred * centred, axis=0, keepdims=True) * (1.0 / chans)
        normed = (centred * lax.rsqrt(spread + 1e-05)).astype(jnp.bfloat16) * weights[layer, :, 10 * chans :]
        inner = normed * (normed * normed * 0.0356774081 + 0.7978845608)
        half = normed * 0.5
        return half + half * jnp.tanh(inner)

    def block(layer, not_yet):
        if not_yet is True:
            pltpu.make_async_copy(weights.at[layer], weights.at[layer], sems.at[layer]).wait()
        elif not_yet is not None:

            @pl.when(not_yet)
            def _():
                pltpu.make_async_copy(weights.at[layer], weights.at[layer], sems.at[layer]).wait()

        for i in range(lat):
            low, high = max(i - 1, 0), min(i + 1, lat - 1)
            conv[i] = jnp.dot(
                weights[layer, :, (low - i + 1) * wide : (high - i + 2) * wide],
                taps[low * wide : (high + 1) * wide, :],
                preferred_element_type=jnp.float32,
            )
        for i in range(lat):
            mix(i, i, land[i], layer)

    def mix(i, row, sea, layer):
        for m in range(members):
            act[i, :, columns(m)] = activate(conv[i, :, columns(m)], layer)
        mixed = jnp.dot(weights[layer, :, taps_wide : 10 * chans], act[i], preferred_element_type=jnp.float32)
        for m in range(members):
            kept = hidden[row, :, columns(m)].astype(jnp.float32)
            later = layer + 1 if layer + 1 < layers else None
            put_hidden(row, m, sea * (kept + mixed[:, columns(m)]), later)

    def decode(row, sea, step):
        change = jnp.dot(dec_ref[...], hidden[row], preferred_element_type=jnp.float32)
        for m in range(members):
            old = field_ref[row, 0:vp, :] if step == 0 else inputs[row, 0:vp, columns(m)]
            new = old.astype(jnp.float32) + sea * change[:, columns(m)]
            inputs[row, 0:vp, columns(m)] = new.astype(jnp.bfloat16)

    def last_block(layer):
        first = pl.multiple_of((1 - band) * wide, wide)
        conv[0] = jnp.dot(weights[layer, :, pl.ds(first, 2 * wide)], taps[...], preferred_element_type=jnp.float32)
        sea = field_ref[band, vp + fp * steps : vp + fp * steps + 1, :].astype(jnp.float32)
        mix(0, band, sea, layer)
        decode(band, sea, steps - 1)

    varied = final_ref.shape[1]

    def window(turn, first):
        for step in range(steps):
            if step > 0 or turns > 1:
                encode(step, turn)
            own_row = step == steps - 1 and step > 0 and lat == 2 and local == 1
            for layer in range(layers):
                if own_row and layer == layers - 1:
                    last_block(layer)
                else:
                    block(layer, first if step == 0 else None)
            if not own_row:
                for i in range(lat):
                    decode(i, land[i], step)
        for i in range(local):
            row = band * local + i
            summed = inputs[row, 0:vp, columns(0)].astype(jnp.float32)
            for m in range(1, members):
                summed = summed + inputs[row, 0:vp, columns(m)].astype(jnp.float32)
            if turns == 1:
                mean_ref[:, i, :] = summed[0:varied] * (1.0 / members)
                final_ref[i] = inputs[row, 0:varied, columns(0)]
            else:
                total[i] = jnp.where(first, summed, total[i] + summed)
                mean_ref[:, i, :] = total[i, 0:varied] * (1.0 / (members * turns))

                @pl.when(first)
                def _():
                    final_ref[i] = inputs[row, 0:varied, columns(0)]

    if turns == 1:
        window(0, True)
    else:
        lax.fori_loop(0, turns, lambda turn, _: window(turn, turn == 0), None)


def per_device(
    init_state,
    forcing_slots,
    atmos_owner,
    land_mask,
    param_index,
    settings,
    scale_weight,
    shift_weight,
    encode_weight,
    conv_weight,
    point_weight,
    norm_gain,
    decode_weight,
):
    members, layers, bands = (lax.axis_size(a) for a in ("members", "segment", "rows"))
    here, band = lax.axis_index("segment"), lax.axis_index("rows")
    _, local, varied, lon = init_state.shape
    steps, forced = forcing_slots.shape[2], forcing_slots.shape[4]
    chans = conv_weight.shape[1]
    lat = local * bands
    vp, fp = padded_rows(varied), padded_rows(forced)
    part = chans // bands
    at_once = next(n for n in (4, 2, 1) if members % n == 0)
    turns, wide = members // at_once, at_once * lon
    smem, vmem, whole = (pl.BlockSpec(memory_space=s) for s in (pltpu.SMEM, pltpu.VMEM, pl.ANY))
    small, large = (pltpu.CompilerParams(vmem_limit_bytes=n * MIB) for n in (8, 16 + 2 * layers))
    free = pl.CostEstimate(flops=0, bytes_accessed=0, transcendentals=0)

    groups = lax.axis_size("groups")
    share = 5 * chans // groups
    places = [here, band, lax.axis_index("members"), lax.axis_index("groups")]
    scalars = jnp.stack(places).astype(jnp.int32)
    slots = forcing_slots[0, 0].reshape(-1, lon)
    conv = conv_weight[0]
    relayed = lax.dynamic_slice(conv, (band * part, places[3] * share), (part, share))
    spread = jnp.broadcast_to(norm_gain[0][:, None], (chans, LANES))
    direct = jnp.concatenate([conv[:, groups * share :], point_weight[0], spread], axis=1)
    direct = lax.dynamic_slice_in_dim(direct, band * part, part, 0)
    field = pl.pallas_call(
        functools.partial(pack_kernel, (steps, local, forced, vp, fp)),
        out_shape=jax.ShapeDtypeStruct((local, vp + fp * steps + BF16_ROWS, lon), jnp.bfloat16),
        in_specs=[vmem] * 4 + [whole],
        out_specs=vmem,
        compiler_params=small,
        cost_estimate=free,
    )(slots, init_state[0], land_mask, param_index[None], direct)
    relayed, direct = (all_along(piece, "segment")[1:] for piece in (relayed, direct))
    fields = all_along(field, "rows")
    group = pl.pallas_call(
        functools.partial(group_kernel, (steps, bands, local, forced, vp, fp)),
        out_shape=jax.ShapeDtypeStruct((lat * steps * forced + 8, lon), jnp.float32),
        in_specs=[smem] + [vmem] * bands,
        out_specs=vmem,
        compiler_params=small,
        cost_estimate=free,
    )(scalars, *fields)
    group = by_doubling(group, "members")

    dims = (steps, layers, bands, local, at_once, lon, chans, vp, fp, turns)
    field, scale, shift, enc, dec, hidden, taps = pl.pallas_call(
        functools.partial(first_kernel, dims),
        out_shape=(
            jax.ShapeDtypeStruct((lat, vp + fp * steps + BF16_ROWS, lon), jnp.bfloat16),
            jax.ShapeDtypeStruct((turns, chans, wide), jnp.float32),
            jax.ShapeDtypeStruct((turns, chans, wide), jnp.float32),
            jax.ShapeDtypeStruct((chans, vp + fp), jnp.bfloat16),
            jax.ShapeDtypeStruct((vp, chans), jnp.bfloat16),
            jax.ShapeDtypeStruct((lat, chans, wide), jnp.bfloat16),
            jax.ShapeDtypeStruct((lat * 3 * chans, wide), jnp.bfloat16),
        ),
        in_specs=[smem, smem] + [vmem] * (6 + bands),
        out_specs=(vmem,) * 7,
        scratch_shapes=[pltpu.VMEM((vp + fp, chans), jnp.float32)],
        compiler_params=small,
        cost_estimate=free,
    )(scalars, atmos_owner[0], encode_weight.T, decode_weight, settings, scale_weight.T, shift_weight.T, *fields, group)

    blocks = [conv_weight[0], point_weight[0], spread]
    for k in range(layers - 1):
        shares = all_along(relayed[k], "groups")
        early = all_along(shares[0], "rows")
        blocks += early
        for shared in shares[1:]:
            blocks += all_along(shared, "rows")
        blocks += all_along(after(direct[k], group, *shares[1:], *early[1:]), "rows")

    scratch = [
        pltpu.VMEM((layers, chans, 10 * chans + LANES), jnp.bfloat16),
        pltpu.VMEM((lat, chans, wide), jnp.float32),
        pltpu.VMEM((lat, chans, wide), jnp.bfloat16),
        pltpu.VMEM((lat, vp + fp, wide), jnp.bfloat16),
        pltpu.VMEM((local, vp, lon), jnp.float32),
        pltpu.SemaphoreType.DMA((layers,)),
    ]
    if turns > 1:
        scratch += [pltpu.VMEM(hidden.shape, jnp.bfloat16), pltpu.VMEM(taps.shape, jnp.bfloat16)]
    final, mean = pl.pallas_call(
        functools.partial(window_kernel, dims + (groups,)),
        out_shape=(
            jax.ShapeDtypeStruct((local, varied, lon), jnp.bfloat16),
            jax.ShapeDtypeStruct((varied, local, lon), jnp.float32),
        ),
        in_specs=[smem] + [vmem] * 7 + [whole] * len(blocks),
        out_specs=(vmem, vmem),
        scratch_shapes=scratch,
        compiler_params=large,
        cost_estimate=free,
    )(scalars, field, scale, shift, enc, dec, hidden, taps, *blocks)
    return final[None, None], jnp.swapaxes(mean, 0, 1)[None]
def solution(mesh):
    in_specs = (
        P(("groups", "segment"), "rows", None, None),
        P("members", ("groups", "segment"), None, "rows", None, None),
        P(("groups", "segment"), None),
        P(("groups", "rows"), None),
        P(("groups", "members")),
        P(),
        P(),
        P(),
        P(),
        P("segment", None, None),
        P("segment", None, None),
        P("segment", None),
        P(),
    )
    out_specs = (
        P("members", ("groups", "segment"), "rows", None, None),
        P(("groups", "segment"), "rows", None, None),
    )
    return jax.shard_map(
        per_device, mesh=mesh, in_specs=in_specs, out_specs=out_specs, check_vma=False
    )
```

```python
import functools

import jax
import jax.numpy as jnp
from jax import lax
from jax.experimental import pallas as pl
from jax.experimental.pallas import tpu as pltpu
from jax.sharding import PartitionSpec as P

BF16_ROWS = 16
LANES = 128
MIB = 1024 * 1024


def padded_rows(count):
    return -(-count // BF16_ROWS) * BF16_ROWS


def passed_along(block, axis, distance):
    size = lax.axis_size(axis)
    return lax.ppermute(block, axis, [(i, (i + distance) % size) for i in range(size)])


def all_along(block, axis):
    return [block] + [passed_along(block, axis, k) for k in range(1, lax.axis_size(axis))]


def by_doubling(block, axis):
    size, reach = lax.axis_size(axis), 1
    while reach < size:
        partner = lax.ppermute(block, axis, [(i, i ^ reach) for i in range(size)])
        block = jnp.concatenate([block, partner], axis=0)
        reach *= 2
    return block


def from_place(parts, here, place):
    chosen = parts[0]
    for k in range(1, len(parts)):
        chosen = jnp.where(lax.rem(here - k + len(parts), len(parts)) == place, parts[k], chosen)
    return chosen


def pack_kernel(dims, slots_ref, state_ref, land_ref, earlier_ref, field_ref):
    steps, local, forced, vp, fp = dims
    field_ref[...] = jnp.zeros(field_ref.shape, field_ref.dtype)
    for i in range(local):
        field_ref[i, 0 : state_ref.shape[1]] = state_ref[i]
        for t in range(steps):
            first = (t * local + i) * forced
            field_ref[i, vp + fp * t : vp + fp * t + forced] = slots_ref[first : first + forced]
        field_ref[i, vp + fp * steps : vp + fp * steps + 1] = land_ref[i : i + 1].astype(jnp.bfloat16)


def group_kernel(dims, place_ref, index_ref, *rest):
    steps, bands, local, forced, vp, fp = dims
    fields, group_ref = rest[:bands], rest[bands]
    for b in range(bands):
        field = from_place([f[...] for f in fields], place_ref[1], b)
        for i in range(local):
            for t in range(steps):
                first = ((b * local + i) * steps + t) * forced
                group_ref[first : first + forced] = field[i, vp + fp * t : vp + fp * t + forced].astype(jnp.float32)
    last = bands * local * steps * forced
    group_ref[last : last + 1] = jnp.full((1, group_ref.shape[1]), index_ref[0], jnp.int32).astype(jnp.float32)


def put_taps(taps, value, row, cols, spacing):
    chans, lon = value.shape
    lane = lax.broadcasted_iota(jnp.int32, (chans, lon), 1)
    zero = jnp.zeros_like(value)
    base = 3 * chans * row
    taps[base : base + chans, cols] = jnp.where(lane >= spacing, pltpu.roll(value, spacing, 1), zero)
    taps[base + chans : base + 2 * chans, cols] = value
    taps[base + 2 * chans : base + 3 * chans, cols] = jnp.where(
        lane < lon - spacing, pltpu.roll(value, lon - spacing, 1), zero
    )


def first_kernel(dims, scalar_ref, owner_ref, enc_w_ref, dec_w_ref, settings_ref, scale_w_ref, shift_w_ref, *rest):
    steps, layers, bands, local, members, lon, chans, vp, fp, turns = dims
    fields, rest = rest[:bands], rest[bands:]
    everyone, rest = rest[0], rest[1:]
    forced = enc_w_ref.shape[0] - dec_w_ref.shape[0]
    used = bands * local * steps * forced
    group = [everyone.at[k * (used + 8) : (k + 1) * (used + 8)] for k in range(members * turns)]
    field_ref, scale_ref, shift_ref, enc_ref, dec_ref, hidden_ref, taps_ref, turned, lines = rest
    varied = dec_w_ref.shape[0]
    turned[...] = jnp.zeros(turned.shape, turned.dtype)
    turned[0:varied] = enc_w_ref[0:varied].astype(jnp.float32)
    turned[vp : vp + forced] = enc_w_ref[varied : varied + forced].astype(jnp.float32)
    enc_ref[...] = turned[...].T.astype(jnp.bfloat16)
    dec_ref[...] = jnp.zeros(dec_ref.shape, dec_ref.dtype)
    dec_ref[0:varied, :] = dec_w_ref[...]
    band = scalar_ref[1]
    for b in range(bands):
        field_ref[b * local : (b + 1) * local] = from_place([f[...] for f in fields], band, b)
    for i in range(bands * local):
        for t in range(steps):
            rows = slice((i * steps + t) * forced, (i * steps + t + 1) * forced)
            place = scalar_ref[2] ^ owner_ref[t]
            force = group[0][rows, :]
            for k in range(1, members * turns):
                force = jnp.where(place == k, group[k][rows, :], force)
            field_ref[i, vp + fp * t : vp + fp * t + forced, :] = force.astype(jnp.bfloat16)

    settings = settings_ref[...]
    numbers = lax.broadcasted_iota(jnp.int32, settings.shape, 1).astype(jnp.float32)
    for m, entry in enumerate(group):
        chosen = entry[used : used + 1, 0 : settings.shape[1]]
        column = jnp.sum(jnp.where(numbers == chosen, settings, 0.0), axis=1, keepdims=True)
        lines[2 * m : 2 * m + 1] = 1.0 + jnp.sum(scale_w_ref[...] * column, axis=0, keepdims=True)
        lines[2 * m + 1 : 2 * m + 2] = jnp.sum(shift_w_ref[...] * column, axis=0, keepdims=True)
    columns = lines[...].T
    for m in range(len(group)):
        cols = slice((m % members) * lon, (m % members + 1) * lon)
        scale_ref[m // members, :, cols] = jnp.broadcast_to(columns[:, 2 * m : 2 * m + 1], (chans, lon))
        shift_ref[m // members, :, cols] = jnp.broadcast_to(columns[:, 2 * m + 1 : 2 * m + 2], (chans, lon))

    if turns == 1:
        for i in range(bands * local):
            land = field_ref[i, vp + fp * steps : vp + fp * steps + 1, :].astype(jnp.float32)
            lifted = jnp.dot(enc_ref[...], field_ref[i, 0 : vp + fp, :], preferred_element_type=jnp.float32)
            for m in range(members):
                cols = slice(m * lon, (m + 1) * lon)
                value = land * (lifted * scale_ref[0, :, cols] + shift_ref[0, :, cols])
                value = value.astype(jnp.bfloat16)
                hidden_ref[i, :, cols] = value
                put_taps(taps_ref, value, i, cols, 1)


def after_kernel(*refs):
    pass


def after(section, *earlier):
    whole = pl.BlockSpec(memory_space=pl.ANY)
    return pl.pallas_call(
        after_kernel,
        out_shape=jax.ShapeDtypeStruct(section.shape, section.dtype),
        in_specs=[whole] * (1 + len(earlier)),
        out_specs=whole,
        input_output_aliases={0: 0},
        compiler_params=pltpu.CompilerParams(vmem_limit_bytes=MIB),
        cost_estimate=pl.CostEstimate(flops=0, bytes_accessed=0, transcendentals=0),
    )(section, *earlier)


def window_kernel(dims, scalar_ref, field_ref, scale_ref, shift_ref, enc_ref, dec_ref, *rest):
    steps, layers, bands, local, members, lon, chans, vp, fp, turns, groups = dims
    lat = bands * local
    hidden, taps = rest[:2]
    pieces = 3 + (layers - 1) * (groups + 1) * bands
    blocks, rest = rest[2 : 2 + pieces], rest[2 + pieces :]
    final_ref, mean_ref, weights, conv, act, inputs, total, sems = rest[:8]
    here, band = scalar_ref[0], scalar_ref[1]
    taps_wide, wide = 9 * chans, 3 * chans
    part = chans // bands

    pltpu.make_async_copy(blocks[0], weights.at[here, :, pl.ds(0, taps_wide)], sems.at[here]).start()
    pltpu.make_async_copy(blocks[1], weights.at[here, :, pl.ds(taps_wide, chans)], sems.at[here]).start()
    pltpu.make_async_copy(blocks[2], weights.at[here, :, pl.ds(10 * chans, LANES)], sems.at[here]).start()
    share = 5 * chans // groups
    for k in range(1, layers):
        slot = lax.rem(here - k + layers, layers)
        for g in range(groups + 1):
            if g < groups:
                place = lax.rem(scalar_ref[3] - g + groups, groups)
                cols = pl.ds(pl.multiple_of(place * share, LANES), share)
            else:
                cols = pl.ds(groups * share, 10 * chans + LANES - groups * share)
            for j in range(bands):
                rows = pl.ds(pl.multiple_of(lax.rem(band - j + bands, bands) * part, part), part)
                block = blocks[3 + ((k - 1) * (groups + 1) + g) * bands + j]
                pltpu.make_async_copy(block, weights.at[slot, rows, cols], sems.at[slot]).start()

    if turns > 1:
        hidden, taps = rest[8:]

    def columns(m):
        return slice(m * lon, (m + 1) * lon)

    land = [field_ref[i, vp + fp * steps : vp + fp * steps + 1, :].astype(jnp.float32) for i in range(lat)]

    def put_hidden(i, m, value, layer):
        value = value.astype(jnp.bfloat16)
        hidden[i, :, columns(m)] = value
        if layer is not None:
            put_taps(taps, value, i, columns(m), 2 ** (layer % 3))

    def encode(step, turn):
        for i in range(lat):
            force = field_ref[i, vp + fp * step : vp + fp * (step + 1), :]
            for m in range(members):
                inputs[i, vp : vp + fp, columns(m)] = force
                if step == 0:
                    inputs[i, 0:vp, columns(m)] = field_ref[i, 0:vp, :]
            lifted = jnp.dot(enc_ref[...], inputs[i], preferred_element_type=jnp.float32)
            for m in range(members):
                value = lifted[:, columns(m)] * scale_ref[turn, :, columns(m)] + shift_ref[turn, :, columns(m)]
                put_hidden(i, m, land[i] * value, 0)

    def activate(value, layer):
        centred = value - jnp.sum(value, axis=0, keepdims=True) * (1.0 / chans)
        spread = jnp.sum(centred * centred, axis=0, keepdims=True) * (1.0 / chans)
        half = (centred * lax.rsqrt(spread + 1e-05)).astype(jnp.bfloat16) * weights[layer, :, 10 * chans :]
        inner = half * (half * half * 0.2854192648 + 1.5957691216)
        return half + half * jnp.tanh(inner)

    def block(layer, not_yet):
        if not_yet is True:
            pltpu.make_async_copy(weights.at[layer], weights.at[layer], sems.at[layer]).wait()
        elif not_yet is not None:

            @pl.when(not_yet)
            def _():
                pltpu.make_async_copy(weights.at[layer], weights.at[layer], sems.at[layer]).wait()

        for i in range(lat):
            low, high = max(i - 1, 0), min(i + 1, lat - 1)
            conv[i] = jnp.dot(
                weights[layer, :, (low - i + 1) * wide : (high - i + 2) * wide],
                taps[low * wide : (high + 1) * wide, :],
                preferred_element_type=jnp.float32,
            )
        for i in range(lat):
            mix(i, i, land[i], layer)

    def mix(i, row, sea, layer):
        for m in range(members):
            act[i, :, columns(m)] = activate(conv[i, :, columns(m)], layer)
        mixed = jnp.dot(weights[layer, :, taps_wide : 10 * chans], act[i], preferred_element_type=jnp.float32)
        for m in range(members):
            kept = hidden[row, :, columns(m)].astype(jnp.float32)
            later = layer + 1 if layer + 1 < layers else None
            put_hidden(row, m, sea * (kept + mixed[:, columns(m)]), later)

    def decode(row, sea, step):
        change = jnp.dot(dec_ref[...], hidden[row], preferred_element_type=jnp.float32)
        for m in range(members):
            old = field_ref[row, 0:vp, :] if step == 0 else inputs[row, 0:vp, columns(m)]
            new = old.astype(jnp.float32) + sea * change[:, columns(m)]
            inputs[row, 0:vp, columns(m)] = new.astype(jnp.bfloat16)

    def last_block(layer):
        first = pl.multiple_of((1 - band) * wide, wide)
        conv[0] = jnp.dot(weights[layer, :, pl.ds(first, 2 * wide)], taps[...], preferred_element_type=jnp.float32)
        sea = field_ref[band, vp + fp * steps : vp + fp * steps + 1, :].astype(jnp.float32)
        mix(0, band, sea, layer)
        decode(band, sea, steps - 1)

    varied = final_ref.shape[1]

    def window(turn, first):
        for step in range(steps):
            if step > 0 or turns > 1:
                encode(step, turn)
            own_row = step == steps - 1 and step > 0 and lat == 2 and local == 1
            for layer in range(layers):
                if own_row and layer == layers - 1:
                    last_block(layer)
                else:
                    block(layer, first if step == 0 else None)
            if not own_row:
                for i in range(lat):
                    decode(i, land[i], step)
        for i in range(local):
            row = band * local + i
            summed = inputs[row, 0:vp, columns(0)].astype(jnp.float32)
            for m in range(1, members):
                summed = summed + inputs[row, 0:vp, columns(m)].astype(jnp.float32)
            if turns == 1:
                mean_ref[:, i, :] = summed[0:varied] * (1.0 / members)
                final_ref[i] = inputs[row, 0:varied, columns(0)]
            else:
                total[i] = jnp.where(first, summed, total[i] + summed)
                mean_ref[:, i, :] = total[i, 0:varied] * (1.0 / (members * turns))

                @pl.when(first)
                def _():
                    final_ref[i] = inputs[row, 0:varied, columns(0)]

    if turns == 1:
        window(0, True)
    else:
        lax.fori_loop(0, turns, lambda turn, _: window(turn, turn == 0), None)


def per_device(
    init_state,
    forcing_slots,
    atmos_owner,
    land_mask,
    param_index,
    settings,
    scale_weight,
    shift_weight,
    encode_weight,
    conv_weight,
    point_weight,
    norm_gain,
    decode_weight,
):
    members, layers, bands = (lax.axis_size(a) for a in ("members", "segment", "rows"))
    here, band = lax.axis_index("segment"), lax.axis_index("rows")
    _, local, varied, lon = init_state.shape
    steps, forced = forcing_slots.shape[2], forcing_slots.shape[4]
    chans = conv_weight.shape[1]
    lat = local * bands
    vp, fp = padded_rows(varied), padded_rows(forced)
    part = chans // bands
    at_once = next(n for n in (4, 2, 1) if members % n == 0)
    turns, wide = members // at_once, at_once * lon
    smem, vmem, whole = (pl.BlockSpec(memory_space=s) for s in (pltpu.SMEM, pltpu.VMEM, pl.ANY))
    small, large = (pltpu.CompilerParams(vmem_limit_bytes=n * MIB) for n in (8, 16 + 2 * layers))
    free = pl.CostEstimate(flops=0, bytes_accessed=0, transcendentals=0)

    groups = lax.axis_size("groups")
    share = 5 * chans // groups
    places = [here, band, lax.axis_index("members"), lax.axis_index("groups")]
    scalars = jnp.stack(places).astype(jnp.int32)
    slots = forcing_slots[0, 0].reshape(-1, lon)
    conv = conv_weight[0]
    relayed = lax.dynamic_slice(conv, (band * part, places[3] * share), (part, share))
    spread = jnp.broadcast_to((norm_gain[0] * 0.5)[:, None], (chans, LANES))
    direct = jnp.concatenate([conv[:, groups * share :], point_weight[0], spread], axis=1)
    direct = lax.dynamic_slice_in_dim(direct, band * part, part, 0)
    field = pl.pallas_call(
        functools.partial(pack_kernel, (steps, local, forced, vp, fp)),
        out_shape=jax.ShapeDtypeStruct((local, vp + fp * steps + BF16_ROWS, lon), jnp.bfloat16),
        in_specs=[vmem] * 3 + [whole],
        out_specs=vmem,
        compiler_params=small,
        cost_estimate=free,
    )(slots, init_state[0], land_mask, direct)
    relayed, direct = (all_along(piece, "segment")[1:] for piece in (relayed, direct))
    fields = all_along(field, "rows")
    group = pl.pallas_call(
        functools.partial(group_kernel, (steps, bands, local, forced, vp, fp)),
        out_shape=jax.ShapeDtypeStruct((lat * steps * forced + 8, lon), jnp.float32),
        in_specs=[smem, smem] + [vmem] * bands,
        out_specs=vmem,
        compiler_params=small,
        cost_estimate=free,
    )(scalars, param_index, *fields)
    group = by_doubling(group, "members")

    dims = (steps, layers, bands, local, at_once, lon, chans, vp, fp, turns)
    field, scale, shift, enc, dec, hidden, taps = pl.pallas_call(
        functools.partial(first_kernel, dims),
        out_shape=(
            jax.ShapeDtypeStruct((lat, vp + fp * steps + BF16_ROWS, lon), jnp.bfloat16),
            jax.ShapeDtypeStruct((turns, chans, wide), jnp.float32),
            jax.ShapeDtypeStruct((turns, chans, wide), jnp.float32),
            jax.ShapeDtypeStruct((chans, vp + fp), jnp.bfloat16),
            jax.ShapeDtypeStruct((vp, chans), jnp.bfloat16),
            jax.ShapeDtypeStruct((lat, chans, wide), jnp.bfloat16),
            jax.ShapeDtypeStruct((lat * 3 * chans, wide), jnp.bfloat16),
        ),
        in_specs=[smem, smem] + [vmem] * (6 + bands),
        out_specs=(vmem,) * 7,
        scratch_shapes=[
            pltpu.VMEM((vp + fp, chans), jnp.float32),
            pltpu.VMEM((-(-2 * members // 8) * 8, chans), jnp.float32),
        ],
        compiler_params=small,
        cost_estimate=free,
    )(scalars, atmos_owner[0], encode_weight.T, decode_weight, settings.T, scale_weight, shift_weight, *fields, group)

    blocks = [conv_weight[0], point_weight[0], spread]
    for k in range(layers - 1):
        shares = all_along(relayed[k], "groups")
        early = all_along(shares[0], "rows")
        blocks += early
        for shared in shares[1:]:
            blocks += all_along(shared, "rows")
        blocks += all_along(after(direct[k], group, *shares[1:], *early[1:]), "rows")

    scratch = [
        pltpu.VMEM((layers, chans, 10 * chans + LANES), jnp.bfloat16),
        pltpu.VMEM((lat, chans, wide), jnp.float32),
        pltpu.VMEM((lat, chans, wide), jnp.bfloat16),
        pltpu.VMEM((lat, vp + fp, wide), jnp.bfloat16),
        pltpu.VMEM((local, vp, lon), jnp.float32),
        pltpu.SemaphoreType.DMA((layers,)),
    ]
    if turns > 1:
        scratch += [pltpu.VMEM(hidden.shape, jnp.bfloat16), pltpu.VMEM(taps.shape, jnp.bfloat16)]
    final, mean = pl.pallas_call(
        functools.partial(window_kernel, dims + (groups,)),
        out_shape=(
            jax.ShapeDtypeStruct((local, varied, lon), jnp.bfloat16),
            jax.ShapeDtypeStruct((varied, local, lon), jnp.float32),
        ),
        in_specs=[smem] + [vmem] * 7 + [whole] * len(blocks),
        out_specs=(vmem, vmem),
        scratch_shapes=scratch,
        compiler_params=large,
        cost_estimate=free,
    )(scalars, field, scale, shift, enc, dec, hidden, taps, *blocks)
    return final[None, None], jnp.swapaxes(mean, 0, 1)[None]
def solution(mesh):
    in_specs = (
        P(("groups", "segment"), "rows", None, None),
        P("members", ("groups", "segment"), None, "rows", None, None),
        P(("groups", "segment"), None),
        P(("groups", "rows"), None),
        P(("groups", "members")),
        P(),
        P(),
        P(),
        P(),
        P("segment", None, None),
        P("segment", None, None),
        P("segment", None),
        P(),
    )
    out_specs = (
        P("members", ("groups", "segment"), "rows", None, None),
        P(("groups", "segment"), "rows", None, None),
    )
    return jax.shard_map(
        per_device, mesh=mesh, in_specs=in_specs, out_specs=out_specs, check_vma=False
    )
```

```python
import functools

import jax
import jax.numpy as jnp
from jax import lax
from jax.experimental import pallas as pl
from jax.experimental.pallas import tpu as pltpu
from jax.sharding import PartitionSpec as P

BF16_ROWS = 16
LANES = 128
MIB = 1024 * 1024


def padded_rows(count):
    return -(-count // BF16_ROWS) * BF16_ROWS


def passed_along(block, axis, distance):
    size = lax.axis_size(axis)
    return lax.ppermute(block, axis, [(i, (i + distance) % size) for i in range(size)])


def all_along(block, axis):
    return [block] + [passed_along(block, axis, k) for k in range(1, lax.axis_size(axis))]


def by_doubling(block, axis):
    size, reach = lax.axis_size(axis), 1
    while reach < size:
        partner = lax.ppermute(block, axis, [(i, i ^ reach) for i in range(size)])
        block = jnp.concatenate([block, partner], axis=0)
        reach *= 2
    return block


def from_place(parts, here, place):
    chosen = parts[0]
    for k in range(1, len(parts)):
        chosen = jnp.where(lax.rem(here - k + len(parts), len(parts)) == place, parts[k], chosen)
    return chosen


def pack_kernel(dims, slots_ref, state_ref, land_ref, earlier_ref, field_ref):
    steps, local, forced, vp, fp = dims
    field_ref[...] = jnp.zeros(field_ref.shape, field_ref.dtype)
    for i in range(local):
        field_ref[i, 0 : state_ref.shape[1]] = state_ref[i]
        for t in range(steps):
            first = (t * local + i) * forced
            field_ref[i, vp + fp * t : vp + fp * t + forced] = slots_ref[first : first + forced]
        field_ref[i, vp + fp * steps : vp + fp * steps + 1] = land_ref[i : i + 1].astype(jnp.bfloat16)


def group_kernel(dims, place_ref, index_ref, *rest):
    steps, bands, local, forced, vp, fp = dims
    fields, group_ref = rest[:bands], rest[bands]
    for b in range(bands):
        field = from_place([f[...] for f in fields], place_ref[1], b)
        for i in range(local):
            for t in range(steps):
                first = ((b * local + i) * steps + t) * forced
                group_ref[first : first + forced] = field[i, vp + fp * t : vp + fp * t + forced].astype(jnp.float32)
    last = bands * local * steps * forced
    group_ref[last : last + 1] = jnp.full((1, group_ref.shape[1]), index_ref[0], jnp.int32).astype(jnp.float32)


def put_taps(taps, value, row, cols, spacing):
    chans, lon = value.shape
    lane = lax.broadcasted_iota(jnp.int32, (chans, lon), 1)
    zero = jnp.zeros_like(value)
    base = 3 * chans * row
    taps[base : base + chans, cols] = jnp.where(lane >= spacing, pltpu.roll(value, spacing, 1), zero)
    taps[base + chans : base + 2 * chans, cols] = value
    taps[base + 2 * chans : base + 3 * chans, cols] = jnp.where(
        lane < lon - spacing, pltpu.roll(value, lon - spacing, 1), zero
    )


def prepare_kernel(dims, scalar_ref, enc_w_ref, dec_w_ref, *rest):
    steps, bands, local, vp, fp = dims
    fields, (field_ref, enc_ref, dec_ref, lifted_ref, turned) = rest[:bands], rest[bands:]
    for b in range(bands):
        field_ref[b * local : (b + 1) * local] = from_place([f[...] for f in fields], scalar_ref[1], b)
    varied = dec_w_ref.shape[0]
    forced = enc_w_ref.shape[0] - varied
    turned[...] = jnp.zeros(turned.shape, turned.dtype)
    turned[0:varied] = enc_w_ref[0:varied].astype(jnp.float32)
    turned[vp : vp + forced] = enc_w_ref[varied : varied + forced].astype(jnp.float32)
    enc_ref[...] = turned[...].T.astype(jnp.bfloat16)
    dec_ref[...] = jnp.zeros(dec_ref.shape, dec_ref.dtype)
    dec_ref[0:varied, :] = dec_w_ref[...]
    for i in range(bands * local):
        lifted_ref[i] = jnp.dot(enc_ref[:, 0:vp], field_ref[i, 0:vp, :], preferred_element_type=jnp.float32)


def first_kernel(dims, scalar_ref, owner_ref, enc_ref, settings_ref, scale_w_ref, shift_w_ref, *rest):
    steps, layers, bands, local, members, lon, chans, vp, fp, turns, forced = dims
    field_ref, lifted_ref, everyone, force_ref, scale_ref, shift_ref, hidden_ref, taps_ref, lines = rest
    used = bands * local * steps * forced
    group = [everyone.at[k * (used + 8) : (k + 1) * (used + 8)] for k in range(members * turns)]
    force_ref[...] = jnp.zeros(force_ref.shape, force_ref.dtype)
    for i in range(bands * local):
        for t in range(steps):
            rows = slice((i * steps + t) * forced, (i * steps + t + 1) * forced)
            place = scalar_ref[2] ^ owner_ref[t]
            force = group[0][rows, :]
            for k in range(1, members * turns):
                force = jnp.where(place == k, group[k][rows, :], force)
            force_ref[i, fp * t : fp * t + forced, :] = force.astype(jnp.bfloat16)

    settings = settings_ref[...]
    numbers = lax.broadcasted_iota(jnp.int32, settings.shape, 1).astype(jnp.float32)
    for m, entry in enumerate(group):
        chosen = entry[used : used + 1, 0 : settings.shape[1]]
        column = jnp.sum(jnp.where(numbers == chosen, settings, 0.0), axis=1, keepdims=True)
        lines[2 * m : 2 * m + 1] = 1.0 + jnp.sum(scale_w_ref[...] * column, axis=0, keepdims=True)
        lines[2 * m + 1 : 2 * m + 2] = jnp.sum(shift_w_ref[...] * column, axis=0, keepdims=True)
    columns = lines[...].T
    for m in range(len(group)):
        cols = slice((m % members) * lon, (m % members + 1) * lon)
        scale_ref[m // members, :, cols] = jnp.broadcast_to(columns[:, 2 * m : 2 * m + 1], (chans, lon))
        shift_ref[m // members, :, cols] = jnp.broadcast_to(columns[:, 2 * m + 1 : 2 * m + 2], (chans, lon))

    if turns == 1:
        for i in range(bands * local):
            land = field_ref[i, vp + fp * steps : vp + fp * steps + 1, :].astype(jnp.float32)
            lifted = lifted_ref[i] + jnp.dot(
                enc_ref[:, vp : vp + fp], force_ref[i, 0:fp, :], preferred_element_type=jnp.float32
            )
            for m in range(members):
                cols = slice(m * lon, (m + 1) * lon)
                value = land * (lifted * scale_ref[0, :, cols] + shift_ref[0, :, cols])
                value = value.astype(jnp.bfloat16)
                hidden_ref[i, :, cols] = value
                put_taps(taps_ref, value, i, cols, 1)


def after_kernel(*refs):
    pass


def after(section, *earlier):
    whole = pl.BlockSpec(memory_space=pl.ANY)
    return pl.pallas_call(
        after_kernel,
        out_shape=jax.ShapeDtypeStruct(section.shape, section.dtype),
        in_specs=[whole] * (1 + len(earlier)),
        out_specs=whole,
        input_output_aliases={0: 0},
        compiler_params=pltpu.CompilerParams(vmem_limit_bytes=MIB),
        cost_estimate=pl.CostEstimate(flops=0, bytes_accessed=0, transcendentals=0),
    )(section, *earlier)


def window_kernel(dims, scalar_ref, field_ref, force_ref, scale_ref, shift_ref, enc_ref, dec_ref, *rest):
    steps, layers, bands, local, members, lon, chans, vp, fp, turns, groups = dims
    lat = bands * local
    hidden, taps = rest[:2]
    pieces = 3 + (layers - 1) * (groups + 1) * bands
    blocks, rest = rest[2 : 2 + pieces], rest[2 + pieces :]
    final_ref, mean_ref, weights, conv, act, inputs, total, sems = rest[:8]
    here, band = scalar_ref[0], scalar_ref[1]
    taps_wide, wide = 9 * chans, 3 * chans
    part = chans // bands

    pltpu.make_async_copy(blocks[0], weights.at[here, :, pl.ds(0, taps_wide)], sems.at[here]).start()
    pltpu.make_async_copy(blocks[1], weights.at[here, :, pl.ds(taps_wide, chans)], sems.at[here]).start()
    pltpu.make_async_copy(blocks[2], weights.at[here, :, pl.ds(10 * chans, LANES)], sems.at[here]).start()
    share = 5 * chans // groups
    for k in range(1, layers):
        slot = lax.rem(here - k + layers, layers)
        for g in range(groups + 1):
            if g < groups:
                place = lax.rem(scalar_ref[3] - g + groups, groups)
                cols = pl.ds(pl.multiple_of(place * share, LANES), share)
            else:
                cols = pl.ds(groups * share, 10 * chans + LANES - groups * share)
            for j in range(bands):
                rows = pl.ds(pl.multiple_of(lax.rem(band - j + bands, bands) * part, part), part)
                block = blocks[3 + ((k - 1) * (groups + 1) + g) * bands + j]
                pltpu.make_async_copy(block, weights.at[slot, rows, cols], sems.at[slot]).start()

    if turns > 1:
        hidden, taps = rest[8:]

    def columns(m):
        return slice(m * lon, (m + 1) * lon)

    land = [field_ref[i, vp + fp * steps : vp + fp * steps + 1, :].astype(jnp.float32) for i in range(lat)]

    def put_hidden(i, m, value, layer):
        value = value.astype(jnp.bfloat16)
        hidden[i, :, columns(m)] = value
        if layer is not None:
            put_taps(taps, value, i, columns(m), 2 ** (layer % 3))

    def encode(step, turn):
        for i in range(lat):
            force = force_ref[i, fp * step : fp * (step + 1), :]
            for m in range(members):
                inputs[i, vp : vp + fp, columns(m)] = force
                if step == 0:
                    inputs[i, 0:vp, columns(m)] = field_ref[i, 0:vp, :]
            lifted = jnp.dot(enc_ref[...], inputs[i], preferred_element_type=jnp.float32)
            for m in range(members):
                value = lifted[:, columns(m)] * scale_ref[turn, :, columns(m)] + shift_ref[turn, :, columns(m)]
                put_hidden(i, m, land[i] * value, 0)

    def activate(value, layer):
        centred = value - jnp.sum(value, axis=0, keepdims=True) * (1.0 / chans)
        spread = jnp.sum(centred * centred, axis=0, keepdims=True) * (1.0 / chans)
        half = (centred * lax.rsqrt(spread + 1e-05)).astype(jnp.bfloat16) * weights[layer, :, 10 * chans :]
        inner = half * (half * half * 0.2854192648 + 1.5957691216)
        return half + half * jnp.tanh(inner)

    def block(layer, not_yet):
        if not_yet is True:
            pltpu.make_async_copy(weights.at[layer], weights.at[layer], sems.at[layer]).wait()
        elif not_yet is not None:

            @pl.when(not_yet)
            def _():
                pltpu.make_async_copy(weights.at[layer], weights.at[layer], sems.at[layer]).wait()

        for i in range(lat):
            low, high = max(i - 1, 0), min(i + 1, lat - 1)
            conv[i] = jnp.dot(
                weights[layer, :, (low - i + 1) * wide : (high - i + 2) * wide],
                taps[low * wide : (high + 1) * wide, :],
                preferred_element_type=jnp.float32,
            )
        for i in range(lat):
            mix(i, i, land[i], layer)

    def mix(i, row, sea, layer):
        for m in range(members):
            act[i, :, columns(m)] = activate(conv[i, :, columns(m)], layer)
        mixed = jnp.dot(weights[layer, :, taps_wide : 10 * chans], act[i], preferred_element_type=jnp.float32)
        for m in range(members):
            kept = hidden[row, :, columns(m)].astype(jnp.float32)
            later = layer + 1 if layer + 1 < layers else None
            put_hidden(row, m, sea * (kept + mixed[:, columns(m)]), later)

    def decode(row, sea, step):
        change = jnp.dot(dec_ref[...], hidden[row], preferred_element_type=jnp.float32)
        for m in range(members):
            old = field_ref[row, 0:vp, :] if step == 0 else inputs[row, 0:vp, columns(m)]
            new = old.astype(jnp.float32) + sea * change[:, columns(m)]
            inputs[row, 0:vp, columns(m)] = new.astype(jnp.bfloat16)

    def last_block(layer):
        first = pl.multiple_of((1 - band) * wide, wide)
        conv[0] = jnp.dot(weights[layer, :, pl.ds(first, 2 * wide)], taps[...], preferred_element_type=jnp.float32)
        sea = field_ref[band, vp + fp * steps : vp + fp * steps + 1, :].astype(jnp.float32)
        mix(0, band, sea, layer)
        decode(band, sea, steps - 1)

    varied = final_ref.shape[1]

    def window(turn, first):
        for step in range(steps):
            if step > 0 or turns > 1:
                encode(step, turn)
            own_row = step == steps - 1 and step > 0 and lat == 2 and local == 1
            for layer in range(layers):
                if own_row and layer == layers - 1:
                    last_block(layer)
                else:
                    block(layer, first if step == 0 else None)
            if not own_row:
                for i in range(lat):
                    decode(i, land[i], step)
        for i in range(local):
            row = band * local + i
            summed = inputs[row, 0:vp, columns(0)].astype(jnp.float32)
            for m in range(1, members):
                summed = summed + inputs[row, 0:vp, columns(m)].astype(jnp.float32)
            if turns == 1:
                mean_ref[:, i, :] = summed[0:varied] * (1.0 / members)
                final_ref[i] = inputs[row, 0:varied, columns(0)]
            else:
                total[i] = jnp.where(first, summed, total[i] + summed)
                mean_ref[:, i, :] = total[i, 0:varied] * (1.0 / (members * turns))

                @pl.when(first)
                def _():
                    final_ref[i] = inputs[row, 0:varied, columns(0)]

    if turns == 1:
        window(0, True)
    else:
        lax.fori_loop(0, turns, lambda turn, _: window(turn, turn == 0), None)


def per_device(
    init_state,
    forcing_slots,
    atmos_owner,
    land_mask,
    param_index,
    settings,
    scale_weight,
    shift_weight,
    encode_weight,
    conv_weight,
    point_weight,
    norm_gain,
    decode_weight,
):
    members, layers, bands = (lax.axis_size(a) for a in ("members", "segment", "rows"))
    here, band = lax.axis_index("segment"), lax.axis_index("rows")
    _, local, varied, lon = init_state.shape
    steps, forced = forcing_slots.shape[2], forcing_slots.shape[4]
    chans = conv_weight.shape[1]
    lat = local * bands
    vp, fp = padded_rows(varied), padded_rows(forced)
    part = chans // bands
    at_once = next(n for n in (4, 2, 1) if members % n == 0)
    turns, wide = members // at_once, at_once * lon
    smem, vmem, whole = (pl.BlockSpec(memory_space=s) for s in (pltpu.SMEM, pltpu.VMEM, pl.ANY))
    small, large = (pltpu.CompilerParams(vmem_limit_bytes=n * MIB) for n in (8, 16 + 2 * layers))
    free = pl.CostEstimate(flops=0, bytes_accessed=0, transcendentals=0)

    groups = lax.axis_size("groups")
    share = 5 * chans // groups
    places = [here, band, lax.axis_index("members"), lax.axis_index("groups")]
    scalars = jnp.stack(places).astype(jnp.int32)
    slots = forcing_slots[0, 0].reshape(-1, lon)
    conv = conv_weight[0]
    relayed = lax.dynamic_slice(conv, (band * part, places[3] * share), (part, share))
    spread = jnp.broadcast_to((norm_gain[0] * 0.5)[:, None], (chans, LANES))
    direct = jnp.concatenate([conv[:, groups * share :], point_weight[0], spread], axis=1)
    direct = lax.dynamic_slice_in_dim(direct, band * part, part, 0)
    field = pl.pallas_call(
        functools.partial(pack_kernel, (steps, local, forced, vp, fp)),
        out_shape=jax.ShapeDtypeStruct((local, vp + fp * steps + BF16_ROWS, lon), jnp.bfloat16),
        in_specs=[vmem] * 3 + [whole],
        out_specs=vmem,
        compiler_params=small,
        cost_estimate=free,
    )(slots, init_state[0], land_mask, direct)
    relayed, direct = (all_along(piece, "segment")[1:] for piece in (relayed, direct))
    fields = all_along(field, "rows")
    group = pl.pallas_call(
        functools.partial(group_kernel, (steps, bands, local, forced, vp, fp)),
        out_shape=jax.ShapeDtypeStruct((lat * steps * forced + 8, lon), jnp.float32),
        in_specs=[smem, smem] + [vmem] * bands,
        out_specs=vmem,
        compiler_params=small,
        cost_estimate=free,
    )(scalars, param_index, *fields)
    group = by_doubling(group, "members")

    dims = (steps, layers, bands, local, at_once, lon, chans, vp, fp, turns)
    field, enc, dec, lifted = pl.pallas_call(
        functools.partial(prepare_kernel, (steps, bands, local, vp, fp)),
        out_shape=(
            jax.ShapeDtypeStruct((lat, vp + fp * steps + BF16_ROWS, lon), jnp.bfloat16),
            jax.ShapeDtypeStruct((chans, vp + fp), jnp.bfloat16),
            jax.ShapeDtypeStruct((vp, chans), jnp.bfloat16),
            jax.ShapeDtypeStruct((lat, chans, lon), jnp.float32),
        ),
        in_specs=[smem] + [vmem] * (2 + bands),
        out_specs=(vmem,) * 4,
        scratch_shapes=[pltpu.VMEM((vp + fp, chans), jnp.float32)],
        compiler_params=small,
        cost_estimate=free,
    )(scalars, encode_weight.T, decode_weight, *fields)
    force, scale, shift, hidden, taps = pl.pallas_call(
        functools.partial(first_kernel, dims + (forced,)),
        out_shape=(
            jax.ShapeDtypeStruct((lat, fp * steps, lon), jnp.bfloat16),
            jax.ShapeDtypeStruct((turns, chans, wide), jnp.float32),
            jax.ShapeDtypeStruct((turns, chans, wide), jnp.float32),
            jax.ShapeDtypeStruct((lat, chans, wide), jnp.bfloat16),
            jax.ShapeDtypeStruct((lat * 3 * chans, wide), jnp.bfloat16),
        ),
        in_specs=[smem, smem] + [vmem] * 7,
        out_specs=(vmem,) * 5,
        scratch_shapes=[pltpu.VMEM((-(-2 * members // 8) * 8, chans), jnp.float32)],
        compiler_params=small,
        cost_estimate=free,
    )(scalars, atmos_owner[0], enc, settings.T, scale_weight, shift_weight, field, lifted, group)

    blocks = [conv_weight[0], point_weight[0], spread]
    for k in range(layers - 1):
        shares = all_along(relayed[k], "groups")
        early = all_along(shares[0], "rows")
        blocks += early
        for shared in shares[1:]:
            blocks += all_along(shared, "rows")
        blocks += all_along(after(direct[k], group, lifted, *shares[1:], *early[1:]), "rows")

    scratch = [
        pltpu.VMEM((layers, chans, 10 * chans + LANES), jnp.bfloat16),
        pltpu.VMEM((lat, chans, wide), jnp.float32),
        pltpu.VMEM((lat, chans, wide), jnp.bfloat16),
        pltpu.VMEM((lat, vp + fp, wide), jnp.bfloat16),
        pltpu.VMEM((local, vp, lon), jnp.float32),
        pltpu.SemaphoreType.DMA((layers,)),
    ]
    if turns > 1:
        scratch += [pltpu.VMEM(hidden.shape, jnp.bfloat16), pltpu.VMEM(taps.shape, jnp.bfloat16)]
    final, mean = pl.pallas_call(
        functools.partial(window_kernel, dims + (groups,)),
        out_shape=(
            jax.ShapeDtypeStruct((local, varied, lon), jnp.bfloat16),
            jax.ShapeDtypeStruct((varied, local, lon), jnp.float32),
        ),
        in_specs=[smem] + [vmem] * 8 + [whole] * len(blocks),
        out_specs=(vmem, vmem),
        scratch_shapes=scratch,
        compiler_params=large,
        cost_estimate=free,
    )(scalars, field, force, scale, shift, enc, dec, hidden, taps, *blocks)
    return final[None, None], jnp.swapaxes(mean, 0, 1)[None]
def solution(mesh):
    in_specs = (
        P(("groups", "segment"), "rows", None, None),
        P("members", ("groups", "segment"), None, "rows", None, None),
        P(("groups", "segment"), None),
        P(("groups", "rows"), None),
        P(("groups", "members")),
        P(),
        P(),
        P(),
        P(),
        P("segment", None, None),
        P("segment", None, None),
        P("segment", None),
        P(),
    )
    out_specs = (
        P("members", ("groups", "segment"), "rows", None, None),
        P(("groups", "segment"), "rows", None, None),
    )
    return jax.shard_map(
        per_device, mesh=mesh, in_specs=in_specs, out_specs=out_specs, check_vma=False
    )
```

```python
import functools

import jax
import jax.numpy as jnp
from jax import lax
from jax.experimental import pallas as pl
from jax.experimental.pallas import tpu as pltpu
from jax.sharding import PartitionSpec as P

BF16_ROWS = 16
LANES = 128
MIB = 1024 * 1024


def padded_rows(count):
    return -(-count // BF16_ROWS) * BF16_ROWS


def passed_along(block, axis, distance):
    size = lax.axis_size(axis)
    return lax.ppermute(block, axis, [(i, (i + distance) % size) for i in range(size)])


def all_along(block, axis):
    return [block] + [passed_along(block, axis, k) for k in range(1, lax.axis_size(axis))]


def by_doubling(block, axis):
    size, reach = lax.axis_size(axis), 1
    while reach < size:
        partner = lax.ppermute(block, axis, [(i, i ^ reach) for i in range(size)])
        block = jnp.concatenate([block, partner], axis=0)
        reach *= 2
    return block


def from_place(parts, here, place):
    chosen = parts[0]
    for k in range(1, len(parts)):
        chosen = jnp.where(lax.rem(here - k + len(parts), len(parts)) == place, parts[k], chosen)
    return chosen


def pack_kernel(dims, slots_ref, state_ref, land_ref, earlier_ref, field_ref):
    steps, local, forced, vp, fp = dims
    field_ref[...] = jnp.zeros(field_ref.shape, field_ref.dtype)
    for i in range(local):
        field_ref[i, 0 : state_ref.shape[1]] = state_ref[i]
        for t in range(steps):
            first = (t * local + i) * forced
            field_ref[i, vp + fp * t : vp + fp * t + forced] = slots_ref[first : first + forced]
        field_ref[i, vp + fp * steps : vp + fp * steps + 1] = land_ref[i : i + 1].astype(jnp.bfloat16)


def group_kernel(dims, index_ref, *rest):
    steps, bands, local, forced, vp, fp = dims
    fields, group_ref = rest[:bands], rest[bands]
    for b in range(bands):
        field = from_place([f[...] for f in fields], lax.axis_index("rows"), b)
        for i in range(local):
            for t in range(steps):
                first = ((b * local + i) * steps + t) * forced
                group_ref[first : first + forced] = field[i, vp + fp * t : vp + fp * t + forced].astype(jnp.float32)
    last = bands * local * steps * forced
    group_ref[last : last + 1] = jnp.full((1, group_ref.shape[1]), index_ref[0], jnp.int32).astype(jnp.float32)


def put_taps(taps, value, row, cols, spacing):
    chans, lon = value.shape
    lane = lax.broadcasted_iota(jnp.int32, (chans, lon), 1)
    zero = jnp.zeros_like(value)
    base = 3 * chans * row
    taps[base : base + chans, cols] = jnp.where(lane >= spacing, pltpu.roll(value, spacing, 1), zero)
    taps[base + chans : base + 2 * chans, cols] = value
    taps[base + 2 * chans : base + 3 * chans, cols] = jnp.where(
        lane < lon - spacing, pltpu.roll(value, lon - spacing, 1), zero
    )


def first_kernel(dims, owner_ref, enc_w_ref, dec_w_ref, settings_ref, scale_w_ref, shift_w_ref, *rest):
    steps, layers, bands, local, members, lon, chans, vp, fp, turns = dims
    fields, rest = rest[:bands], rest[bands:]
    everyone, rest = rest[0], rest[1:]
    forced = enc_w_ref.shape[0] - dec_w_ref.shape[0]
    used = bands * local * steps * forced
    group = [everyone.at[k * (used + 8) : (k + 1) * (used + 8)] for k in range(members * turns)]
    field_ref, scale_ref, shift_ref, enc_ref, dec_ref, hidden_ref, taps_ref, turned, lines = rest
    varied = dec_w_ref.shape[0]
    turned[...] = jnp.zeros(turned.shape, turned.dtype)
    turned[0:varied] = enc_w_ref[0:varied].astype(jnp.float32)
    turned[vp : vp + forced] = enc_w_ref[varied : varied + forced].astype(jnp.float32)
    enc_ref[...] = turned[...].T.astype(jnp.bfloat16)
    dec_ref[...] = jnp.zeros(dec_ref.shape, dec_ref.dtype)
    dec_ref[0:varied, :] = dec_w_ref[...]
    band = lax.axis_index("rows")
    for b in range(bands):
        field_ref[b * local : (b + 1) * local] = from_place([f[...] for f in fields], band, b)
    for i in range(bands * local):
        for t in range(steps):
            rows = slice((i * steps + t) * forced, (i * steps + t + 1) * forced)
            place = lax.axis_index("members") ^ owner_ref[0:1, t : t + 1]
            force = group[0][rows, :]
            for k in range(1, members * turns):
                force = jnp.where(place == k, group[k][rows, :], force)
            field_ref[i, vp + fp * t : vp + fp * t + forced, :] = force.astype(jnp.bfloat16)

    settings = settings_ref[...]
    numbers = lax.broadcasted_iota(jnp.int32, settings.shape, 1).astype(jnp.float32)
    for m, entry in enumerate(group):
        chosen = entry[used : used + 1, 0 : settings.shape[1]]
        column = jnp.sum(jnp.where(numbers == chosen, settings, 0.0), axis=1, keepdims=True)
        lines[2 * m : 2 * m + 1] = 1.0 + jnp.sum(scale_w_ref[...] * column, axis=0, keepdims=True)
        lines[2 * m + 1 : 2 * m + 2] = jnp.sum(shift_w_ref[...] * column, axis=0, keepdims=True)
    columns = lines[...].T
    for m in range(len(group)):
        cols = slice((m % members) * lon, (m % members + 1) * lon)
        scale_ref[m // members, :, cols] = jnp.broadcast_to(columns[:, 2 * m : 2 * m + 1], (chans, lon))
        shift_ref[m // members, :, cols] = jnp.broadcast_to(columns[:, 2 * m + 1 : 2 * m + 2], (chans, lon))

    if turns == 1:
        for i in range(bands * local):
            land = field_ref[i, vp + fp * steps : vp + fp * steps + 1, :].astype(jnp.float32)
            lifted = jnp.dot(enc_ref[...], field_ref[i, 0 : vp + fp, :], preferred_element_type=jnp.float32)
            for m in range(members):
                cols = slice(m * lon, (m + 1) * lon)
                value = land * (lifted * scale_ref[0, :, cols] + shift_ref[0, :, cols])
                value = value.astype(jnp.bfloat16)
                hidden_ref[i, :, cols] = value
                put_taps(taps_ref, value, i, cols, 1)


def after_kernel(*refs):
    pass


def after(section, *earlier):
    whole = pl.BlockSpec(memory_space=pl.ANY)
    return pl.pallas_call(
        after_kernel,
        out_shape=jax.ShapeDtypeStruct(section.shape, section.dtype),
        in_specs=[whole] * (1 + len(earlier)),
        out_specs=whole,
        input_output_aliases={0: 0},
        compiler_params=pltpu.CompilerParams(vmem_limit_bytes=MIB),
        cost_estimate=pl.CostEstimate(flops=0, bytes_accessed=0, transcendentals=0),
    )(section, *earlier)


def window_kernel(dims, field_ref, scale_ref, shift_ref, enc_ref, dec_ref, *rest):
    steps, layers, bands, local, members, lon, chans, vp, fp, turns, groups = dims
    lat = bands * local
    hidden, taps = rest[:2]
    pieces = 3 + (layers - 1) * (groups + 1) * bands
    blocks, rest = rest[2 : 2 + pieces], rest[2 + pieces :]
    final_ref, mean_ref, weights, conv, act, inputs, total, sems = rest[:8]
    here, band = lax.axis_index("segment"), lax.axis_index("rows")
    taps_wide, wide = 9 * chans, 3 * chans
    part = chans // bands

    pltpu.make_async_copy(blocks[0], weights.at[here, :, pl.ds(0, taps_wide)], sems.at[here]).start()
    pltpu.make_async_copy(blocks[1], weights.at[here, :, pl.ds(taps_wide, chans)], sems.at[here]).start()
    pltpu.make_async_copy(blocks[2], weights.at[here, :, pl.ds(10 * chans, LANES)], sems.at[here]).start()
    share = 5 * chans // groups
    for k in range(1, layers):
        slot = lax.rem(here - k + layers, layers)
        for g in range(groups + 1):
            if g < groups:
                place = lax.rem(lax.axis_index("groups") - g + groups, groups)
                cols = pl.ds(pl.multiple_of(place * share, LANES), share)
            else:
                cols = pl.ds(groups * share, 10 * chans + LANES - groups * share)
            for j in range(bands):
                rows = pl.ds(pl.multiple_of(lax.rem(band - j + bands, bands) * part, part), part)
                block = blocks[3 + ((k - 1) * (groups + 1) + g) * bands + j]
                pltpu.make_async_copy(block, weights.at[slot, rows, cols], sems.at[slot]).start()

    if turns > 1:
        hidden, taps = rest[8:]

    def columns(m):
        return slice(m * lon, (m + 1) * lon)

    land = [field_ref[i, vp + fp * steps : vp + fp * steps + 1, :].astype(jnp.float32) for i in range(lat)]

    def put_hidden(i, m, value, layer):
        value = value.astype(jnp.bfloat16)
        hidden[i, :, columns(m)] = value
        if layer is not None:
            put_taps(taps, value, i, columns(m), 2 ** (layer % 3))

    def encode(step, turn):
        for i in range(lat):
            force = field_ref[i, vp + fp * step : vp + fp * (step + 1), :]
            for m in range(members):
                inputs[i, vp : vp + fp, columns(m)] = force
                if step == 0:
                    inputs[i, 0:vp, columns(m)] = field_ref[i, 0:vp, :]
            lifted = jnp.dot(enc_ref[...], inputs[i], preferred_element_type=jnp.float32)
            for m in range(members):
                value = lifted[:, columns(m)] * scale_ref[turn, :, columns(m)] + shift_ref[turn, :, columns(m)]
                put_hidden(i, m, land[i] * value, 0)

    def activate(value, layer):
        centred = value - jnp.sum(value, axis=0, keepdims=True) * (1.0 / chans)
        spread = jnp.sum(centred * centred, axis=0, keepdims=True) * (1.0 / chans)
        half = (centred * lax.rsqrt(spread + 1e-05)).astype(jnp.bfloat16) * weights[layer, :, 10 * chans :]
        inner = half * (half * half * 0.2854192648 + 1.5957691216)
        return half + half * jnp.tanh(inner)

    def block(layer, not_yet):
        if not_yet is True:
            pltpu.make_async_copy(weights.at[layer], weights.at[layer], sems.at[layer]).wait()
        elif not_yet is not None:

            @pl.when(not_yet)
            def _():
                pltpu.make_async_copy(weights.at[layer], weights.at[layer], sems.at[layer]).wait()

        for i in range(lat):
            low, high = max(i - 1, 0), min(i + 1, lat - 1)
            conv[i] = jnp.dot(
                weights[layer, :, (low - i + 1) * wide : (high - i + 2) * wide],
                taps[low * wide : (high + 1) * wide, :],
                preferred_element_type=jnp.float32,
            )
        for i in range(lat):
            mix(i, i, land[i], layer)

    def mix(i, row, sea, layer):
        for m in range(members):
            act[i, :, columns(m)] = activate(conv[i, :, columns(m)], layer)
        mixed = jnp.dot(weights[layer, :, taps_wide : 10 * chans], act[i], preferred_element_type=jnp.float32)
        for m in range(members):
            kept = hidden[row, :, columns(m)].astype(jnp.float32)
            later = layer + 1 if layer + 1 < layers else None
            put_hidden(row, m, sea * (kept + mixed[:, columns(m)]), later)

    def decode(row, sea, step):
        change = jnp.dot(dec_ref[...], hidden[row], preferred_element_type=jnp.float32)
        for m in range(members):
            old = field_ref[row, 0:vp, :] if step == 0 else inputs[row, 0:vp, columns(m)]
            new = old.astype(jnp.float32) + sea * change[:, columns(m)]
            inputs[row, 0:vp, columns(m)] = new.astype(jnp.bfloat16)

    def last_block(layer):
        first = pl.multiple_of((1 - band) * wide, wide)
        conv[0] = jnp.dot(weights[layer, :, pl.ds(first, 2 * wide)], taps[...], preferred_element_type=jnp.float32)
        sea = field_ref[band, vp + fp * steps : vp + fp * steps + 1, :].astype(jnp.float32)
        mix(0, band, sea, layer)
        decode(band, sea, steps - 1)

    varied = final_ref.shape[1]

    def window(turn, first):
        for step in range(steps):
            if step > 0 or turns > 1:
                encode(step, turn)
            own_row = step == steps - 1 and step > 0 and lat == 2 and local == 1
            for layer in range(layers):
                if own_row and layer == layers - 1:
                    last_block(layer)
                else:
                    block(layer, first if step == 0 else None)
            if not own_row:
                for i in range(lat):
                    decode(i, land[i], step)
        for i in range(local):
            row = band * local + i
            summed = inputs[row, 0:vp, columns(0)].astype(jnp.float32)
            for m in range(1, members):
                summed = summed + inputs[row, 0:vp, columns(m)].astype(jnp.float32)
            if turns == 1:
                mean_ref[:, i, :] = summed[0:varied] * (1.0 / members)
                final_ref[i] = inputs[row, 0:varied, columns(0)]
            else:
                total[i] = jnp.where(first, summed, total[i] + summed)
                mean_ref[:, i, :] = total[i, 0:varied] * (1.0 / (members * turns))

                @pl.when(first)
                def _():
                    final_ref[i] = inputs[row, 0:varied, columns(0)]

    if turns == 1:
        window(0, True)
    else:
        lax.fori_loop(0, turns, lambda turn, _: window(turn, turn == 0), None)


def per_device(
    init_state,
    forcing_slots,
    atmos_owner,
    land_mask,
    param_index,
    settings,
    scale_weight,
    shift_weight,
    encode_weight,
    conv_weight,
    point_weight,
    norm_gain,
    decode_weight,
):
    members, layers, bands = (lax.axis_size(a) for a in ("members", "segment", "rows"))
    band = lax.axis_index("rows")
    _, local, varied, lon = init_state.shape
    steps, forced = forcing_slots.shape[2], forcing_slots.shape[4]
    chans = conv_weight.shape[1]
    lat = local * bands
    vp, fp = padded_rows(varied), padded_rows(forced)
    part = chans // bands
    at_once = next(n for n in (4, 2, 1) if members % n == 0)
    turns, wide = members // at_once, at_once * lon
    smem, vmem, whole = (pl.BlockSpec(memory_space=s) for s in (pltpu.SMEM, pltpu.VMEM, pl.ANY))
    small, large = (pltpu.CompilerParams(vmem_limit_bytes=n * MIB) for n in (8, 16 + 2 * layers))
    free = pl.CostEstimate(flops=0, bytes_accessed=0, transcendentals=0)

    groups = lax.axis_size("groups")
    share = 5 * chans // groups
    slots = forcing_slots[0, 0].reshape(-1, lon)
    conv = conv_weight[0]
    relayed = lax.dynamic_slice(conv, (band * part, lax.axis_index("groups") * share), (part, share))
    spread = jnp.broadcast_to((norm_gain[0] * 0.5)[:, None], (chans, LANES))
    direct = jnp.concatenate([conv[:, groups * share :], point_weight[0], spread], axis=1)
    direct = lax.dynamic_slice_in_dim(direct, band * part, part, 0)
    field = pl.pallas_call(
        functools.partial(pack_kernel, (steps, local, forced, vp, fp)),
        out_shape=jax.ShapeDtypeStruct((local, vp + fp * steps + BF16_ROWS, lon), jnp.bfloat16),
        in_specs=[vmem] * 3 + [whole],
        out_specs=vmem,
        compiler_params=small,
        cost_estimate=free,
    )(slots, init_state[0], land_mask, direct)
    relayed, direct = (all_along(piece, "segment")[1:] for piece in (relayed, direct))
    fields = all_along(field, "rows")
    group = pl.pallas_call(
        functools.partial(group_kernel, (steps, bands, local, forced, vp, fp)),
        out_shape=jax.ShapeDtypeStruct((lat * steps * forced + 8, lon), jnp.float32),
        in_specs=[smem] + [vmem] * bands,
        out_specs=vmem,
        compiler_params=small,
        cost_estimate=free,
    )(param_index, *fields)
    group = by_doubling(group, "members")

    dims = (steps, layers, bands, local, at_once, lon, chans, vp, fp, turns)
    field, scale, shift, enc, dec, hidden, taps = pl.pallas_call(
        functools.partial(first_kernel, dims),
        out_shape=(
            jax.ShapeDtypeStruct((lat, vp + fp * steps + BF16_ROWS, lon), jnp.bfloat16),
            jax.ShapeDtypeStruct((turns, chans, wide), jnp.float32),
            jax.ShapeDtypeStruct((turns, chans, wide), jnp.float32),
            jax.ShapeDtypeStruct((chans, vp + fp), jnp.bfloat16),
            jax.ShapeDtypeStruct((vp, chans), jnp.bfloat16),
            jax.ShapeDtypeStruct((lat, chans, wide), jnp.bfloat16),
            jax.ShapeDtypeStruct((lat * 3 * chans, wide), jnp.bfloat16),
        ),
        in_specs=[vmem] * (7 + bands),
        out_specs=(vmem,) * 7,
        scratch_shapes=[
            pltpu.VMEM((vp + fp, chans), jnp.float32),
            pltpu.VMEM((-(-2 * members // 8) * 8, chans), jnp.float32),
        ],
        compiler_params=small,
        cost_estimate=free,
    )(atmos_owner, encode_weight.T, decode_weight, settings.T, scale_weight, shift_weight, *fields, group)

    blocks = [conv_weight[0], point_weight[0], spread]
    for k in range(layers - 1):
        shares = all_along(relayed[k], "groups")
        early = all_along(shares[0], "rows")
        blocks += early
        for shared in shares[1:]:
            blocks += all_along(shared, "rows")
        blocks += all_along(after(direct[k], group, *shares[1:], *early[1:]), "rows")

    scratch = [
        pltpu.VMEM((layers, chans, 10 * chans + LANES), jnp.bfloat16),
        pltpu.VMEM((lat, chans, wide), jnp.float32),
        pltpu.VMEM((lat, chans, wide), jnp.bfloat16),
        pltpu.VMEM((lat, vp + fp, wide), jnp.bfloat16),
        pltpu.VMEM((local, vp, lon), jnp.float32),
        pltpu.SemaphoreType.DMA((layers,)),
    ]
    if turns > 1:
        scratch += [pltpu.VMEM(hidden.shape, jnp.bfloat16), pltpu.VMEM(taps.shape, jnp.bfloat16)]
    final, mean = pl.pallas_call(
        functools.partial(window_kernel, dims + (groups,)),
        out_shape=(
            jax.ShapeDtypeStruct((local, varied, lon), jnp.bfloat16),
            jax.ShapeDtypeStruct((varied, local, lon), jnp.float32),
        ),
        in_specs=[vmem] * 7 + [whole] * len(blocks),
        out_specs=(vmem, vmem),
        scratch_shapes=scratch,
        compiler_params=large,
        cost_estimate=free,
    )(field, scale, shift, enc, dec, hidden, taps, *blocks)
    return final[None, None], jnp.swapaxes(mean, 0, 1)[None]
def solution(mesh):
    in_specs = (
        P(("groups", "segment"), "rows", None, None),
        P("members", ("groups", "segment"), None, "rows", None, None),
        P(("groups", "segment"), None),
        P(("groups", "rows"), None),
        P(("groups", "members")),
        P(),
        P(),
        P(),
        P(),
        P("segment", None, None),
        P("segment", None, None),
        P("segment", None),
        P(),
    )
    out_specs = (
        P("members", ("groups", "segment"), "rows", None, None),
        P(("groups", "segment"), "rows", None, None),
    )
    return jax.shard_map(
        per_device, mesh=mesh, in_specs=in_specs, out_specs=out_specs, check_vma=False
    )
```

```python
import functools

import jax
import jax.numpy as jnp
from jax import lax
from jax.experimental import pallas as pl
from jax.experimental.pallas import tpu as pltpu
from jax.sharding import PartitionSpec as P

BF16_ROWS = 16
LANES = 128
MIB = 1024 * 1024


def padded_rows(count):
    return -(-count // BF16_ROWS) * BF16_ROWS


def passed_along(block, axis, distance):
    size = lax.axis_size(axis)
    return lax.ppermute(block, axis, [(i, (i + distance) % size) for i in range(size)])


def all_along(block, axis):
    return [block] + [passed_along(block, axis, k) for k in range(1, lax.axis_size(axis))]


def by_doubling(block, axis):
    size, reach = lax.axis_size(axis), 1
    while reach < size:
        partner = lax.ppermute(block, axis, [(i, i ^ reach) for i in range(size)])
        block = jnp.concatenate([block, partner], axis=0)
        reach *= 2
    return block


def from_place(parts, here, place):
    chosen = parts[0]
    for k in range(1, len(parts)):
        chosen = jnp.where(lax.rem(here - k + len(parts), len(parts)) == place, parts[k], chosen)
    return chosen


def pack_kernel(dims, slots_ref, state_ref, land_ref, earlier_ref, field_ref):
    steps, local, forced, vp, fp = dims
    field_ref[...] = jnp.zeros(field_ref.shape, field_ref.dtype)
    for i in range(local):
        field_ref[i, 0 : state_ref.shape[1]] = state_ref[i]
        for t in range(steps):
            first = (t * local + i) * forced
            field_ref[i, vp + fp * t : vp + fp * t + forced] = slots_ref[first : first + forced]
        field_ref[i, vp + fp * steps : vp + fp * steps + 1] = land_ref[i : i + 1].astype(jnp.bfloat16)


def group_kernel(dims, index_ref, *rest):
    steps, bands, local, forced, vp, fp = dims
    fields, group_ref = rest[:bands], rest[bands]
    for b in range(bands):
        field = from_place([f[...] for f in fields], lax.axis_index("rows"), b)
        for i in range(local):
            for t in range(steps):
                first = ((b * local + i) * steps + t) * forced
                group_ref[first : first + forced] = field[i, vp + fp * t : vp + fp * t + forced].astype(jnp.float32)
    last = bands * local * steps * forced
    group_ref[last : last + 1] = jnp.full((1, group_ref.shape[1]), index_ref[0], jnp.int32).astype(jnp.float32)


def put_taps(taps, value, row, cols, spacing):
    chans, lon = value.shape
    lane = lax.broadcasted_iota(jnp.int32, (chans, lon), 1)
    zero = jnp.zeros_like(value)
    base = 3 * chans * row
    taps[base : base + chans, cols] = jnp.where(lane >= spacing, pltpu.roll(value, spacing, 1), zero)
    taps[base + chans : base + 2 * chans, cols] = value
    taps[base + 2 * chans : base + 3 * chans, cols] = jnp.where(
        lane < lon - spacing, pltpu.roll(value, lon - spacing, 1), zero
    )


def first_kernel(dims, owner_ref, enc_w_ref, dec_w_ref, settings_ref, scale_w_ref, shift_w_ref, *rest):
    steps, layers, bands, local, members, lon, chans, vp, fp, turns = dims
    fields, rest = rest[:bands], rest[bands:]
    everyone, rest = rest[0], rest[1:]
    forced = enc_w_ref.shape[0] - dec_w_ref.shape[0]
    used = bands * local * steps * forced
    group = [everyone.at[k * (used + 8) : (k + 1) * (used + 8)] for k in range(members * turns)]
    field_ref, scale_ref, shift_ref, enc_ref, dec_ref, hidden_ref, taps_ref, turned, lines = rest
    varied = dec_w_ref.shape[0]
    turned[...] = jnp.zeros(turned.shape, turned.dtype)
    turned[0:varied] = enc_w_ref[0:varied].astype(jnp.float32)
    turned[vp : vp + forced] = enc_w_ref[varied : varied + forced].astype(jnp.float32)
    enc_ref[...] = turned[...].T.astype(jnp.bfloat16)
    dec_ref[...] = jnp.zeros(dec_ref.shape, dec_ref.dtype)
    dec_ref[0:varied, :] = dec_w_ref[...]
    band = lax.axis_index("rows")
    for b in range(bands):
        field_ref[b * local : (b + 1) * local] = from_place([f[...] for f in fields], band, b)
    for i in range(bands * local):
        for t in range(steps):
            rows = slice((i * steps + t) * forced, (i * steps + t + 1) * forced)
            place = lax.axis_index("members") ^ owner_ref[0:1, t : t + 1]
            force = group[0][rows, :]
            for k in range(1, members * turns):
                force = jnp.where(place == k, group[k][rows, :], force)
            field_ref[i, vp + fp * t : vp + fp * t + forced, :] = force.astype(jnp.bfloat16)

    settings = settings_ref[...]
    numbers = lax.broadcasted_iota(jnp.int32, settings.shape, 1).astype(jnp.float32)
    for m, entry in enumerate(group):
        chosen = entry[used : used + 1, 0 : settings.shape[1]]
        column = jnp.sum(jnp.where(numbers == chosen, settings, 0.0), axis=1, keepdims=True)
        lines[2 * m : 2 * m + 1] = 1.0 + jnp.sum(scale_w_ref[...] * column, axis=0, keepdims=True)
        lines[2 * m + 1 : 2 * m + 2] = jnp.sum(shift_w_ref[...] * column, axis=0, keepdims=True)
    columns = lines[...].T
    for m in range(len(group)):
        cols = slice((m % members) * lon, (m % members + 1) * lon)
        scale_ref[m // members, :, cols] = jnp.broadcast_to(columns[:, 2 * m : 2 * m + 1], (chans, lon))
        shift_ref[m // members, :, cols] = jnp.broadcast_to(columns[:, 2 * m + 1 : 2 * m + 2], (chans, lon))

    if turns == 1:
        for i in range(bands * local):
            land = field_ref[i, vp + fp * steps : vp + fp * steps + 1, :].astype(jnp.float32)
            lifted = jnp.dot(enc_ref[...], field_ref[i, 0 : vp + fp, :], preferred_element_type=jnp.float32)
            for m in range(members):
                cols = slice(m * lon, (m + 1) * lon)
                value = land * (lifted * scale_ref[0, :, cols] + shift_ref[0, :, cols])
                value = value.astype(jnp.bfloat16)
                hidden_ref[i, :, cols] = value
                put_taps(taps_ref, value, i, cols, 1)


def after_kernel(*refs):
    pass


def after(section, *earlier):
    whole = pl.BlockSpec(memory_space=pl.ANY)
    return pl.pallas_call(
        after_kernel,
        out_shape=jax.ShapeDtypeStruct(section.shape, section.dtype),
        in_specs=[whole] * (1 + len(earlier)),
        out_specs=whole,
        input_output_aliases={0: 0},
        compiler_params=pltpu.CompilerParams(vmem_limit_bytes=MIB),
        cost_estimate=pl.CostEstimate(flops=0, bytes_accessed=0, transcendentals=0),
    )(section, *earlier)


def window_kernel(dims, field_ref, scale_ref, shift_ref, enc_ref, dec_ref, *rest):
    steps, layers, bands, local, members, lon, chans, vp, fp, turns, groups = dims
    lat = bands * local
    hidden, taps = rest[:2]
    pieces = 3 + (layers - 1) * (groups + 2) * bands
    blocks, rest = rest[2 : 2 + pieces], rest[2 + pieces :]
    final_ref, mean_ref, weights, conv, act, inputs, total, sems = rest[:8]
    here, band = lax.axis_index("segment"), lax.axis_index("rows")
    taps_wide, wide = 9 * chans, 3 * chans
    part = chans // bands

    pltpu.make_async_copy(blocks[0], weights.at[here, :, pl.ds(0, taps_wide)], sems.at[here]).start()
    pltpu.make_async_copy(blocks[1], weights.at[here, :, pl.ds(taps_wide, chans)], sems.at[here]).start()
    pltpu.make_async_copy(blocks[2], weights.at[here, :, pl.ds(10 * chans, LANES)], sems.at[here]).start()
    share = 5 * chans // groups
    for k in range(1, layers):
        slot = lax.rem(here - k + layers, layers)
        for g in range(groups + 2):
            if g < groups:
                place = lax.rem(lax.axis_index("groups") - g + groups, groups)
                cols = pl.ds(pl.multiple_of(place * share, LANES), share)
            elif g == groups:
                cols = pl.ds(groups * share, 6 * LANES)
            else:
                cols = pl.ds(groups * share + 6 * LANES, 10 * chans - groups * share - 5 * LANES)
            for j in range(bands):
                rows = pl.ds(pl.multiple_of(lax.rem(band - j + bands, bands) * part, part), part)
                block = blocks[3 + ((k - 1) * (groups + 2) + g) * bands + j]
                pltpu.make_async_copy(block, weights.at[slot, rows, cols], sems.at[slot]).start()

    if turns > 1:
        hidden, taps = rest[8:]

    def columns(m):
        return slice(m * lon, (m + 1) * lon)

    land = [field_ref[i, vp + fp * steps : vp + fp * steps + 1, :].astype(jnp.float32) for i in range(lat)]

    def put_hidden(i, m, value, layer):
        value = value.astype(jnp.bfloat16)
        hidden[i, :, columns(m)] = value
        if layer is not None:
            put_taps(taps, value, i, columns(m), 2 ** (layer % 3))

    def encode(step, turn):
        for i in range(lat):
            force = field_ref[i, vp + fp * step : vp + fp * (step + 1), :]
            for m in range(members):
                inputs[i, vp : vp + fp, columns(m)] = force
                if step == 0:
                    inputs[i, 0:vp, columns(m)] = field_ref[i, 0:vp, :]
            lifted = jnp.dot(enc_ref[...], inputs[i], preferred_element_type=jnp.float32)
            for m in range(members):
                value = lifted[:, columns(m)] * scale_ref[turn, :, columns(m)] + shift_ref[turn, :, columns(m)]
                put_hidden(i, m, land[i] * value, 0)

    def activate(value, layer):
        centred = value - jnp.sum(value, axis=0, keepdims=True) * (1.0 / chans)
        spread = jnp.sum(centred * centred, axis=0, keepdims=True) * (1.0 / chans)
        half = (centred * lax.rsqrt(spread + 1e-05)).astype(jnp.bfloat16) * weights[layer, :, 10 * chans :]
        inner = half * (half * half * 0.2854192648 + 1.5957691216)
        return half + half * jnp.tanh(inner)

    def block(layer, not_yet):
        if not_yet is True:
            pltpu.make_async_copy(weights.at[layer], weights.at[layer], sems.at[layer]).wait()
        elif not_yet is not None:

            @pl.when(not_yet)
            def _():
                pltpu.make_async_copy(weights.at[layer], weights.at[layer], sems.at[layer]).wait()

        for i in range(lat):
            low, high = max(i - 1, 0), min(i + 1, lat - 1)
            conv[i] = jnp.dot(
                weights[layer, :, (low - i + 1) * wide : (high - i + 2) * wide],
                taps[low * wide : (high + 1) * wide, :],
                preferred_element_type=jnp.float32,
            )
        for i in range(lat):
            mix(i, i, land[i], layer)

    def mix(i, row, sea, layer):
        for m in range(members):
            act[i, :, columns(m)] = activate(conv[i, :, columns(m)], layer)
        mixed = jnp.dot(weights[layer, :, taps_wide : 10 * chans], act[i], preferred_element_type=jnp.float32)
        for m in range(members):
            kept = hidden[row, :, columns(m)].astype(jnp.float32)
            later = layer + 1 if layer + 1 < layers else None
            put_hidden(row, m, sea * (kept + mixed[:, columns(m)]), later)

    def decode(row, sea, step):
        change = jnp.dot(dec_ref[...], hidden[row], preferred_element_type=jnp.float32)
        for m in range(members):
            old = field_ref[row, 0:vp, :] if step == 0 else inputs[row, 0:vp, columns(m)]
            new = old.astype(jnp.float32) + sea * change[:, columns(m)]
            inputs[row, 0:vp, columns(m)] = new.astype(jnp.bfloat16)

    def last_block(layer):
        first = pl.multiple_of((1 - band) * wide, wide)
        conv[0] = jnp.dot(weights[layer, :, pl.ds(first, 2 * wide)], taps[...], preferred_element_type=jnp.float32)
        sea = field_ref[band, vp + fp * steps : vp + fp * steps + 1, :].astype(jnp.float32)
        mix(0, band, sea, layer)
        decode(band, sea, steps - 1)

    varied = final_ref.shape[1]

    def window(turn, first):
        for step in range(steps):
            if step > 0 or turns > 1:
                encode(step, turn)
            own_row = step == steps - 1 and step > 0 and lat == 2 and local == 1
            for layer in range(layers):
                if own_row and layer == layers - 1:
                    last_block(layer)
                else:
                    block(layer, first if step == 0 else None)
            if not own_row:
                for i in range(lat):
                    decode(i, land[i], step)
        for i in range(local):
            row = band * local + i
            summed = inputs[row, 0:vp, columns(0)].astype(jnp.float32)
            for m in range(1, members):
                summed = summed + inputs[row, 0:vp, columns(m)].astype(jnp.float32)
            if turns == 1:
                mean_ref[:, i, :] = summed[0:varied] * (1.0 / members)
                final_ref[i] = inputs[row, 0:varied, columns(0)]
            else:
                total[i] = jnp.where(first, summed, total[i] + summed)
                mean_ref[:, i, :] = total[i, 0:varied] * (1.0 / (members * turns))

                @pl.when(first)
                def _():
                    final_ref[i] = inputs[row, 0:varied, columns(0)]

    if turns == 1:
        window(0, True)
    else:
        lax.fori_loop(0, turns, lambda turn, _: window(turn, turn == 0), None)


def per_device(
    init_state,
    forcing_slots,
    atmos_owner,
    land_mask,
    param_index,
    settings,
    scale_weight,
    shift_weight,
    encode_weight,
    conv_weight,
    point_weight,
    norm_gain,
    decode_weight,
):
    members, layers, bands = (lax.axis_size(a) for a in ("members", "segment", "rows"))
    band = lax.axis_index("rows")
    _, local, varied, lon = init_state.shape
    steps, forced = forcing_slots.shape[2], forcing_slots.shape[4]
    chans = conv_weight.shape[1]
    lat = local * bands
    vp, fp = padded_rows(varied), padded_rows(forced)
    part = chans // bands
    at_once = next(n for n in (4, 2, 1) if members % n == 0)
    turns, wide = members // at_once, at_once * lon
    smem, vmem, whole = (pl.BlockSpec(memory_space=s) for s in (pltpu.SMEM, pltpu.VMEM, pl.ANY))
    small, large = (pltpu.CompilerParams(vmem_limit_bytes=n * MIB) for n in (8, 16 + 2 * layers))
    free = pl.CostEstimate(flops=0, bytes_accessed=0, transcendentals=0)

    groups = lax.axis_size("groups")
    share = 5 * chans // groups
    slots = forcing_slots[0, 0].reshape(-1, lon)
    conv = conv_weight[0]
    relayed = lax.dynamic_slice(conv, (band * part, lax.axis_index("groups") * share), (part, share))
    spread = jnp.broadcast_to((norm_gain[0] * 0.5)[:, None], (chans, LANES))
    middle = groups * share + 6 * LANES
    between = lax.dynamic_slice(conv, (band * part, groups * share), (part, middle - groups * share))
    direct = jnp.concatenate([conv[:, middle:], point_weight[0], spread], axis=1)
    direct = lax.dynamic_slice_in_dim(direct, band * part, part, 0)
    field = pl.pallas_call(
        functools.partial(pack_kernel, (steps, local, forced, vp, fp)),
        out_shape=jax.ShapeDtypeStruct((local, vp + fp * steps + BF16_ROWS, lon), jnp.bfloat16),
        in_specs=[vmem] * 3 + [whole],
        out_specs=vmem,
        compiler_params=small,
        cost_estimate=free,
    )(slots, init_state[0], land_mask, direct)
    relayed, between, direct = (all_along(piece, "segment")[1:] for piece in (relayed, between, direct))
    fields = all_along(field, "rows")
    group = pl.pallas_call(
        functools.partial(group_kernel, (steps, bands, local, forced, vp, fp)),
        out_shape=jax.ShapeDtypeStruct((lat * steps * forced + 8, lon), jnp.float32),
        in_specs=[smem] + [vmem] * bands,
        out_specs=vmem,
        compiler_params=small,
        cost_estimate=free,
    )(param_index, *fields)
    group = by_doubling(group, "members")

    dims = (steps, layers, bands, local, at_once, lon, chans, vp, fp, turns)
    field, scale, shift, enc, dec, hidden, taps = pl.pallas_call(
        functools.partial(first_kernel, dims),
        out_shape=(
            jax.ShapeDtypeStruct((lat, vp + fp * steps + BF16_ROWS, lon), jnp.bfloat16),
            jax.ShapeDtypeStruct((turns, chans, wide), jnp.float32),
            jax.ShapeDtypeStruct((turns, chans, wide), jnp.float32),
            jax.ShapeDtypeStruct((chans, vp + fp), jnp.bfloat16),
            jax.ShapeDtypeStruct((vp, chans), jnp.bfloat16),
            jax.ShapeDtypeStruct((lat, chans, wide), jnp.bfloat16),
            jax.ShapeDtypeStruct((lat * 3 * chans, wide), jnp.bfloat16),
        ),
        in_specs=[vmem] * (7 + bands),
        out_specs=(vmem,) * 7,
        scratch_shapes=[
            pltpu.VMEM((vp + fp, chans), jnp.float32),
            pltpu.VMEM((-(-2 * members // 8) * 8, chans), jnp.float32),
        ],
        compiler_params=small,
        cost_estimate=free,
    )(atmos_owner, encode_weight.T, decode_weight, settings.T, scale_weight, shift_weight, *fields, group)

    blocks = [conv_weight[0], point_weight[0], spread]
    for k in range(layers - 1):
        shares = all_along(relayed[k], "groups")
        early = all_along(shares[0], "rows")
        blocks += early
        for shared in shares[1:]:
            blocks += all_along(shared, "rows")
        blocks += all_along(after(between[k], *fields[1:]), "rows")
        blocks += all_along(after(direct[k], group, *shares[1:], *early[1:]), "rows")

    scratch = [
        pltpu.VMEM((layers, chans, 10 * chans + LANES), jnp.bfloat16),
        pltpu.VMEM((lat, chans, wide), jnp.float32),
        pltpu.VMEM((lat, chans, wide), jnp.bfloat16),
        pltpu.VMEM((lat, vp + fp, wide), jnp.bfloat16),
        pltpu.VMEM((local, vp, lon), jnp.float32),
        pltpu.SemaphoreType.DMA((layers,)),
    ]
    if turns > 1:
        scratch += [pltpu.VMEM(hidden.shape, jnp.bfloat16), pltpu.VMEM(taps.shape, jnp.bfloat16)]
    final, mean = pl.pallas_call(
        functools.partial(window_kernel, dims + (groups,)),
        out_shape=(
            jax.ShapeDtypeStruct((local, varied, lon), jnp.bfloat16),
            jax.ShapeDtypeStruct((varied, local, lon), jnp.float32),
        ),
        in_specs=[vmem] * 7 + [whole] * len(blocks),
        out_specs=(vmem, vmem),
        scratch_shapes=scratch,
        compiler_params=large,
        cost_estimate=free,
    )(field, scale, shift, enc, dec, hidden, taps, *blocks)
    return final[None, None], jnp.swapaxes(mean, 0, 1)[None]
def solution(mesh):
    in_specs = (
        P(("groups", "segment"), "rows", None, None),
        P("members", ("groups", "segment"), None, "rows", None, None),
        P(("groups", "segment"), None),
        P(("groups", "rows"), None),
        P(("groups", "members")),
        P(),
        P(),
        P(),
        P(),
        P("segment", None, None),
        P("segment", None, None),
        P("segment", None),
        P(),
    )
    out_specs = (
        P("members", ("groups", "segment"), "rows", None, None),
        P(("groups", "segment"), "rows", None, None),
    )
    return jax.shard_map(
        per_device, mesh=mesh, in_specs=in_specs, out_specs=out_specs, check_vma=False
    )
```

```python
import functools

import jax
import jax.numpy as jnp
from jax import lax
from jax.experimental import pallas as pl
from jax.experimental.pallas import tpu as pltpu
from jax.sharding import PartitionSpec as P

BF16_ROWS = 16
LANES = 128
MIB = 1024 * 1024


def padded_rows(count):
    return -(-count // BF16_ROWS) * BF16_ROWS


def passed_along(block, axis, distance):
    size = lax.axis_size(axis)
    return lax.ppermute(block, axis, [(i, (i + distance) % size) for i in range(size)])


def all_along(block, axis):
    return [block] + [passed_along(block, axis, k) for k in range(1, lax.axis_size(axis))]


def by_doubling(block, axis):
    size, reach = lax.axis_size(axis), 1
    while reach < size:
        partner = lax.ppermute(block, axis, [(i, i ^ reach) for i in range(size)])
        block = jnp.concatenate([block, partner], axis=0)
        reach *= 2
    return block


def from_place(parts, here, place):
    chosen = parts[0]
    for k in range(1, len(parts)):
        chosen = jnp.where(lax.rem(here - k + len(parts), len(parts)) == place, parts[k], chosen)
    return chosen


def pack_kernel(dims, slots_ref, state_ref, land_ref, earlier_ref, field_ref):
    steps, local, forced, vp, fp = dims
    field_ref[...] = jnp.zeros(field_ref.shape, field_ref.dtype)
    for i in range(local):
        field_ref[i, 0 : state_ref.shape[1]] = state_ref[i]
        for t in range(steps):
            first = (t * local + i) * forced
            field_ref[i, vp + fp * t : vp + fp * t + forced] = slots_ref[first : first + forced]
        field_ref[i, vp + fp * steps : vp + fp * steps + 1] = land_ref[i : i + 1].astype(jnp.bfloat16)


def group_kernel(dims, index_ref, *rest):
    steps, bands, local, forced, vp, fp = dims
    fields, group_ref = rest[:bands], rest[bands]
    for b in range(bands):
        field = from_place([f[...] for f in fields], lax.axis_index("rows"), b)
        for i in range(local):
            for t in range(steps):
                first = ((b * local + i) * steps + t) * forced
                group_ref[first : first + forced] = field[i, vp + fp * t : vp + fp * t + forced].astype(jnp.float32)
    last = bands * local * steps * forced
    group_ref[last : last + 1] = jnp.full((1, group_ref.shape[1]), index_ref[0], jnp.int32).astype(jnp.float32)


def put_taps(taps, value, row, cols, spacing):
    chans, lon = value.shape
    lane = lax.broadcasted_iota(jnp.int32, (chans, lon), 1)
    zero = jnp.zeros_like(value)
    base = 3 * chans * row
    taps[base : base + chans, cols] = jnp.where(lane >= spacing, pltpu.roll(value, spacing, 1), zero)
    taps[base + chans : base + 2 * chans, cols] = value
    taps[base + 2 * chans : base + 3 * chans, cols] = jnp.where(
        lane < lon - spacing, pltpu.roll(value, lon - spacing, 1), zero
    )


def first_kernel(dims, owner_ref, enc_w_ref, dec_w_ref, settings_ref, scale_w_ref, shift_w_ref, *rest):
    steps, layers, bands, local, members, lon, chans, vp, fp, turns = dims
    fields, rest = rest[:bands], rest[bands:]
    everyone, rest = rest[0], rest[1:]
    forced = enc_w_ref.shape[0] - dec_w_ref.shape[0]
    used = bands * local * steps * forced
    group = [everyone.at[k * (used + 8) : (k + 1) * (used + 8)] for k in range(members * turns)]
    field_ref, scale_ref, shift_ref, enc_ref, dec_ref, hidden_ref, taps_ref, turned, lines = rest
    varied = dec_w_ref.shape[0]
    turned[...] = jnp.zeros(turned.shape, turned.dtype)
    turned[0:varied] = enc_w_ref[0:varied].astype(jnp.float32)
    turned[vp : vp + forced] = enc_w_ref[varied : varied + forced].astype(jnp.float32)
    enc_ref[...] = turned[...].T.astype(jnp.bfloat16)
    dec_ref[...] = jnp.zeros(dec_ref.shape, dec_ref.dtype)
    dec_ref[0:varied, :] = dec_w_ref[...]
    band = lax.axis_index("rows")
    for b in range(bands):
        field_ref[b * local : (b + 1) * local] = from_place([f[...] for f in fields], band, b)
    for i in range(bands * local):
        for t in range(steps):
            rows = slice((i * steps + t) * forced, (i * steps + t + 1) * forced)
            place = lax.axis_index("members") ^ owner_ref[0:1, t : t + 1]
            force = group[0][rows, :]
            for k in range(1, members * turns):
                force = jnp.where(place == k, group[k][rows, :], force)
            field_ref[i, vp + fp * t : vp + fp * t + forced, :] = force.astype(jnp.bfloat16)

    settings = settings_ref[...]
    numbers = lax.broadcasted_iota(jnp.int32, settings.shape, 1).astype(jnp.float32)
    for m, entry in enumerate(group):
        chosen = entry[used : used + 1, 0 : settings.shape[1]]
        column = jnp.sum(jnp.where(numbers == chosen, settings, 0.0), axis=1, keepdims=True)
        lines[2 * m : 2 * m + 1] = 1.0 + jnp.sum(scale_w_ref[...] * column, axis=0, keepdims=True)
        lines[2 * m + 1 : 2 * m + 2] = jnp.sum(shift_w_ref[...] * column, axis=0, keepdims=True)
    columns = lines[...].T
    for m in range(len(group)):
        cols = slice((m % members) * lon, (m % members + 1) * lon)
        scale_ref[m // members, :, cols] = jnp.broadcast_to(columns[:, 2 * m : 2 * m + 1], (chans, lon))
        shift_ref[m // members, :, cols] = jnp.broadcast_to(columns[:, 2 * m + 1 : 2 * m + 2], (chans, lon))

    if turns == 1:
        for i in range(bands * local):
            land = field_ref[i, vp + fp * steps : vp + fp * steps + 1, :].astype(jnp.float32)
            lifted = jnp.dot(enc_ref[...], field_ref[i, 0 : vp + fp, :], preferred_element_type=jnp.float32)
            for m in range(members):
                cols = slice(m * lon, (m + 1) * lon)
                value = land * (lifted * scale_ref[0, :, cols] + shift_ref[0, :, cols])
                value = value.astype(jnp.bfloat16)
                hidden_ref[i, :, cols] = value
                put_taps(taps_ref, value, i, cols, 1)


def after_kernel(*refs):
    pass


def after(section, *earlier):
    whole = pl.BlockSpec(memory_space=pl.ANY)
    return pl.pallas_call(
        after_kernel,
        out_shape=jax.ShapeDtypeStruct(section.shape, section.dtype),
        in_specs=[whole] * (1 + len(earlier)),
        out_specs=whole,
        input_output_aliases={0: 0},
        compiler_params=pltpu.CompilerParams(vmem_limit_bytes=MIB),
        cost_estimate=pl.CostEstimate(flops=0, bytes_accessed=0, transcendentals=0),
    )(section, *earlier)


def window_kernel(dims, field_ref, scale_ref, shift_ref, enc_ref, dec_ref, *rest):
    steps, layers, bands, local, members, lon, chans, vp, fp, turns, groups = dims
    lat = bands * local
    hidden, taps = rest[:2]
    pieces = 3 + (layers - 1) * (groups + 1) * bands
    blocks, rest = rest[2 : 2 + pieces], rest[2 + pieces :]
    final_ref, mean_ref, weights, conv, act, inputs, total, sems = rest[:8]
    here, band = lax.axis_index("segment"), lax.axis_index("rows")
    taps_wide, wide = 9 * chans, 3 * chans
    part = chans // bands

    pltpu.make_async_copy(blocks[0], weights.at[here, :, pl.ds(0, taps_wide)], sems.at[here]).start()
    pltpu.make_async_copy(blocks[1], weights.at[here, :, pl.ds(taps_wide, chans)], sems.at[here]).start()
    pltpu.make_async_copy(blocks[2], weights.at[here, :, pl.ds(10 * chans, LANES)], sems.at[here]).start()
    share = 5 * chans // groups
    for k in range(1, layers):
        slot = lax.rem(here - k + layers, layers)
        for g in range(groups + 1):
            if g < groups:
                place = lax.rem(lax.axis_index("groups") - g + groups, groups)
                cols = pl.ds(pl.multiple_of(place * share, LANES), share)
            else:
                cols = pl.ds(groups * share, 10 * chans + LANES - groups * share)
            for j in range(bands):
                rows = pl.ds(pl.multiple_of(lax.rem(band - j + bands, bands) * part, part), part)
                block = blocks[3 + ((k - 1) * (groups + 1) + g) * bands + j]
                pltpu.make_async_copy(block, weights.at[slot, rows, cols], sems.at[slot]).start()

    if turns > 1:
        hidden, taps = rest[8:]

    def columns(m):
        return slice(m * lon, (m + 1) * lon)

    land = [field_ref[i, vp + fp * steps : vp + fp * steps + 1, :].astype(jnp.float32) for i in range(lat)]

    def put_hidden(i, m, value, layer):
        value = value.astype(jnp.bfloat16)
        hidden[i, :, columns(m)] = value
        if layer is not None:
            put_taps(taps, value, i, columns(m), 2 ** (layer % 3))

    def encode(step, turn):
        for i in range(lat):
            force = field_ref[i, vp + fp * step : vp + fp * (step + 1), :]
            for m in range(members):
                inputs[i, vp : vp + fp, columns(m)] = force
                if step == 0:
                    inputs[i, 0:vp, columns(m)] = field_ref[i, 0:vp, :]
            lifted = jnp.dot(enc_ref[...], inputs[i], preferred_element_type=jnp.float32)
            for m in range(members):
                value = lifted[:, columns(m)] * scale_ref[turn, :, columns(m)] + shift_ref[turn, :, columns(m)]
                put_hidden(i, m, land[i] * value, 0)

    def activate(value, layer):
        centred = value - jnp.sum(value, axis=0, keepdims=True) * (1.0 / chans)
        spread = jnp.sum(centred * centred, axis=0, keepdims=True) * (1.0 / chans)
        half = (centred * lax.rsqrt(spread + 1e-05)).astype(jnp.bfloat16) * weights[layer, :, 10 * chans :]
        inner = half * (half * half * 0.2854192648 + 1.5957691216)
        return half + half * jnp.tanh(inner)

    def block(layer, not_yet):
        if not_yet is True:
            pltpu.make_async_copy(weights.at[layer], weights.at[layer], sems.at[layer]).wait()
        elif not_yet is not None:

            @pl.when(not_yet)
            def _():
                pltpu.make_async_copy(weights.at[layer], weights.at[layer], sems.at[layer]).wait()

        for i in range(lat):
            low, high = max(i - 1, 0), min(i + 1, lat - 1)
            conv[i] = jnp.dot(
                weights[layer, :, (low - i + 1) * wide : (high - i + 2) * wide],
                taps[low * wide : (high + 1) * wide, :],
                preferred_element_type=jnp.float32,
            )
        activate_row(0, layer)
        for i in range(lat):
            conv[i] = mixed_row(i, layer)
            if i + 1 < lat:
                activate_row(i + 1, layer)
            add_row(conv[i], i, land[i], layer)

    def activate_row(i, layer):
        for m in range(members):
            act[i, :, columns(m)] = activate(conv[i, :, columns(m)], layer)

    def mixed_row(i, layer):
        return jnp.dot(weights[layer, :, taps_wide : 10 * chans], act[i], preferred_element_type=jnp.float32)

    def add_row(mixed, row, sea, layer):
        for m in range(members):
            kept = hidden[row, :, columns(m)].astype(jnp.float32)
            later = layer + 1 if layer + 1 < layers else None
            put_hidden(row, m, sea * (kept + mixed[:, columns(m)]), later)

    def decode(row, sea, step):
        change = jnp.dot(dec_ref[...], hidden[row], preferred_element_type=jnp.float32)
        for m in range(members):
            old = field_ref[row, 0:vp, :] if step == 0 else inputs[row, 0:vp, columns(m)]
            new = old.astype(jnp.float32) + sea * change[:, columns(m)]
            inputs[row, 0:vp, columns(m)] = new.astype(jnp.bfloat16)

    def last_block(layer):
        first = pl.multiple_of((1 - band) * wide, wide)
        conv[0] = jnp.dot(weights[layer, :, pl.ds(first, 2 * wide)], taps[...], preferred_element_type=jnp.float32)
        sea = field_ref[band, vp + fp * steps : vp + fp * steps + 1, :].astype(jnp.float32)
        activate_row(0, layer)
        add_row(mixed_row(0, layer), band, sea, layer)
        decode(band, sea, steps - 1)

    varied = final_ref.shape[1]

    def window(turn, first):
        for step in range(steps):
            if step > 0 or turns > 1:
                encode(step, turn)
            own_row = step == steps - 1 and step > 0 and lat == 2 and local == 1
            for layer in range(layers):
                if own_row and layer == layers - 1:
                    last_block(layer)
                else:
                    block(layer, first if step == 0 else None)
            if not own_row:
                for i in range(lat):
                    decode(i, land[i], step)
        for i in range(local):
            row = band * local + i
            summed = inputs[row, 0:vp, columns(0)].astype(jnp.float32)
            for m in range(1, members):
                summed = summed + inputs[row, 0:vp, columns(m)].astype(jnp.float32)
            if turns == 1:
                mean_ref[:, i, :] = summed[0:varied] * (1.0 / members)
                final_ref[i] = inputs[row, 0:varied, columns(0)]
            else:
                total[i] = jnp.where(first, summed, total[i] + summed)
                mean_ref[:, i, :] = total[i, 0:varied] * (1.0 / (members * turns))

                @pl.when(first)
                def _():
                    final_ref[i] = inputs[row, 0:varied, columns(0)]

    if turns == 1:
        window(0, True)
    else:
        lax.fori_loop(0, turns, lambda turn, _: window(turn, turn == 0), None)


def per_device(
    init_state,
    forcing_slots,
    atmos_owner,
    land_mask,
    param_index,
    settings,
    scale_weight,
    shift_weight,
    encode_weight,
    conv_weight,
    point_weight,
    norm_gain,
    decode_weight,
):
    members, layers, bands = (lax.axis_size(a) for a in ("members", "segment", "rows"))
    band = lax.axis_index("rows")
    _, local, varied, lon = init_state.shape
    steps, forced = forcing_slots.shape[2], forcing_slots.shape[4]
    chans = conv_weight.shape[1]
    lat = local * bands
    vp, fp = padded_rows(varied), padded_rows(forced)
    part = chans // bands
    at_once = next(n for n in (4, 2, 1) if members % n == 0)
    turns, wide = members // at_once, at_once * lon
    smem, vmem, whole = (pl.BlockSpec(memory_space=s) for s in (pltpu.SMEM, pltpu.VMEM, pl.ANY))
    small, large = (pltpu.CompilerParams(vmem_limit_bytes=n * MIB) for n in (8, 16 + 2 * layers))
    free = pl.CostEstimate(flops=0, bytes_accessed=0, transcendentals=0)

    groups = lax.axis_size("groups")
    share = 5 * chans // groups
    slots = forcing_slots[0, 0].reshape(-1, lon)
    conv = conv_weight[0]
    relayed = lax.dynamic_slice(conv, (band * part, lax.axis_index("groups") * share), (part, share))
    spread = jnp.broadcast_to((norm_gain[0] * 0.5)[:, None], (chans, LANES))
    direct = jnp.concatenate([conv[:, groups * share :], point_weight[0], spread], axis=1)
    direct = lax.dynamic_slice_in_dim(direct, band * part, part, 0)
    field = pl.pallas_call(
        functools.partial(pack_kernel, (steps, local, forced, vp, fp)),
        out_shape=jax.ShapeDtypeStruct((local, vp + fp * steps + BF16_ROWS, lon), jnp.bfloat16),
        in_specs=[vmem] * 3 + [whole],
        out_specs=vmem,
        compiler_params=small,
        cost_estimate=free,
    )(slots, init_state[0], land_mask, direct)
    relayed, direct = (all_along(piece, "segment")[1:] for piece in (relayed, direct))
    fields = all_along(field, "rows")
    group = pl.pallas_call(
        functools.partial(group_kernel, (steps, bands, local, forced, vp, fp)),
        out_shape=jax.ShapeDtypeStruct((lat * steps * forced + 8, lon), jnp.float32),
        in_specs=[smem] + [vmem] * bands,
        out_specs=vmem,
        compiler_params=small,
        cost_estimate=free,
    )(param_index, *fields)
    group = by_doubling(group, "members")

    dims = (steps, layers, bands, local, at_once, lon, chans, vp, fp, turns)
    field, scale, shift, enc, dec, hidden, taps = pl.pallas_call(
        functools.partial(first_kernel, dims),
        out_shape=(
            jax.ShapeDtypeStruct((lat, vp + fp * steps + BF16_ROWS, lon), jnp.bfloat16),
            jax.ShapeDtypeStruct((turns, chans, wide), jnp.float32),
            jax.ShapeDtypeStruct((turns, chans, wide), jnp.float32),
            jax.ShapeDtypeStruct((chans, vp + fp), jnp.bfloat16),
            jax.ShapeDtypeStruct((vp, chans), jnp.bfloat16),
            jax.ShapeDtypeStruct((lat, chans, wide), jnp.bfloat16),
            jax.ShapeDtypeStruct((lat * 3 * chans, wide), jnp.bfloat16),
        ),
        in_specs=[vmem] * (7 + bands),
        out_specs=(vmem,) * 7,
        scratch_shapes=[
            pltpu.VMEM((vp + fp, chans), jnp.float32),
            pltpu.VMEM((-(-2 * members // 8) * 8, chans), jnp.float32),
        ],
        compiler_params=small,
        cost_estimate=free,
    )(atmos_owner, encode_weight.T, decode_weight, settings.T, scale_weight, shift_weight, *fields, group)

    blocks = [conv_weight[0], point_weight[0], spread]
    for k in range(layers - 1):
        shares = all_along(relayed[k], "groups")
        early = all_along(shares[0], "rows")
        blocks += early
        for shared in shares[1:]:
            blocks += all_along(shared, "rows")
        blocks += all_along(after(direct[k], group, *shares[1:], *early[1:]), "rows")

    scratch = [
        pltpu.VMEM((layers, chans, 10 * chans + LANES), jnp.bfloat16),
        pltpu.VMEM((lat, chans, wide), jnp.float32),
        pltpu.VMEM((lat, chans, wide), jnp.bfloat16),
        pltpu.VMEM((lat, vp + fp, wide), jnp.bfloat16),
        pltpu.VMEM((local, vp, lon), jnp.float32),
        pltpu.SemaphoreType.DMA((layers,)),
    ]
    if turns > 1:
        scratch += [pltpu.VMEM(hidden.shape, jnp.bfloat16), pltpu.VMEM(taps.shape, jnp.bfloat16)]
    final, mean = pl.pallas_call(
        functools.partial(window_kernel, dims + (groups,)),
        out_shape=(
            jax.ShapeDtypeStruct((local, varied, lon), jnp.bfloat16),
            jax.ShapeDtypeStruct((varied, local, lon), jnp.float32),
        ),
        in_specs=[vmem] * 7 + [whole] * len(blocks),
        out_specs=(vmem, vmem),
        scratch_shapes=scratch,
        compiler_params=large,
        cost_estimate=free,
    )(field, scale, shift, enc, dec, hidden, taps, *blocks)
    return final[None, None], jnp.swapaxes(mean, 0, 1)[None]
def solution(mesh):
    in_specs = (
        P(("groups", "segment"), "rows", None, None),
        P("members", ("groups", "segment"), None, "rows", None, None),
        P(("groups", "segment"), None),
        P(("groups", "rows"), None),
        P(("groups", "members")),
        P(),
        P(),
        P(),
        P(),
        P("segment", None, None),
        P("segment", None, None),
        P("segment", None),
        P(),
    )
    out_specs = (
        P("members", ("groups", "segment"), "rows", None, None),
        P(("groups", "segment"), "rows", None, None),
    )
    return jax.shard_map(
        per_device, mesh=mesh, in_specs=in_specs, out_specs=out_specs, check_vma=False
    )
```
